32 devices in a mesh: fsdp: 8 (over y, x, core), ctx: 4 (over z).
Axes of the slice: x: 2, y: 2, z: 4, core: 2. Of those that a mesh axis runs over, the one named last changes fastest.
Arguments:
- features: bfloat16 [3, 4096, 8192], P(None, 'ctx', 'fsdp'), may hold values from -6 to 6
- short_taps: float32 [3, 3, 8192], P(None, None, 'fsdp'), may hold values from -3.5 to 3.5
- decay_rates: float32 [512, 16], P('fsdp'), may hold values from 6.1035156e-05 to 0.1
- mode_gains: float32 [512, 16], P('fsdp'), may hold values from -2.5 to 2.5
- cotangent: bfloat16 [4096, 8192], P('ctx', 'fsdp'), may hold values from -6 to 6
Outputs:
- mixer_output: bfloat16 [4096, 8192], P('ctx', 'fsdp')
- feature_grads: bfloat16 [3, 4096, 8192], P(None, 'ctx', 'fsdp')
- gain_grads: float32 [512, 16], P('fsdp')
- rate_grads: float32 [512, 16], P('fsdp')
The draws below stay inside these ranges and needn't reach their ends.
All inputs are finite; a program needn't handle non-finite values.
Results may differ from the reference program's by a relative error of at most 0.0048.
Values may be sent and summed in bfloat16 or wider, within the bound.
No kernel may reach another device: no remote copies, remote signals or barrier semaphores. Data moves between devices by JAX's collectives and lax.ppermute only.
A program may use at most 128 MiB of HBM per device.

```python
import jax
import jax.numpy as jnp
from jax import lax

D = 8192
GROUP = 16
ORDER = 16
SHORT = 3
SEQ = 4096
GROUPS = 512


def draw_decay_rates(key, part):
    base = jax.random.fold_in(key, 11)
    choose_key, slow_key, other_key = jax.random.split(base, 3)
    slow_share = 0.5
    lowest = 0.25 / SEQ
    slow_top = 2.0 / SEQ
    slow_pick = jax.random.uniform(choose_key, (GROUPS, ORDER), jnp.float32) < slow_share
    slow_log = jax.random.uniform(slow_key, (GROUPS, ORDER), jnp.float32, jnp.log(lowest), jnp.log(slow_top))
    other_log = jax.random.uniform(other_key, (GROUPS, ORDER), jnp.float32, jnp.log(slow_top), jnp.log(0.1))
    rates = jnp.exp(jnp.where(slow_pick, slow_log, other_log))
    return jnp.clip(rates, lowest, 0.1).astype(jnp.float32)


def levels(key, shape, shards, least, largest):
    def one(axis_at, blocks):
        heights = jax.random.uniform(jax.random.fold_in(jax.random.fold_in(key, 6), axis_at), (blocks,), jnp.float32, least / len(shards), largest / len(shards))
        return jnp.repeat(jnp.exp(heights), shape[axis_at] // blocks).reshape((-1,) + (1,) * (len(shape) - axis_at - 1))

    loudness = one(*shards[0])
    for cut in shards[1:]:
        loudness = loudness * one(*cut)
    return loudness


def noise(own_key, shape, scale, limit, cuts=(), kind=jnp.bfloat16):
    entries = jax.random.normal(own_key, shape, jnp.float32) * scale
    if len(cuts) > 0:
        entries = levels(own_key, shape, cuts, -0.22, 0.18) * entries
    return jnp.clip(entries, min=-limit, max=limit).astype(kind)


def setup_inputs(seed: int = 0) -> dict:
    streams_of = jax.random.split(jax.random.key(seed), 6)
    features = noise(streams_of[0], (3, SEQ, D), 1.0, 6.0, ((1, 4), (2, 8)))
    short_taps = noise(streams_of[1], (3, SHORT, D), SHORT ** -0.5, 3.5, ((2, 8),), jnp.float32)
    decay_rates = draw_decay_rates(jax.random.fold_in(streams_of[5], 71), 0)
    mode_gains = noise(streams_of[3], (GROUPS, ORDER), 0.5, 2.5, ((0, 8),), jnp.float32)
    cotangent = noise(streams_of[4], (SEQ, D), 1.0, 6.0, ((0, 4), (1, 8)))
    return dict(features=features, short_taps=short_taps, decay_rates=decay_rates, mode_gains=mode_gains, cotangent=cotangent)


def spread(gn_table):
    return jnp.repeat(gn_table.T, GROUP, axis=1)

def reference(features, short_taps, decay_rates, mode_gains, cotangent):
    seq_len = features.shape[1]
    total_width = features.shape[2]
    slab_width = min(total_width, 32 * GROUP)
    slab_count = total_width // slab_width
    slab_groups = slab_width // GROUP
    rim_rows = SHORT - 1

    def slab_pass(slab_index):
        slab_start = (slab_index * slab_width).astype(jnp.int32)
        group_start = (slab_index * slab_groups).astype(jnp.int32)
        feature_slab = lax.dynamic_slice_in_dim(features, slab_start, slab_width, 2)
        taps_slab = lax.dynamic_slice_in_dim(short_taps, slab_start, slab_width, 2)
        rate_slab = lax.dynamic_slice_in_dim(decay_rates, group_start, slab_groups, 0)
        gain_slab = lax.dynamic_slice_in_dim(mode_gains, group_start, slab_groups, 0)
        upstream = lax.dynamic_slice_in_dim(cotangent, slab_start, slab_width, 1)
        padded = jnp.pad(feature_slab, ((0, 0), (rim_rows, 0), (0, 0)))
        shaped = jnp.zeros((3, seq_len, slab_width), jnp.float32)
        for offset in range(SHORT):
            shaped = shaped + taps_slab[:, offset, None, :] * padded[:, rim_rows - offset:rim_rows - offset + seq_len, :]
        product = lax.optimization_barrier((shaped[1] * shaped[2]).astype(jnp.bfloat16)).astype(jnp.float32)
        adjoint = upstream * shaped[0]
        mode_coefs = gain_slab * jnp.sqrt(2.0 * rate_slab)
        decay_cols = spread(jnp.exp(-rate_slab))
        weight_cols = spread(mode_coefs)
        zero_state = jnp.zeros((ORDER, slab_width), jnp.float32)

        def forward_step(carried_in, inputs):
            mode_state, lagged, first_acc, lag_acc = carried_in
            z_row, e_row = inputs
            lagged = decay_cols * (lagged - mode_state)
            mode_state = decay_cols * mode_state + z_row[None, :]
            first_acc = first_acc + e_row[None, :] * mode_state
            lag_acc = lag_acc + e_row[None, :] * lagged
            return ((mode_state, lagged, first_acc, lag_acc), lax.optimization_barrier(jnp.sum(weight_cols * mode_state, axis=0)))
        final_carry, inner_sum = lax.scan(forward_step, (zero_state, zero_state, zero_state, zero_state), (product, adjoint))
        first_acc, lag_acc = (final_carry[2], final_carry[3])

        def backward_step(later_state, e_row):
            mode_state = decay_cols * later_state + e_row[None, :]
            return (mode_state, lax.optimization_barrier(jnp.sum(weight_cols * mode_state, axis=0)))
        first_state, product_grad = lax.scan(backward_step, zero_state, adjoint, reverse=True)
        mixed_slab = (shaped[0] * inner_sum).astype(jnp.bfloat16)
        adjoints = jnp.stack([upstream * inner_sum, product_grad * shaped[2], product_grad * shaped[1]])
        appended = jnp.pad(adjoints, ((0, 0), (0, rim_rows), (0, 0)))
        grad_acc = jnp.zeros((3, seq_len, slab_width), jnp.float32)
        for offset in range(SHORT):
            grad_acc = grad_acc + taps_slab[:, offset, None, :] * appended[:, offset:offset + seq_len, :]
        first_total = first_acc.reshape(ORDER, slab_groups, GROUP).sum(axis=2).T
        lag_total = lag_acc.reshape(ORDER, slab_groups, GROUP).sum(axis=2).T
        gain_part = jnp.sqrt(2.0 * rate_slab) * first_total
        rate_part = mode_coefs * (0.5 * first_total + rate_slab * lag_total)
        return (mixed_slab, grad_acc.astype(jnp.bfloat16), gain_part, rate_part)
    indices = jnp.arange(slab_count, dtype=jnp.int32)
    mixed_slabs, grad_slabs, gain_slabs, rate_slabs = lax.map(slab_pass, indices)
    mixer_output = jnp.moveaxis(mixed_slabs, 0, 1).reshape(seq_len, total_width)
    feature_grads = jnp.moveaxis(grad_slabs, 0, 2).reshape(3, seq_len, total_width)
    gain_raw = gain_slabs.reshape(GROUPS, ORDER)
    rate_raw = rate_slabs.reshape(GROUPS, ORDER)
    mean_square = (jnp.sum(gain_raw * gain_raw) + jnp.sum(rate_raw * rate_raw)) / (2 * GROUPS * ORDER)
    factor = jnp.minimum(1.0, lax.rsqrt(mean_square + 1e-06))
    return (mixer_output, feature_grads, factor * gain_raw, factor * rate_raw)
```

```python
import jax
import jax.numpy as jnp
from jax import lax
from jax.experimental import pallas as pl
from jax.experimental.pallas import tpu as pltpu
from jax.sharding import PartitionSpec as P

LANES = 128
MODES = 16
MEMBERS = 16
TILE_GROUPS = LANES // MEMBERS
ROWS = LANES
f32 = jnp.float32
bf16 = jnp.bfloat16


def split(value):
    high = value.astype(bf16)
    return high, (value - high.astype(f32)).astype(bf16)


def dot_nt(left, right):
    return lax.dot_general(left, right, (((1,), (1,)), ((), ())), preferred_element_type=f32)


def dot_tn(left, right):
    return lax.dot_general(left, right, (((0,), (0,)), ((), ())), preferred_element_type=f32)


def dot_nn(left, right):
    return lax.dot_general(left, right, (((1,), (0,)), ((), ())), preferred_element_type=f32)


def iota(axis, shape):
    return lax.broadcasted_iota(jnp.int32, shape, axis)


def widen(feat_ref, halo_ref, wide, tokens):
    for i in range(3):
        wide[i, 0:8, :] = halo_ref[i]
        wide[i, 8 : 8 + tokens, :] = feat_ref[i].astype(f32)


def short_block(wide, taps_ref, i, start, count):
    return (
        taps_ref[i, 0:1, :] * wide[i, start + 8 : start + 8 + count, :]
        + taps_ref[i, 1:2, :] * wide[i, start + 7 : start + 7 + count, :]
        + taps_ref[i, 2:3, :] * wide[i, start + 6 : start + 6 + count, :]
    )


def sheared(row8):
    which = iota(0, row8.shape)
    for bit in (1, 2, 4):
        row8 = jnp.where((which & bit) != 0, pltpu.roll(row8, LANES - bit, 1), row8)
    return row8


def spread_rows(row):
    rows = jnp.broadcast_to(row, (8, LANES))
    which = iota(0, rows.shape)
    for bit in (1, 2, 4):
        rows = jnp.where((which & bit) != 0, pltpu.roll(rows, bit, 1), rows)
    return rows


def circulant(row):
    base = spread_rows(row)
    return jnp.concatenate(
        [base if r == 0 else pltpu.roll(base, 8 * r, 1) for r in range(LANES // 8)], axis=0
    )


def local_kernel(
    feat_ref, halo_ref, taps_ref, cot_ref, par_ref, rate_ref,
    inner_ref, grad_ref, carry_ref, state_ref, diag_ref, cross_ref,
    wide, z_all, eh_all, el_all,
):
    tokens = feat_ref.shape[1]
    blocks = tokens // LANES
    widen(feat_ref, halo_ref, wide, tokens)
    for b in range(blocks):
        query = short_block(wide, taps_ref, 0, b * LANES, LANES)
        key = short_block(wide, taps_ref, 1, b * LANES, LANES)
        value = short_block(wide, taps_ref, 2, b * LANES, LANES)
        z_t = jnp.transpose((key * value).astype(bf16))
        e_t = jnp.transpose(cot_ref[b * LANES : (b + 1) * LANES, :].astype(f32) * query)
        e_high, e_low = split(e_t)
        at = slice(b * MEMBERS, (b + 1) * MEMBERS)
        for g in range(TILE_GROUPS):
            of = slice(g * MEMBERS, (g + 1) * MEMBERS)
            z_all[g, at, :] = z_t[of]
            eh_all[g, at, :] = e_high[of]
            el_all[g, at, :] = e_low[of]

    lag = iota(1, (MODES, LANES)).astype(f32)
    row_at = iota(0, (LANES, LANES))
    lane_at = iota(1, (LANES, LANES))
    lane_row = iota(1, (1, LANES))
    slot_x = jnp.where((lane_row >= 48) & (lane_row < 64), float(LANES), 0.0)
    slot_y = jnp.where((lane_row >= 96) & (lane_row < 112), float(LANES), 0.0)
    nothing = jnp.zeros((4 * MODES, LANES), bf16)
    first_acc = jnp.zeros((MODES, LANES), f32)
    lag_acc = jnp.zeros((MODES, LANES), f32)
    ends, starts = [], []
    for g in range(TILE_GROUPS):
        rates = par_ref[0, g]
        coefs = par_ref[1, g]
        power = jnp.exp(-rates * lag)
        power_back = jnp.exp(-rates * (LANES - 1.0 - lag))
        power_after = power * jnp.exp(-rates)
        taps = jnp.sum(coefs * power, axis=0, keepdims=True)
        taps_back = jnp.sum(coefs * power_back, axis=0, keepdims=True)
        toep_f = jnp.where(row_at >= lane_at, circulant(pltpu.roll(taps_back, 1, 1)), 0.0)
        toep_b = jnp.where(lane_at >= row_at, circulant(taps), 0.0)
        tf_high, tf_low = split(toep_f)
        tb_high, tb_low = split(toep_b)
        s_high, s_low = split(power_back)
        l_high, l_low = split((LANES - 1.0 - lag) * power_back)
        m_high, m_low = split(power_after)
        n_high, n_low = split((lag + 1.0) * power_after)
        wf_high = jnp.concatenate([tf_high, s_high, s_high, s_high, l_high, nothing], axis=0)
        wf_low = jnp.concatenate([tf_low, s_low, s_low, s_low, l_low, nothing], axis=0)
        wb_high = jnp.concatenate([tb_high, nothing, m_high, m_high, n_high, m_high], axis=0)
        wb_low = jnp.concatenate([tb_low, nothing, m_low, m_low, n_low, m_low], axis=0)
        z = z_all[g]
        eh = eh_all[g]
        el = el_all[g]
        from_z = dot_nt(jnp.concatenate([z, z], axis=1), jnp.concatenate([wf_high, wf_low], axis=1))
        from_e = dot_nt(
            jnp.concatenate([eh, el], axis=1), jnp.concatenate([wb_high, wb_high], axis=1)
        ) + dot_nt(eh, wb_low)
        inner_ref[g] = from_z[:, :LANES]
        grad_ref[g] = from_e[:, :LANES]
        x_own = from_z[:, LANES:]
        y_own = from_e[:, LANES:]
        span = jnp.exp(rate_ref[g : g + 1, :] * (-float(LANES)))
        x_now = jnp.zeros((MEMBERS, LANES), f32)
        y_now = jnp.zeros((MEMBERS, LANES), f32)
        x_prev = []
        y_next = [None] * blocks
        for b in range(blocks):
            x_prev.append(x_now)
            x_now = (
                span * (x_now + slot_x * pltpu.roll(x_now, MODES, 1))
                + x_own[b * MEMBERS : (b + 1) * MEMBERS]
            )
        for b in reversed(range(blocks)):
            y_next[b] = y_now
            y_now = (
                span * (y_now + slot_y * pltpu.roll(y_now, MODES, 1))
                + y_own[b * MEMBERS : (b + 1) * MEMBERS]
            )
        ends.append(x_now)
        starts.append(y_now)
        x_prev = jnp.concatenate(x_prev, axis=0)
        carry_ref[g] = x_prev + jnp.concatenate(y_next, axis=0)
        cross_ref[g : g + 1, :] = jnp.sum(
            x_prev * pltpu.roll(y_own, 4 * MODES, 1), axis=0, keepdims=True
        )
        gram = dot_tn(jnp.concatenate([z, z], axis=0), jnp.concatenate([eh, el], axis=0))
        gram = jnp.where(lane_at >= row_at, gram, 0.0)
        folded = gram[0:8]
        for r in range(1, LANES // 8):
            folded = folded + pltpu.roll(gram[8 * r : 8 * r + 8], LANES - 8 * r, 1)
        corr = jnp.sum(sheared(folded), axis=0, keepdims=True)
        weighted = power * corr
        first_col = jnp.sum(weighted, axis=1, keepdims=True)
        lag_col = jnp.sum(lag * weighted, axis=1, keepdims=True)
        mine = iota(1, (MODES, LANES)) == g
        first_acc = first_acc + jnp.where(mine, first_col, 0.0)
        lag_acc = lag_acc + jnp.where(mine, lag_col, 0.0)
    diag_ref[0, 0] = first_acc
    diag_ref[0, 1] = lag_acc
    both = jnp.concatenate(ends, axis=0) + jnp.concatenate(starts, axis=0)
    turned = jnp.transpose(both)
    state_ref[0:16] = turned[0:16]
    state_ref[16:32] = turned[48:64]
    state_ref[32:48] = turned[64:80]
    state_ref[48:64] = turned[96:112]


def output_kernel(
    feat_ref, halo_ref, next_ref, taps_ref, cot_ref, par_ref, rate_ref,
    inner_ref, grad_ref, carry_ref, bound_ref, wide_rate_ref, wide_coef_ref,
    mixer_ref, fgrad_ref,
    wide, adj, inner_t, grad_t,
):
    tokens = feat_ref.shape[1]
    blocks = tokens // LANES
    widen(feat_ref, halo_ref, wide, tokens)
    for i in range(3):
        wide[i, 8 + tokens : 16 + tokens, :] = next_ref[i]
    lag = iota(1, (MODES, LANES)).astype(f32)
    lane_row = iota(1, (1, LANES))
    lane_16 = iota(1, (MEMBERS, LANES))
    is_low = ((lane_16 >= 16) & (lane_16 < 32)) | ((lane_16 >= 80) & (lane_16 < 96))
    before = bound_ref[0:16]
    after = bound_ref[16:32]
    gap = jnp.zeros((MODES, LANES), f32)
    stacked = jnp.concatenate([before, before, before, gap, after, after, gap, after], axis=0)
    turned = jnp.transpose(stacked)
    none_16 = jnp.zeros((MODES, LANES), bf16)
    none_64 = jnp.zeros((4 * MODES, LANES), bf16)
    for g in range(TILE_GROUPS):
        rates = par_ref[0, g]
        coefs = par_ref[1, g]
        cz_high, cz_low = split(coefs * jnp.exp(-rates * (lag + 1.0)))
        ce_high, ce_low = split(coefs * jnp.exp(-rates * (LANES - 1.0 - lag)))
        right = jnp.concatenate(
            [
                jnp.concatenate([cz_high, cz_high, cz_low, none_16, none_64], axis=0),
                jnp.concatenate([none_64, ce_high, ce_high, none_16, ce_low], axis=0),
            ],
            axis=1,
        )
        rate_row = rate_ref[g : g + 1, :]
        mine = turned[g * MEMBERS : (g + 1) * MEMBERS]
        rows = []
        for b in range(blocks):
            steps = jnp.where(lane_row < 64, float(b * LANES), float((blocks - 1 - b) * LANES))
            value = carry_ref[g, b * MEMBERS : (b + 1) * MEMBERS, :] + mine * jnp.exp(
                -rate_row * steps
            )
            high, low = split(value)
            rows.append(jnp.where(is_low, low.astype(f32), high.astype(f32)).astype(bf16))
        carried = dot_nn(jnp.concatenate(rows, axis=0), right)
        whole_inner = inner_ref[g] + carried[:, :LANES]
        whole_grad = grad_ref[g] + carried[:, LANES:]
        of = slice(g * MEMBERS, (g + 1) * MEMBERS)
        for b in range(blocks):
            at = slice(b * MEMBERS, (b + 1) * MEMBERS)
            inner_t[b, of, :] = whole_inner[at]
            grad_t[b, of, :] = whole_grad[at]
    for b in range(blocks):
        at = slice(b * LANES, (b + 1) * LANES)
        query = short_block(wide, taps_ref, 0, b * LANES, LANES)
        key = short_block(wide, taps_ref, 1, b * LANES, LANES)
        value = short_block(wide, taps_ref, 2, b * LANES, LANES)
        inner = jnp.transpose(inner_t[b])
        grad = jnp.transpose(grad_t[b])
        mixer_ref[at, :] = (query * inner).astype(bf16)
        adj[0, at, :] = cot_ref[at, :].astype(f32) * inner
        adj[1, at, :] = grad * value
        adj[2, at, :] = grad * key
    key = short_block(wide, taps_ref, 1, tokens, 8)
    value = short_block(wide, taps_ref, 2, tokens, 8)
    query = short_block(wide, taps_ref, 0, tokens, 8)
    z = (key * value).astype(bf16).astype(f32)
    e = next_ref[3] * query
    rates = wide_rate_ref[...]
    coefs = wide_coef_ref[...]
    decay = jnp.exp(-rates)
    grow = jnp.exp(rates)
    state = bound_ref[32:48]
    sum_0 = jnp.sum(coefs, axis=0, keepdims=True)
    sum_1 = jnp.sum(coefs * decay, axis=0, keepdims=True)
    inner_0 = jnp.sum(coefs * decay * state, axis=0, keepdims=True) + sum_0 * z[0:1]
    inner_1 = (
        jnp.sum(coefs * decay * decay * state, axis=0, keepdims=True)
        + sum_1 * z[0:1]
        + sum_0 * z[1:2]
    )
    grad_0 = jnp.sum(coefs * grow * after, axis=0, keepdims=True)
    grad_1 = jnp.sum(coefs * grow * (grow * after - e[0:1]), axis=0, keepdims=True)
    which = iota(0, (8, LANES))
    inner_8 = jnp.where(which == 0, inner_0, jnp.where(which == 1, inner_1, 0.0))
    grad_8 = jnp.where(which == 0, grad_0, jnp.where(which == 1, grad_1, 0.0))
    adj[0, tokens : tokens + 8, :] = next_ref[3] * inner_8
    adj[1, tokens : tokens + 8, :] = grad_8 * value
    adj[2, tokens : tokens + 8, :] = grad_8 * key
    for b in range(blocks):
        start = b * LANES
        for i in range(3):
            fgrad_ref[i, start : start + LANES, :] = (
                taps_ref[i, 0:1, :] * adj[i, start : start + LANES, :]
                + taps_ref[i, 1:2, :] * adj[i, start + 1 : start + 1 + LANES, :]
                + taps_ref[i, 2:3, :] * adj[i, start + 2 : start + 2 + LANES, :]
            ).astype(bf16)


def shifted(value, axis, steps):
    count = lax.axis_size(axis)
    return lax.ppermute(value, axis, [(i, (i + steps) % count) for i in range(count)])


def swapped(value, axis, key):
    count = lax.axis_size(axis)
    return lax.ppermute(value, axis, [(i, i ^ key) for i in range(count)])


def per_device(features, short_taps, decay_rates, mode_gains, cotangent):
    tokens = features.shape[1]
    channels = features.shape[2]
    groups = decay_rates.shape[0]
    tiles = channels // LANES
    blocks = tokens // LANES
    ctx_count = lax.axis_size("ctx")
    ctx_index = lax.axis_index("ctx")

    tail = shifted(features[:, tokens - 2 :, :], "ctx", 1).astype(f32)
    tail = jnp.where(ctx_index == 0, 0.0, tail)
    halo = jnp.pad(tail, ((0, 0), (6, 0), (0, 0)))
    head = jnp.concatenate([features[:, :2, :], cotangent[None, :2, :]], axis=0)
    ahead = shifted(head, "ctx", -1).astype(f32)
    ahead = jnp.where(ctx_index == ctx_count - 1, 0.0, ahead)
    ahead = jnp.pad(ahead, ((0, 0), (0, 6), (0, 0)))

    mode_coefs = mode_gains * jnp.sqrt(2.0 * decay_rates)
    params = jnp.broadcast_to(
        jnp.stack([decay_rates, mode_coefs])[:, :, :, None], (2, groups, MODES, LANES)
    )
    rate_rows = jnp.tile(decay_rates, (1, LANES // MODES))
    rate_cols = jnp.repeat(decay_rates.T, MEMBERS, axis=1)
    coef_cols = jnp.repeat(mode_coefs.T, MEMBERS, axis=1)

    per_group = pl.BlockSpec((TILE_GROUPS, ROWS, LANES), lambda j: (j, 0, 0))
    feat_spec = pl.BlockSpec((3, tokens, LANES), lambda j: (0, 0, j))
    halo_spec = pl.BlockSpec((3, 8, LANES), lambda j: (0, 0, j))
    taps_spec = pl.BlockSpec((3, 3, LANES), lambda j: (0, 0, j))
    cot_spec = pl.BlockSpec((tokens, LANES), lambda j: (0, j))
    par_spec = pl.BlockSpec((2, TILE_GROUPS, MODES, LANES), lambda j: (0, j, 0, 0))
    rate_spec = pl.BlockSpec((TILE_GROUPS, LANES), lambda j: (j, 0))
    rows = blocks * MEMBERS
    big = jax.ShapeDtypeStruct((groups, rows, LANES), f32)
    inner, grad, carry, states, diag, cross = pl.pallas_call(
        local_kernel,
        grid=(tiles,),
        in_specs=[feat_spec, halo_spec, taps_spec, cot_spec, par_spec, rate_spec],
        out_specs=[
            per_group,
            per_group,
            per_group,
            pl.BlockSpec((4 * MODES, LANES), lambda j: (0, j)),
            pl.BlockSpec((1, 2, MODES, LANES), lambda j: (j, 0, 0, 0)),
            rate_spec,
        ],
        out_shape=[
            big,
            big,
            big,
            jax.ShapeDtypeStruct((4 * MODES, channels), f32),
            jax.ShapeDtypeStruct((tiles, 2, MODES, LANES), f32),
            jax.ShapeDtypeStruct((groups, LANES), f32),
        ],
        scratch_shapes=[
            pltpu.VMEM((3, tokens + 8, LANES), f32),
            pltpu.VMEM((TILE_GROUPS, rows, LANES), bf16),
            pltpu.VMEM((TILE_GROUPS, rows, LANES), bf16),
            pltpu.VMEM((TILE_GROUPS, rows, LANES), bf16),
        ],
        compiler_params=pltpu.CompilerParams(vmem_limit_bytes=40 * 2**20),
        name="local_part",
    )(features, halo, short_taps, cotangent, params, rate_rows)

    ends, lagged, moment_0, moment_1 = (
        states[0:16],
        states[16:32],
        states[32:48],
        states[48:64],
    )
    s_prev = jnp.zeros_like(ends)
    l_prev = jnp.zeros_like(ends)
    e_next = jnp.zeros_like(ends)
    for key in range(1, ctx_count):
        other = ctx_index ^ key
        earlier = other < ctx_index
        sent = jnp.where(earlier, states[32:64], states[0:32])
        got = swapped(sent, "ctx", key)
        away = (jnp.abs(ctx_index - other) - 1).astype(f32) * tokens
        weight = jnp.exp(-rate_cols * away)
        s_part = weight * got[:16]
        s_prev = s_prev + jnp.where(earlier, s_part, 0.0)
        l_prev = l_prev + jnp.where(earlier, weight * got[16:] + away * s_part, 0.0)
        e_next = e_next + jnp.where(earlier, 0.0, s_part)
    own_end = ends + jnp.exp(-rate_cols * tokens) * s_prev
    bound = jnp.concatenate([s_prev, e_next, own_end], axis=0)

    summed_first = (moment_0 * s_prev).reshape(MODES, groups, MEMBERS).sum(axis=2).T
    summed_lag = (
        (moment_1 * s_prev + moment_0 * l_prev).reshape(MODES, groups, MEMBERS).sum(axis=2).T
    )
    diag = diag[:, :, :, :TILE_GROUPS].transpose(1, 0, 3, 2).reshape(2, groups, MODES)
    first_total = diag[0] + cross[:, 0:16] + summed_first
    lag_total = -(diag[1] + cross[:, 32:48] + cross[:, 48:64] + summed_lag)
    gain_part = jnp.sqrt(2.0 * decay_rates) * first_total
    rate_part = mode_coefs * (0.5 * first_total + decay_rates * lag_total)
    local = jnp.stack([gain_part, rate_part])
    terms = [local] + [swapped(local, "ctx", key) for key in range(1, ctx_count)]
    while len(terms) > 1:
        terms = [terms[i] + terms[i + 1] for i in range(0, len(terms), 2)]
    summed = terms[0]
    squares = jnp.broadcast_to(jnp.sum(summed * summed), (8, LANES))
    fsdp_count = lax.axis_size("fsdp")
    step = 1
    while step < fsdp_count:
        squares = squares + swapped(squares, "fsdp", step)
        step *= 2
    entry_count = 2 * groups * MODES * fsdp_count
    factor = jnp.minimum(1.0, lax.rsqrt(squares[0, 0] / entry_count + 1e-06))
    clipped = summed * factor

    wide_spec = pl.BlockSpec((MODES, LANES), lambda j: (0, j))
    mixer, feature_grads = pl.pallas_call(
        output_kernel,
        grid=(tiles,),
        in_specs=[
            feat_spec,
            halo_spec,
            pl.BlockSpec((4, 8, LANES), lambda j: (0, 0, j)),
            taps_spec,
            cot_spec,
            par_spec,
            rate_spec,
            per_group,
            per_group,
            per_group,
            pl.BlockSpec((3 * MODES, LANES), lambda j: (0, j)),
            wide_spec,
            wide_spec,
        ],
        out_specs=[cot_spec, feat_spec],
        out_shape=[
            jax.ShapeDtypeStruct((tokens, channels), bf16),
            jax.ShapeDtypeStruct((3, tokens, channels), bf16),
        ],
        scratch_shapes=[
            pltpu.VMEM((3, tokens + 16, LANES), f32),
            pltpu.VMEM((3, tokens + 8, LANES), f32),
            pltpu.VMEM((blocks, LANES, LANES), f32),
            pltpu.VMEM((blocks, LANES, LANES), f32),
        ],
        compiler_params=pltpu.CompilerParams(vmem_limit_bytes=40 * 2**20),
        name="output_part",
    )(
        features, halo, ahead, short_taps, cotangent, params, rate_rows,
        inner, grad, carry, bound, rate_cols, coef_cols,
    )
    return (mixer, feature_grads, clipped[0], clipped[1])


def solution(mesh):
    return jax.shard_map(
        per_device,
        mesh=mesh,
        in_specs=(
            P(None, "ctx", "fsdp"),
            P(None, None, "fsdp"),
            P("fsdp", None),
            P("fsdp", None),
            P("ctx", "fsdp"),
        ),
        out_specs=(P("ctx", "fsdp"), P(None, "ctx", "fsdp"), P("fsdp", None), P("fsdp", None)),
        check_vma=False,
    )
```

```python
import jax
import jax.numpy as jnp
from jax import lax
from jax.experimental import pallas as pl
from jax.experimental.pallas import tpu as pltpu
from jax.sharding import PartitionSpec as P

LANES = 128
MODES = 16
MEMBERS = 16
TILE_GROUPS = LANES // MEMBERS
ROWS = LANES
f32 = jnp.float32
bf16 = jnp.bfloat16


def split(value):
    high = value.astype(bf16)
    return high, (value - high.astype(f32)).astype(bf16)


def dot_nt(left, right):
    return lax.dot_general(left, right, (((1,), (1,)), ((), ())), preferred_element_type=f32)


def dot_tn(left, right):
    return lax.dot_general(left, right, (((0,), (0,)), ((), ())), preferred_element_type=f32)


def dot_nn(left, right):
    return lax.dot_general(left, right, (((1,), (0,)), ((), ())), preferred_element_type=f32)


def iota(axis, shape):
    return lax.broadcasted_iota(jnp.int32, shape, axis)


def widen(feat_ref, halo_ref, wide, tokens):
    for i in range(3):
        wide[i, 0:8, :] = halo_ref[i]
        wide[i, 8 : 8 + tokens, :] = feat_ref[i].astype(f32)


def short_block(wide, taps_ref, i, start, count):
    return (
        taps_ref[i, 0:1, :] * wide[i, start + 8 : start + 8 + count, :]
        + taps_ref[i, 1:2, :] * wide[i, start + 7 : start + 7 + count, :]
        + taps_ref[i, 2:3, :] * wide[i, start + 6 : start + 6 + count, :]
    )


def sheared(row8, period):
    which = iota(0, row8.shape) % period
    for bit in (1, 2, 4):
        row8 = jnp.where((which & bit) != 0, pltpu.roll(row8, LANES - bit, 1), row8)
    return row8


def circulant(row):
    return pltpu.roll(jnp.broadcast_to(row, (LANES, LANES)), 0, 1, stride=1, stride_axis=0)


def parameters(rate_ref, gain_ref):
    rates = jnp.concatenate([rate_ref[...]] * (LANES // MODES), axis=1)
    gains = jnp.concatenate([gain_ref[...]] * (LANES // MODES), axis=1)
    coefs = gains * jnp.sqrt(2.0 * rates)
    own = iota(0, (TILE_GROUPS, LANES)) == iota(1, (TILE_GROUPS, LANES)) // MODES

    def columns(rows):
        flat = jnp.sum(jnp.where(own, rows, 0.0), axis=0, keepdims=True)
        return jnp.transpose(jnp.broadcast_to(flat, (LANES, LANES)))

    return rates, coefs, columns(rates), columns(coefs)


def per_member(rows):
    return jnp.concatenate(
        [jnp.broadcast_to(rows[g : g + 1], (MEMBERS, LANES)) for g in range(TILE_GROUPS)], axis=0
    )


def local_kernel(
    feat_ref, halo_ref, taps_ref, cot_ref, rate_ref, gain_ref,
    inner_ref, grad_ref, carry_ref, state_ref, diag_ref, cross_ref,
    wide, z_all, eh_all, el_all, wf_all, wb_all, x_all, y_all, power_all, fold_all,
):
    tokens = feat_ref.shape[1]
    blocks = tokens // LANES
    rate_rows, _, rates, coefs = parameters(rate_ref, gain_ref)
    lag = iota(1, (LANES, LANES)).astype(f32)
    row_at = iota(0, (LANES, LANES))
    lane_at = iota(1, (LANES, LANES))
    lane_row = iota(1, (1, LANES))

    power = jnp.exp(-rates * lag)
    power_back = jnp.exp(-rates * (LANES - 1.0 - lag))
    power_after = power * jnp.exp(-rates)
    power_all[...] = power
    by_group = (TILE_GROUPS, MODES, LANES)
    taps = jnp.sum((coefs * power).reshape(by_group), axis=1)
    taps_back = pltpu.roll(jnp.sum((coefs * power_back).reshape(by_group), axis=1), 1, 1)
    s_parts = split(power_back)
    l_parts = split((LANES - 1.0 - lag) * power_back)
    m_parts = split(power_after)
    n_parts = split((lag + 1.0) * power_after)
    nothing = jnp.zeros((4 * MODES, LANES), bf16)
    for g in range(TILE_GROUPS):
        of = slice(g * MODES, (g + 1) * MODES)
        toep_f = split(jnp.where(row_at >= lane_at, circulant(taps_back[g : g + 1]), 0.0))
        toep_b = split(jnp.where(lane_at >= row_at, circulant(taps[g : g + 1]), 0.0))
        for part in range(2):
            at = slice(part * LANES, (part + 1) * LANES)
            wf_all[g, 0:LANES, at] = toep_f[part]
            wb_all[g, 0:LANES, at] = toep_b[part]
            s_of, l_of = s_parts[part][of], l_parts[part][of]
            m_of, n_of = m_parts[part][of], n_parts[part][of]
            wf_all[g, LANES:, at] = jnp.concatenate([s_of, s_of, s_of, l_of, nothing], axis=0)
            wb_all[g, LANES:, at] = jnp.concatenate([nothing, m_of, m_of, n_of, m_of], axis=0)

    widen(feat_ref, halo_ref, wide, tokens)
    for b in range(blocks):
        query = short_block(wide, taps_ref, 0, b * LANES, LANES)
        key = short_block(wide, taps_ref, 1, b * LANES, LANES)
        value = short_block(wide, taps_ref, 2, b * LANES, LANES)
        z_t = jnp.transpose((key * value).astype(bf16))
        e_t = jnp.transpose(cot_ref[b * LANES : (b + 1) * LANES, :].astype(f32) * query)
        e_high, e_low = split(e_t)
        at = slice(b * MEMBERS, (b + 1) * MEMBERS)
        for g in range(TILE_GROUPS):
            of = slice(g * MEMBERS, (g + 1) * MEMBERS)
            z_all[g, at, :] = z_t[of]
            eh_all[g, at, :] = e_high[of]
            el_all[g, at, :] = e_low[of]

    for g in range(TILE_GROUPS):
        of = slice(g * MEMBERS, (g + 1) * MEMBERS)
        z = z_all[g]
        eh = eh_all[g]
        el = el_all[g]
        from_z = dot_nt(jnp.concatenate([z, z], axis=1), wf_all[g])
        wb = wb_all[g]
        wb_high = wb[:, :LANES]
        from_e = dot_nt(
            jnp.concatenate([eh, el, eh], axis=1),
            jnp.concatenate([wb_high, wb_high, wb[:, LANES:]], axis=1),
        )
        inner_ref[g] = from_z[:, :LANES]
        grad_ref[g] = from_e[:, :LANES]
        for b in range(blocks):
            at = slice(b * MEMBERS, (b + 1) * MEMBERS)
            x_all[b, of, :] = from_z[at, LANES:]
            y_all[b, of, :] = from_e[at, LANES:]
        z_back = jnp.transpose(z)
        gram = dot_nn(jnp.concatenate([z_back, z_back], axis=1), jnp.concatenate([eh, el], axis=0))
        gram = jnp.where(lane_at >= row_at, gram, 0.0)
        folded = [gram[0:8]] + [
            pltpu.roll(gram[8 * r : 8 * r + 8], LANES - 8 * r, 1) for r in range(1, LANES // 8)
        ]
        while len(folded) > 1:
            folded = [folded[i] + folded[i + 1] for i in range(0, len(folded), 2)]
        fold_all[8 * g : 8 * g + 8, :] = folded[0]

    span = per_member(jnp.exp(rate_rows * (-float(LANES))))
    in_x = jnp.where((lane_row >= 48) & (lane_row < 64), float(LANES), 0.0)
    in_y = jnp.where((lane_row >= 96) & (lane_row < 112), float(LANES), 0.0)
    x_now = jnp.zeros((LANES, LANES), f32)
    y_now = jnp.zeros((LANES, LANES), f32)
    x_lag = jnp.zeros((LANES, LANES), f32)
    y_lag = jnp.zeros((LANES, LANES), f32)
    cross = jnp.zeros((LANES, LANES), f32)
    for b in range(blocks):
        own = x_all[b]
        cross = cross + x_now * pltpu.roll(y_all[b], 4 * MODES, 1)
        carry_ref[0, b] = x_now
        x_now = span * (x_now + x_lag) + own
        x_lag = span * x_lag + in_x * pltpu.roll(own, MODES, 1)
    for b in reversed(range(blocks)):
        own = y_all[b]
        carry_ref[0, b] = carry_ref[0, b] + y_now
        y_now = span * (y_now + y_lag) + own
        y_lag = span * y_lag + in_y * pltpu.roll(own, MODES, 1)
    cross_ref[...] = jnp.sum(cross.reshape(TILE_GROUPS, MEMBERS, LANES), axis=1)
    turned = jnp.transpose(x_now + y_now)
    state_ref[0:16] = turned[0:16]
    state_ref[16:32] = turned[48:64]
    state_ref[32:48] = turned[64:80]
    state_ref[48:64] = turned[96:112]

    corr = jnp.sum(
        sheared(fold_all[...], 8).reshape(TILE_GROUPS, 8, LANES), axis=1
    )
    weighted = power_all[...] * per_member(corr)
    first_col = jnp.sum(weighted, axis=1, keepdims=True)
    lag_col = jnp.sum(lag * weighted, axis=1, keepdims=True)
    packed = jnp.where(lane_at == 0, first_col, jnp.where(lane_at == 1, lag_col, 0.0))
    diag_ref[0] = jnp.transpose(packed)[0:8]


def output_kernel(
    feat_ref, halo_ref, next_ref, taps_ref, cot_ref, rate_ref, gain_ref,
    inner_ref, grad_ref, carry_ref, bound_ref,
    mixer_ref, fgrad_ref,
    wide, adj, inner_t, grad_t, left_all,
):
    tokens = feat_ref.shape[1]
    blocks = tokens // LANES
    widen(feat_ref, halo_ref, wide, tokens)
    for i in range(3):
        wide[i, 8 + tokens : 16 + tokens, :] = next_ref[i]
    rate_rows, coef_rows, rates, coefs = parameters(rate_ref, gain_ref)
    lag = iota(1, (LANES, LANES)).astype(f32)
    lane_row = iota(1, (1, LANES))
    lane_at = iota(1, (LANES, LANES))
    is_low = ((lane_at >= 16) & (lane_at < 32)) | ((lane_at >= 80) & (lane_at < 96))
    before = bound_ref[0:16]
    after = bound_ref[16:32]
    gap = jnp.zeros((MODES, LANES), f32)
    stacked = jnp.concatenate([before, before, before, gap, after, after, gap, after], axis=0)
    turned = jnp.transpose(stacked)
    none_16 = jnp.zeros((MODES, LANES), bf16)
    none_64 = jnp.zeros((4 * MODES, LANES), bf16)
    member_rates = per_member(rate_rows)
    for b in range(blocks):
        steps = jnp.where(lane_row < 64, float(b * LANES), float((blocks - 1 - b) * LANES))
        value = carry_ref[0, b] + turned * jnp.exp(-member_rates * steps)
        high = value.astype(bf16).astype(f32)
        mixed = jnp.where(is_low, value - high, value).astype(bf16)
        for g in range(TILE_GROUPS):
            left_all[g, b * MEMBERS : (b + 1) * MEMBERS, :] = mixed[
                g * MEMBERS : (g + 1) * MEMBERS
            ]
    cz_parts = split(coefs * jnp.exp(-rates * (lag + 1.0)))
    ce_parts = split(coefs * jnp.exp(-rates * (LANES - 1.0 - lag)))
    for g in range(TILE_GROUPS):
        of = slice(g * MODES, (g + 1) * MODES)
        cz_high, cz_low = cz_parts[0][of], cz_parts[1][of]
        ce_high, ce_low = ce_parts[0][of], ce_parts[1][of]
        right = jnp.concatenate(
            [
                jnp.concatenate([cz_high, cz_high, cz_low, none_16, none_64], axis=0),
                jnp.concatenate([none_64, ce_high, ce_high, none_16, ce_low], axis=0),
            ],
            axis=1,
        )
        carried = dot_nn(left_all[g], right)
        whole_inner = inner_ref[g] + carried[:, :LANES]
        whole_grad = grad_ref[g] + carried[:, LANES:]
        for b in range(blocks):
            at = slice(b * MEMBERS, (b + 1) * MEMBERS)
            inner_t[b, of, :] = whole_inner[at]
            grad_t[b, of, :] = whole_grad[at]
    for b in range(blocks):
        at = slice(b * LANES, (b + 1) * LANES)
        query = short_block(wide, taps_ref, 0, b * LANES, LANES)
        key = short_block(wide, taps_ref, 1, b * LANES, LANES)
        value = short_block(wide, taps_ref, 2, b * LANES, LANES)
        inner = jnp.transpose(inner_t[b])
        grad = jnp.transpose(grad_t[b])
        mixer_ref[at, :] = (query * inner).astype(bf16)
        adj[0, at, :] = cot_ref[at, :].astype(f32) * inner
        adj[1, at, :] = grad * value
        adj[2, at, :] = grad * key
    key = short_block(wide, taps_ref, 1, tokens, 8)
    value = short_block(wide, taps_ref, 2, tokens, 8)
    query = short_block(wide, taps_ref, 0, tokens, 8)
    z = (key * value).astype(bf16).astype(f32)
    e = next_ref[3] * query
    rates = jnp.transpose(member_rates)[0:MODES]
    coefs = jnp.transpose(per_member(coef_rows))[0:MODES]
    decay = jnp.exp(-rates)
    grow = jnp.exp(rates)
    state = bound_ref[32:48]
    sum_0 = jnp.sum(coefs, axis=0, keepdims=True)
    sum_1 = jnp.sum(coefs * decay, axis=0, keepdims=True)
    inner_0 = jnp.sum(coefs * decay * state, axis=0, keepdims=True) + sum_0 * z[0:1]
    inner_1 = (
        jnp.sum(coefs * decay * decay * state, axis=0, keepdims=True)
        + sum_1 * z[0:1]
        + sum_0 * z[1:2]
    )
    grad_0 = jnp.sum(coefs * grow * after, axis=0, keepdims=True)
    grad_1 = jnp.sum(coefs * grow * (grow * after - e[0:1]), axis=0, keepdims=True)
    which = iota(0, (8, LANES))
    inner_8 = jnp.where(which == 0, inner_0, jnp.where(which == 1, inner_1, 0.0))
    grad_8 = jnp.where(which == 0, grad_0, jnp.where(which == 1, grad_1, 0.0))
    adj[0, tokens : tokens + 8, :] = next_ref[3] * inner_8
    adj[1, tokens : tokens + 8, :] = grad_8 * value
    adj[2, tokens : tokens + 8, :] = grad_8 * key
    for b in range(blocks):
        start = b * LANES
        for i in range(3):
            fgrad_ref[i, start : start + LANES, :] = (
                taps_ref[i, 0:1, :] * adj[i, start : start + LANES, :]
                + taps_ref[i, 1:2, :] * adj[i, start + 1 : start + 1 + LANES, :]
                + taps_ref[i, 2:3, :] * adj[i, start + 2 : start + 2 + LANES, :]
            ).astype(bf16)


def shifted(value, axis, steps):
    count = lax.axis_size(axis)
    return lax.ppermute(value, axis, [(i, (i + steps) % count) for i in range(count)])


def swapped(value, axis, key):
    count = lax.axis_size(axis)
    return lax.ppermute(value, axis, [(i, i ^ key) for i in range(count)])


def per_device(features, short_taps, decay_rates, mode_gains, cotangent):
    tokens = features.shape[1]
    channels = features.shape[2]
    groups = decay_rates.shape[0]
    tiles = channels // LANES
    blocks = tokens // LANES
    ctx_count = lax.axis_size("ctx")
    ctx_index = lax.axis_index("ctx")

    tail = shifted(features[:, tokens - 2 :, :], "ctx", 1).astype(f32)
    tail = jnp.where(ctx_index == 0, 0.0, tail)
    halo = jnp.pad(tail, ((0, 0), (6, 0), (0, 0)))
    head = jnp.concatenate([features[:, :2, :], cotangent[None, :2, :]], axis=0)
    ahead = shifted(head, "ctx", -1).astype(f32)
    ahead = jnp.where(ctx_index == ctx_count - 1, 0.0, ahead)
    ahead = jnp.pad(ahead, ((0, 0), (0, 6), (0, 0)))

    mode_coefs = mode_gains * jnp.sqrt(2.0 * decay_rates)
    rate_cols = jnp.repeat(decay_rates.T, MEMBERS, axis=1)

    per_group = pl.BlockSpec((TILE_GROUPS, ROWS, LANES), lambda j: (j, 0, 0))
    feat_spec = pl.BlockSpec((3, tokens, LANES), lambda j: (0, 0, j))
    halo_spec = pl.BlockSpec((3, 8, LANES), lambda j: (0, 0, j))
    taps_spec = pl.BlockSpec((3, 3, LANES), lambda j: (0, 0, j))
    cot_spec = pl.BlockSpec((tokens, LANES), lambda j: (0, j))
    rate_spec = pl.BlockSpec((TILE_GROUPS, MODES), lambda j: (j, 0))
    carry_spec = pl.BlockSpec((1, blocks, LANES, LANES), lambda j: (j, 0, 0, 0))
    rows = blocks * MEMBERS
    big = jax.ShapeDtypeStruct((groups, rows, LANES), f32)
    inner, grad, carry, states, diag, cross = pl.pallas_call(
        local_kernel,
        grid=(tiles,),
        in_specs=[feat_spec, halo_spec, taps_spec, cot_spec, rate_spec, rate_spec],
        out_specs=[
            per_group,
            per_group,
            carry_spec,
            pl.BlockSpec((4 * MODES, LANES), lambda j: (0, j)),
            pl.BlockSpec((1, 8, LANES), lambda j: (j, 0, 0)),
            pl.BlockSpec((TILE_GROUPS, LANES), lambda j: (j, 0)),
        ],
        out_shape=[
            big,
            big,
            jax.ShapeDtypeStruct((tiles, blocks, LANES, LANES), f32),
            jax.ShapeDtypeStruct((4 * MODES, channels), f32),
            jax.ShapeDtypeStruct((tiles, 8, LANES), f32),
            jax.ShapeDtypeStruct((groups, LANES), f32),
        ],
        scratch_shapes=[
            pltpu.VMEM((3, tokens + 8, LANES), f32),
            pltpu.VMEM((TILE_GROUPS, rows, LANES), bf16),
            pltpu.VMEM((TILE_GROUPS, rows, LANES), bf16),
            pltpu.VMEM((TILE_GROUPS, rows, LANES), bf16),
            pltpu.VMEM((TILE_GROUPS, 2 * LANES, 2 * LANES), bf16),
            pltpu.VMEM((TILE_GROUPS, 2 * LANES, 2 * LANES), bf16),
            pltpu.VMEM((blocks, LANES, LANES), f32),
            pltpu.VMEM((blocks, LANES, LANES), f32),
            pltpu.VMEM((LANES, LANES), f32),
            pltpu.VMEM((8 * TILE_GROUPS, LANES), f32),
        ],
        compiler_params=pltpu.CompilerParams(vmem_limit_bytes=40 * 2**20),
        name="local_part",
    )(features, halo, short_taps, cotangent, decay_rates, mode_gains)

    ends, lagged, moment_0, moment_1 = (
        states[0:16],
        states[16:32],
        states[32:48],
        states[48:64],
    )
    s_prev = jnp.zeros_like(ends)
    l_prev = jnp.zeros_like(ends)
    e_next = jnp.zeros_like(ends)
    for key in range(1, ctx_count):
        other = ctx_index ^ key
        earlier = other < ctx_index
        sent = jnp.where(earlier, states[32:64], states[0:32])
        got = swapped(sent, "ctx", key)
        away = (jnp.abs(ctx_index - other) - 1).astype(f32) * tokens
        weight = jnp.exp(-rate_cols * away)
        s_part = weight * got[:16]
        s_prev = s_prev + jnp.where(earlier, s_part, 0.0)
        l_prev = l_prev + jnp.where(earlier, weight * got[16:] + away * s_part, 0.0)
        e_next = e_next + jnp.where(earlier, 0.0, s_part)
    own_end = ends + jnp.exp(-rate_cols * tokens) * s_prev
    bound = jnp.concatenate([s_prev, e_next, own_end], axis=0)

    summed_first = (moment_0 * s_prev).reshape(MODES, groups, MEMBERS).sum(axis=2).T
    summed_lag = (
        (moment_1 * s_prev + moment_0 * l_prev).reshape(MODES, groups, MEMBERS).sum(axis=2).T
    )
    diag = [diag[:, i, :].reshape(groups, MODES) for i in range(2)]
    first_total = diag[0] + cross[:, 0:16] + summed_first
    lag_total = -(diag[1] + cross[:, 32:48] + cross[:, 48:64] + summed_lag)
    gain_part = jnp.sqrt(2.0 * decay_rates) * first_total
    rate_part = mode_coefs * (0.5 * first_total + decay_rates * lag_total)
    local = jnp.stack([gain_part, rate_part])
    terms = [local] + [swapped(local, "ctx", key) for key in range(1, ctx_count)]
    while len(terms) > 1:
        terms = [terms[i] + terms[i + 1] for i in range(0, len(terms), 2)]
    summed = terms[0]
    squares = jnp.broadcast_to(jnp.sum(summed * summed), (8, LANES))
    fsdp_count = lax.axis_size("fsdp")
    step = 1
    while step < fsdp_count:
        squares = squares + swapped(squares, "fsdp", step)
        step *= 2
    entry_count = 2 * groups * MODES * fsdp_count
    factor = jnp.minimum(1.0, lax.rsqrt(squares[0, 0] / entry_count + 1e-06))
    clipped = summed * factor

    mixer, feature_grads = pl.pallas_call(
        output_kernel,
        grid=(tiles,),
        in_specs=[
            feat_spec,
            halo_spec,
            pl.BlockSpec((4, 8, LANES), lambda j: (0, 0, j)),
            taps_spec,
            cot_spec,
            rate_spec,
            rate_spec,
            per_group,
            per_group,
            carry_spec,
            pl.BlockSpec((3 * MODES, LANES), lambda j: (0, j)),
        ],
        out_specs=[cot_spec, feat_spec],
        out_shape=[
            jax.ShapeDtypeStruct((tokens, channels), bf16),
            jax.ShapeDtypeStruct((3, tokens, channels), bf16),
        ],
        scratch_shapes=[
            pltpu.VMEM((3, tokens + 16, LANES), f32),
            pltpu.VMEM((3, tokens + 8, LANES), f32),
            pltpu.VMEM((blocks, LANES, LANES), f32),
            pltpu.VMEM((blocks, LANES, LANES), f32),
            pltpu.VMEM((TILE_GROUPS, rows, LANES), bf16),
        ],
        compiler_params=pltpu.CompilerParams(vmem_limit_bytes=40 * 2**20),
        name="output_part",
    )(
        features, halo, ahead, short_taps, cotangent, decay_rates, mode_gains,
        inner, grad, carry, bound,
    )
    return (mixer, feature_grads, clipped[0], clipped[1])


def solution(mesh):
    return jax.shard_map(
        per_device,
        mesh=mesh,
        in_specs=(
            P(None, "ctx", "fsdp"),
            P(None, None, "fsdp"),
            P("fsdp", None),
            P("fsdp", None),
            P("ctx", "fsdp"),
        ),
        out_specs=(P("ctx", "fsdp"), P(None, "ctx", "fsdp"), P("fsdp", None), P("fsdp", None)),
        check_vma=False,
    )
```

```python
import functools

import jax
import jax.numpy as jnp
from jax import lax
from jax.experimental import pallas as pl
from jax.experimental.pallas import tpu as pltpu
from jax.sharding import PartitionSpec as P

LANES = 128
MODES = 16
MEMBERS = 16
TILE_GROUPS = LANES // MEMBERS
ROWS = LANES
f32 = jnp.float32
bf16 = jnp.bfloat16
VMEM_LIMIT = 58 * 2**20


def split(value):
    high = value.astype(bf16)
    return high, (value - high.astype(f32)).astype(bf16)


def dot_nt(left, right):
    return lax.dot_general(left, right, (((1,), (1,)), ((), ())), preferred_element_type=f32)


def dot_tn(left, right):
    return lax.dot_general(left, right, (((0,), (0,)), ((), ())), preferred_element_type=f32)


def dot_nn(left, right):
    return lax.dot_general(left, right, (((1,), (0,)), ((), ())), preferred_element_type=f32)


def iota(axis, shape):
    return lax.broadcasted_iota(jnp.int32, shape, axis)


def widen(feat_ref, tail_ref, me_ref, wide, tokens):
    for i in range(3):
        wide[i, 6:8, :] = jnp.where(me_ref[0] == 0, 0.0, tail_ref[i].astype(f32))
        wide[i, 8 : 8 + tokens, :] = feat_ref[i].astype(f32)


def short_block(wide, taps_ref, i, start, count):
    return (
        taps_ref[i, 0:1, :] * wide[i, start + 8 : start + 8 + count, :]
        + taps_ref[i, 1:2, :] * wide[i, start + 7 : start + 7 + count, :]
        + taps_ref[i, 2:3, :] * wide[i, start + 6 : start + 6 + count, :]
    )


def sheared(row8, period):
    which = iota(0, row8.shape) % period
    for bit in (1, 2, 4):
        row8 = jnp.where((which & bit) != 0, pltpu.roll(row8, LANES - bit, 1), row8)
    return row8


def circulant(row):
    return pltpu.roll(jnp.broadcast_to(row, (LANES, LANES)), 0, 1, stride=1, stride_axis=0)


def table_rows(source_ref, rows_ref):
    tall = jnp.concatenate([source_ref[...]] * (LANES // MODES), axis=0)
    missing = LANES - tall.shape[1]
    if missing:
        tall = jnp.concatenate([tall, jnp.zeros((LANES, missing), f32)], axis=1)
    rows_ref[...] = jnp.transpose(tall)


def parameters(rate_ref, gain_ref, rate_rows, gain_rows):
    tile = pl.program_id(0)

    @pl.when(tile == 0)
    def _():
        table_rows(rate_ref, rate_rows)
        table_rows(gain_ref, gain_rows)

    at = pl.ds(pl.multiple_of(tile * TILE_GROUPS, TILE_GROUPS), TILE_GROUPS)
    rates = rate_rows[at, :]
    return rates, gain_rows[at, :] * jnp.sqrt(2.0 * rates)


def per_mode(rows):
    own = iota(0, (TILE_GROUPS, LANES)) == iota(1, (TILE_GROUPS, LANES)) // MODES
    flat = jnp.sum(jnp.where(own, rows, 0.0), axis=0, keepdims=True)
    return jnp.transpose(jnp.broadcast_to(flat, (LANES, LANES)))


def per_member(rows):
    return jnp.concatenate(
        [jnp.broadcast_to(rows[g : g + 1], (MEMBERS, LANES)) for g in range(TILE_GROUPS)], axis=0
    )


def state_kernel(
    me_ref, feat_ref, tail_ref, taps_ref, cot_ref, rate_ref, gain_ref,
    z_ref, eh_ref, el_ref, carry_ref, state_ref, cross_ref,
    wide, own_all, table_all, rate_rows, gain_rows,
):
    tokens = feat_ref.shape[1]
    blocks = tokens // LANES
    rate_tile, _ = parameters(rate_ref, gain_ref, rate_rows, gain_rows)
    rates = per_mode(rate_tile)
    lag = iota(1, (LANES, LANES)).astype(f32)
    lane_at = iota(1, (LANES, LANES))
    lane_row = iota(1, (1, LANES))

    back = jnp.exp(-rates * (LANES - 1.0 - lag))
    after = jnp.exp(-rates * (lag + 1.0))
    s_parts = split(back)
    l_parts = split((LANES - 1.0 - lag) * back)
    m_parts = split(after)
    n_parts = split((lag + 1.0) * after)
    for g in range(TILE_GROUPS):
        of = slice(g * MODES, (g + 1) * MODES)
        for part in range(2):
            s_of, l_of = s_parts[part][of], l_parts[part][of]
            m_of, n_of = m_parts[part][of], n_parts[part][of]
            table_all[g, :, part * LANES : (part + 1) * LANES] = jnp.concatenate(
                [s_of, s_of, s_of, l_of, m_of, m_of, n_of, m_of], axis=0
            )

    widen(feat_ref, tail_ref, me_ref, wide, tokens)
    for b in range(blocks):
        query = short_block(wide, taps_ref, 0, b * LANES, LANES)
        key = short_block(wide, taps_ref, 1, b * LANES, LANES)
        value = short_block(wide, taps_ref, 2, b * LANES, LANES)
        z_t = jnp.transpose((key * value).astype(bf16))
        e_t = jnp.transpose(cot_ref[b * LANES : (b + 1) * LANES, :].astype(f32) * query)
        e_high, e_low = split(e_t)
        at = slice(b * MEMBERS, (b + 1) * MEMBERS)
        for g in range(TILE_GROUPS):
            of = slice(g * MEMBERS, (g + 1) * MEMBERS)
            z_ref[g, at, :] = z_t[of]
            eh_ref[g, at, :] = e_high[of]
            el_ref[g, at, :] = e_low[of]

    for g in range(TILE_GROUPS):
        of = slice(g * MEMBERS, (g + 1) * MEMBERS)
        z, eh, el = z_ref[g], eh_ref[g], el_ref[g]
        left = jnp.concatenate(
            [
                jnp.concatenate([z, z], axis=1),
                jnp.concatenate([eh, eh], axis=1),
                jnp.concatenate([el, jnp.zeros_like(el)], axis=1),
            ],
            axis=0,
        )
        got = dot_nt(left, table_all[g])
        rows = z.shape[0]
        own = jnp.where(
            iota(1, (rows, LANES)) < 64, got[:rows], got[rows : 2 * rows] + got[2 * rows :]
        )
        for b in range(blocks):
            own_all[b, of, :] = own[b * MEMBERS : (b + 1) * MEMBERS]

    span = per_member(jnp.exp(rate_tile * (-float(LANES))))
    in_x = jnp.where((lane_row >= 48) & (lane_row < 64), float(LANES), 0.0)
    in_y = jnp.where((lane_row >= 96) & (lane_row < 112), float(LANES), 0.0)
    x_now = jnp.zeros((LANES, LANES), f32)
    y_now = jnp.zeros((LANES, LANES), f32)
    x_lag = jnp.zeros((LANES, LANES), f32)
    y_lag = jnp.zeros((LANES, LANES), f32)
    cross = jnp.zeros((LANES, LANES), f32)
    for b in range(blocks):
        own = own_all[b]
        cross = cross + x_now * pltpu.roll(own, 4 * MODES, 1)
        carry_ref[0, b] = x_now
        x_now = span * (x_now + x_lag) + own
        x_lag = span * x_lag + in_x * pltpu.roll(own, MODES, 1)
    for b in reversed(range(blocks)):
        own = own_all[b]
        carry_ref[0, b] = jnp.where(lane_at < 64, carry_ref[0, b], y_now)
        y_now = span * (y_now + y_lag) + own
        y_lag = span * y_lag + in_y * pltpu.roll(own, MODES, 1)
    cross_ref[...] = jnp.sum(cross.reshape(TILE_GROUPS, MEMBERS, LANES), axis=1)
    turned = jnp.transpose(jnp.where(lane_at < 64, x_now, y_now))
    state_ref[0:16] = turned[0:16]
    state_ref[16:32] = turned[48:64]
    state_ref[32:48] = turned[64:80]
    state_ref[48:64] = turned[96:112]


def inside_kernel(
    z_ref, eh_ref, el_ref, rate_ref, gain_ref,
    inner_ref, grad_ref, diag_ref,
    toep_all, power_all, fold_all, rate_rows, gain_rows,
):
    rate_tile, coef_tile = parameters(rate_ref, gain_ref, rate_rows, gain_rows)
    rates, coefs = per_mode(rate_tile), per_mode(coef_tile)
    lag = iota(1, (LANES, LANES)).astype(f32)
    row_at = iota(0, (LANES, LANES))
    lane_at = iota(1, (LANES, LANES))
    power = jnp.exp(-rates * lag)
    power_all[...] = power
    taps = jnp.sum((coefs * power).reshape(TILE_GROUPS, MODES, LANES), axis=1)
    for g in range(TILE_GROUPS):
        high, low = split(jnp.where(lane_at >= row_at, circulant(taps[g : g + 1]), 0.0))
        toep_all[g, 0:LANES, :] = high
        toep_all[g, LANES:, :] = low
    for g in range(TILE_GROUPS):
        z, eh, el = z_ref[g], eh_ref[g], el_ref[g]
        high = toep_all[g, 0:LANES, :]
        inner_ref[g] = dot_nn(jnp.concatenate([z, z], axis=1), toep_all[g])
        grad_ref[g] = dot_nt(
            jnp.concatenate([eh, el, eh], axis=1),
            jnp.concatenate([high, high, toep_all[g, LANES:, :]], axis=1),
        )
        z_back = jnp.transpose(z)
        gram = dot_nn(jnp.concatenate([z_back, z_back], axis=1), jnp.concatenate([eh, el], axis=0))
        gram = jnp.where(lane_at >= row_at, gram, 0.0)
        folded = [gram[0:8]] + [
            pltpu.roll(gram[8 * r : 8 * r + 8], LANES - 8 * r, 1) for r in range(1, LANES // 8)
        ]
        while len(folded) > 1:
            folded = [folded[i] + folded[i + 1] for i in range(0, len(folded), 2)]
        fold_all[8 * g : 8 * g + 8, :] = folded[0]

    corr = jnp.sum(sheared(fold_all[...], 8).reshape(TILE_GROUPS, 8, LANES), axis=1)
    weighted = power_all[...] * per_member(corr)
    first_col = jnp.sum(weighted, axis=1, keepdims=True)
    lag_col = jnp.sum(lag * weighted, axis=1, keepdims=True)
    mode_at = row_at % MODES
    placed = jnp.where(lane_at == mode_at, first_col, 0.0) + jnp.where(
        lane_at == mode_at + 32, lag_col, 0.0
    )
    diag_ref[...] = jnp.sum(placed.reshape(TILE_GROUPS, MODES, LANES), axis=1)


def exact_dot(left, right, dims):
    return lax.dot_general(
        left, right, (dims, ((), ())), precision=lax.Precision.HIGHEST, preferred_element_type=f32
    )


def join_kernel(tokens, me_ref, state_ref, diag_ref, cross_ref, rate_ref, gain_ref, *refs):
    gots, (bound_ref, local_ref) = refs[:-2], refs[-2:]
    me = me_ref[0]
    channels = state_ref.shape[1]
    groups = rate_ref.shape[1]
    chosen = (iota(0, (groups, channels)) == iota(1, (groups, channels)) // MEMBERS).astype(f32)
    rates = rate_ref[...]
    rate_cols = exact_dot(rates, chosen, ((1,), (0,)))
    zero = jnp.zeros((MODES, channels), f32)
    s_prev, l_prev, e_next = zero, zero, zero
    ahead = jnp.zeros((8, channels), f32)
    for key, got in enumerate(gots, 1):
        other = me ^ key
        earlier = other < me
        away = ((jnp.abs(me - other) - 1) * tokens).astype(f32)
        weight = jnp.exp(-rate_cols * away)
        part = weight * got[0:16]
        s_prev = s_prev + jnp.where(earlier, part, 0.0)
        l_prev = l_prev + jnp.where(earlier, weight * got[16:32] + away * part, 0.0)
        e_next = e_next + jnp.where(earlier, 0.0, part)
        ahead = ahead + jnp.where(other == me + 1, got[32:40], 0.0)
    bound_ref[0:16] = s_prev
    bound_ref[16:32] = e_next
    bound_ref[32:48] = state_ref[0:16] + jnp.exp(-rate_cols * float(tokens)) * s_prev
    bound_ref[48:56] = ahead
    moment_0, moment_1 = state_ref[32:48], state_ref[48:64]
    terms = jnp.concatenate([moment_0 * s_prev, moment_1 * s_prev + moment_0 * l_prev], axis=0)
    sums = exact_dot(terms, chosen, ((1,), (1,)))
    own = jnp.transpose(cross_ref[...] + diag_ref[...])
    first = sums[0:16] + own[0:16]
    lagged = -(sums[16:32] + own[32:48] + own[48:64])
    root = jnp.sqrt(2.0 * rates)
    local_ref[0:16] = root * first
    local_ref[16:32] = gain_ref[...] * root * (0.5 * first + rates * lagged)


def output_kernel(
    me_ref, feat_ref, tail_ref, taps_ref, cot_ref, rate_ref, gain_ref,
    inner_ref, grad_ref, carry_ref, bound_ref,
    mixer_ref, fgrad_ref,
    wide, adj, inner_t, grad_t, left_all, rate_rows, gain_rows,
):
    tokens = feat_ref.shape[1]
    blocks = tokens // LANES
    widen(feat_ref, tail_ref, me_ref, wide, tokens)
    for i in range(3):
        wide[i, 8 + tokens : 16 + tokens, :] = jnp.zeros((8, LANES), f32)
        wide[i, 8 + tokens : 10 + tokens, :] = bound_ref[48 + 2 * i : 50 + 2 * i]
    rate_tile, coef_tile = parameters(rate_ref, gain_ref, rate_rows, gain_rows)
    rates, coefs = per_mode(rate_tile), per_mode(coef_tile)
    lag = iota(1, (LANES, LANES)).astype(f32)
    lane_row = iota(1, (1, LANES))
    lane_at = iota(1, (LANES, LANES))
    is_low = ((lane_at >= 16) & (lane_at < 32)) | ((lane_at >= 80) & (lane_at < 96))
    before = bound_ref[0:16]
    after = bound_ref[16:32]
    gap = jnp.zeros((MODES, LANES), f32)
    stacked = jnp.concatenate([before, before, before, gap, after, after, gap, after], axis=0)
    turned = jnp.transpose(stacked)
    none_16 = jnp.zeros((MODES, LANES), bf16)
    none_64 = jnp.zeros((4 * MODES, LANES), bf16)
    member_rates = per_member(rate_tile)
    for b in range(blocks):
        steps = jnp.where(lane_row < 64, float(b * LANES), float((blocks - 1 - b) * LANES))
        value = carry_ref[0, b] + turned * jnp.exp(-member_rates * steps)
        high = value.astype(bf16).astype(f32)
        mixed = jnp.where(is_low, value - high, value).astype(bf16)
        for g in range(TILE_GROUPS):
            left_all[g, b * MEMBERS : (b + 1) * MEMBERS, :] = mixed[
                g * MEMBERS : (g + 1) * MEMBERS
            ]
    cz_parts = split(coefs * jnp.exp(-rates * (lag + 1.0)))
    ce_parts = split(coefs * jnp.exp(-rates * (LANES - 1.0 - lag)))
    for g in range(TILE_GROUPS):
        of = slice(g * MODES, (g + 1) * MODES)
        cz_high, cz_low = cz_parts[0][of], cz_parts[1][of]
        ce_high, ce_low = ce_parts[0][of], ce_parts[1][of]
        right = jnp.concatenate(
            [
                jnp.concatenate([cz_high, cz_high, cz_low, none_16, none_64], axis=0),
                jnp.concatenate([none_64, ce_high, ce_high, none_16, ce_low], axis=0),
            ],
            axis=1,
        )
        carried = dot_nn(left_all[g], right)
        whole_inner = inner_ref[g] + carried[:, :LANES]
        whole_grad = grad_ref[g] + carried[:, LANES:]
        for b in range(blocks):
            at = slice(b * MEMBERS, (b + 1) * MEMBERS)
            inner_t[b, of, :] = whole_inner[at]
            grad_t[b, of, :] = whole_grad[at]
    for b in range(blocks):
        at = slice(b * LANES, (b + 1) * LANES)
        query = short_block(wide, taps_ref, 0, b * LANES, LANES)
        key = short_block(wide, taps_ref, 1, b * LANES, LANES)
        value = short_block(wide, taps_ref, 2, b * LANES, LANES)
        inner = jnp.transpose(inner_t[b])
        grad = jnp.transpose(grad_t[b])
        mixer_ref[at, :] = (query * inner).astype(bf16)
        adj[0, at, :] = cot_ref[at, :].astype(f32) * inner
        adj[1, at, :] = grad * value
        adj[2, at, :] = grad * key
    key = short_block(wide, taps_ref, 1, tokens, 8)
    value = short_block(wide, taps_ref, 2, tokens, 8)
    query = short_block(wide, taps_ref, 0, tokens, 8)
    z = (key * value).astype(bf16).astype(f32)
    upstream = jnp.concatenate([bound_ref[54:56], jnp.zeros((6, LANES), f32)], axis=0)
    e = upstream * query
    rates = jnp.transpose(member_rates)[0:MODES]
    coefs = jnp.transpose(per_member(coef_tile))[0:MODES]
    decay = jnp.exp(-rates)
    grow = jnp.exp(rates)
    state = bound_ref[32:48]
    sum_0 = jnp.sum(coefs, axis=0, keepdims=True)
    sum_1 = jnp.sum(coefs * decay, axis=0, keepdims=True)
    inner_0 = jnp.sum(coefs * decay * state, axis=0, keepdims=True) + sum_0 * z[0:1]
    inner_1 = (
        jnp.sum(coefs * decay * decay * state, axis=0, keepdims=True)
        + sum_1 * z[0:1]
        + sum_0 * z[1:2]
    )
    grad_0 = jnp.sum(coefs * grow * after, axis=0, keepdims=True)
    grad_1 = jnp.sum(coefs * grow * (grow * after - e[0:1]), axis=0, keepdims=True)
    which = iota(0, (8, LANES))
    inner_8 = jnp.where(which == 0, inner_0, jnp.where(which == 1, inner_1, 0.0))
    grad_8 = jnp.where(which == 0, grad_0, jnp.where(which == 1, grad_1, 0.0))
    adj[0, tokens : tokens + 8, :] = upstream * inner_8
    adj[1, tokens : tokens + 8, :] = grad_8 * value
    adj[2, tokens : tokens + 8, :] = grad_8 * key
    for b in range(blocks):
        start = b * LANES
        for i in range(3):
            fgrad_ref[i, start : start + LANES, :] = (
                taps_ref[i, 0:1, :] * adj[i, start : start + LANES, :]
                + taps_ref[i, 1:2, :] * adj[i, start + 1 : start + 1 + LANES, :]
                + taps_ref[i, 2:3, :] * adj[i, start + 2 : start + 2 + LANES, :]
            ).astype(bf16)


def shifted(value, axis, steps):
    count = lax.axis_size(axis)
    return lax.ppermute(value, axis, [(i, (i + steps) % count) for i in range(count)])


def swapped(value, axis, key):
    count = lax.axis_size(axis)
    return lax.ppermute(value, axis, [(i, i ^ key) for i in range(count)])


def per_device(features, short_taps, decay_rates, mode_gains, cotangent):
    tokens = features.shape[1]
    channels = features.shape[2]
    groups = decay_rates.shape[0]
    tiles = channels // LANES
    blocks = tokens // LANES
    ctx_count = lax.axis_size("ctx")
    ctx_index = lax.axis_index("ctx")

    tail = shifted(features[:, tokens - 2 :, :], "ctx", 1)
    head = jnp.concatenate([features[:, :2, :], cotangent[None, :2, :]], axis=0)
    head = head.astype(f32).reshape(8, channels)
    me = ctx_index.astype(jnp.int32).reshape(1)
    rates, gains = decay_rates.T, mode_gains.T

    per_group = pl.BlockSpec((TILE_GROUPS, ROWS, LANES), lambda j: (j, 0, 0))
    feat_spec = pl.BlockSpec((3, tokens, LANES), lambda j: (0, 0, j))
    tail_spec = pl.BlockSpec((3, 2, LANES), lambda j: (0, 0, j))
    taps_spec = pl.BlockSpec((3, 3, LANES), lambda j: (0, 0, j))
    cot_spec = pl.BlockSpec((tokens, LANES), lambda j: (0, j))
    table_spec = pl.BlockSpec((MODES, groups), lambda j: (0, 0))
    carry_spec = pl.BlockSpec((1, blocks, LANES, LANES), lambda j: (j, 0, 0, 0))
    slot_spec = pl.BlockSpec((TILE_GROUPS, LANES), lambda j: (j, 0))
    me_spec = pl.BlockSpec(memory_space=pltpu.SMEM)
    rows = blocks * MEMBERS
    turned = jax.ShapeDtypeStruct((groups, rows, LANES), bf16)
    wide_turned = jax.ShapeDtypeStruct((groups, rows, LANES), f32)
    slots = jax.ShapeDtypeStruct((groups, LANES), f32)
    table_scratch = [pltpu.VMEM((LANES, LANES), f32), pltpu.VMEM((LANES, LANES), f32)]
    compiler_params = pltpu.CompilerParams(vmem_limit_bytes=VMEM_LIMIT)
    z, eh, el, carry, states, cross = pl.pallas_call(
        state_kernel,
        grid=(tiles,),
        in_specs=[me_spec, feat_spec, tail_spec, taps_spec, cot_spec, table_spec, table_spec],
        out_specs=[
            per_group,
            per_group,
            per_group,
            carry_spec,
            pl.BlockSpec((4 * MODES, LANES), lambda j: (0, j)),
            slot_spec,
        ],
        out_shape=[
            turned,
            turned,
            turned,
            jax.ShapeDtypeStruct((tiles, blocks, LANES, LANES), f32),
            jax.ShapeDtypeStruct((4 * MODES, channels), f32),
            slots,
        ],
        scratch_shapes=[
            pltpu.VMEM((3, tokens + 8, LANES), f32),
            pltpu.VMEM((blocks, LANES, LANES), f32),
            pltpu.VMEM((TILE_GROUPS, LANES, 2 * LANES), bf16),
        ]
        + table_scratch,
        compiler_params=compiler_params,
        name="state_part",
    )(me, features, tail, short_taps, cotangent, rates, gains)

    gots = []
    for key in range(1, ctx_count):
        earlier = (ctx_index ^ key) < ctx_index
        sent = jnp.where(earlier, states[32:64], states[0:32])
        gots.append(swapped(jnp.concatenate([sent, head], axis=0), "ctx", key))

    inner, grad, diag = pl.pallas_call(
        inside_kernel,
        grid=(tiles,),
        in_specs=[per_group, per_group, per_group, table_spec, table_spec],
        out_specs=[per_group, per_group, slot_spec],
        out_shape=[wide_turned, wide_turned, slots],
        scratch_shapes=[
            pltpu.VMEM((TILE_GROUPS, 2 * LANES, LANES), bf16),
            pltpu.VMEM((LANES, LANES), f32),
            pltpu.VMEM((8 * TILE_GROUPS, LANES), f32),
        ]
        + table_scratch,
        compiler_params=compiler_params,
        cost_estimate=pl.CostEstimate(
            flops=2 * groups * rows * LANES * LANES * 7, bytes_accessed=14 * 2**20, transcendentals=0
        ),
        name="inside_part",
    )(z, eh, el, rates, gains)

    whole = pl.BlockSpec(memory_space=pltpu.VMEM)
    bound, local = pl.pallas_call(
        functools.partial(join_kernel, tokens),
        in_specs=[me_spec] + [whole] * (5 + len(gots)),
        out_specs=[whole, whole],
        out_shape=[
            jax.ShapeDtypeStruct((56, channels), f32),
            jax.ShapeDtypeStruct((2 * MODES, groups), f32),
        ],
        compiler_params=compiler_params,
        name="join_part",
    )(me, states, diag, cross, rates, gains, *gots)

    terms = [local] + [swapped(local, "ctx", key) for key in range(1, ctx_count)]
    while len(terms) > 1:
        terms = [terms[i] + terms[i + 1] for i in range(0, len(terms), 2)]
    summed = terms[0]
    squares = jnp.broadcast_to(jnp.sum(summed * summed), (8, LANES))
    fsdp_count = lax.axis_size("fsdp")
    step = 1
    while step < fsdp_count:
        squares = squares + swapped(squares, "fsdp", step)
        step *= 2
    entry_count = 2 * groups * MODES * fsdp_count
    factor = jnp.minimum(1.0, lax.rsqrt(squares[0, 0] / entry_count + 1e-06))
    clipped = summed * factor

    mixer, feature_grads = pl.pallas_call(
        output_kernel,
        grid=(tiles,),
        in_specs=[
            me_spec,
            feat_spec,
            tail_spec,
            taps_spec,
            cot_spec,
            table_spec,
            table_spec,
            per_group,
            per_group,
            carry_spec,
            pl.BlockSpec((56, LANES), lambda j: (0, j)),
        ],
        out_specs=[cot_spec, feat_spec],
        out_shape=[
            jax.ShapeDtypeStruct((tokens, channels), bf16),
            jax.ShapeDtypeStruct((3, tokens, channels), bf16),
        ],
        scratch_shapes=[
            pltpu.VMEM((3, tokens + 16, LANES), f32),
            pltpu.VMEM((3, tokens + 8, LANES), f32),
            pltpu.VMEM((blocks, LANES, LANES), f32),
            pltpu.VMEM((blocks, LANES, LANES), f32),
            pltpu.VMEM((TILE_GROUPS, rows, LANES), bf16),
        ]
        + table_scratch,
        compiler_params=compiler_params,
        cost_estimate=pl.CostEstimate(
            flops=2 * groups * rows * LANES * LANES * 4, bytes_accessed=28 * 2**20, transcendentals=0
        ),
        name="output_part",
    )(me, features, tail, short_taps, cotangent, rates, gains, inner, grad, carry, bound)
    return (mixer, feature_grads, clipped[:MODES].T, clipped[MODES:].T)


def solution(mesh):
    return jax.shard_map(
        per_device,
        mesh=mesh,
        in_specs=(
            P(None, "ctx", "fsdp"),
            P(None, None, "fsdp"),
            P("fsdp", None),
            P("fsdp", None),
            P("ctx", "fsdp"),
        ),
        out_specs=(P("ctx", "fsdp"), P(None, "ctx", "fsdp"), P("fsdp", None), P("fsdp", None)),
        check_vma=False,
    )
```

```python
import functools

import jax
import jax.numpy as jnp
from jax import lax
from jax.experimental import pallas as pl
from jax.experimental.pallas import tpu as pltpu
from jax.sharding import PartitionSpec as P

LANES = 128
MODES = 16
MEMBERS = 16
TILE_GROUPS = LANES // MEMBERS
ROWS = LANES
f32 = jnp.float32
bf16 = jnp.bfloat16


def split(value):
    high = value.astype(bf16)
    return high, (value - high.astype(f32)).astype(bf16)


def dot_nt(left, right):
    return lax.dot_general(left, right, (((1,), (1,)), ((), ())), preferred_element_type=f32)


def dot_tn(left, right):
    return lax.dot_general(left, right, (((0,), (0,)), ((), ())), preferred_element_type=f32)


def dot_nn(left, right):
    return lax.dot_general(left, right, (((1,), (0,)), ((), ())), preferred_element_type=f32)


def iota(axis, shape):
    return lax.broadcasted_iota(jnp.int32, shape, axis)


def widen(feat_ref, tail_ref, me_ref, wide, tokens):
    for i in range(3):
        wide[i, 6:8, :] = jnp.where(me_ref[0] == 0, 0.0, tail_ref[i].astype(f32))
        wide[i, 8 : 8 + tokens, :] = feat_ref[i].astype(f32)


def short_block(wide, taps_ref, i, start, count):
    return (
        taps_ref[i, 0:1, :] * wide[i, start + 8 : start + 8 + count, :]
        + taps_ref[i, 1:2, :] * wide[i, start + 7 : start + 7 + count, :]
        + taps_ref[i, 2:3, :] * wide[i, start + 6 : start + 6 + count, :]
    )


def sheared(row8, period):
    which = iota(0, row8.shape) % period
    for bit in (1, 2, 4):
        row8 = jnp.where((which & bit) != 0, pltpu.roll(row8, LANES - bit, 1), row8)
    return row8


def circulant(row):
    return pltpu.roll(jnp.broadcast_to(row, (LANES, LANES)), 0, 1, stride=1, stride_axis=0)


def table_rows(source_ref, rows_ref):
    tall = jnp.concatenate([source_ref[...]] * (LANES // MODES), axis=0)
    missing = LANES - tall.shape[1]
    if missing:
        tall = jnp.concatenate([tall, jnp.zeros((LANES, missing), f32)], axis=1)
    rows_ref[...] = jnp.transpose(tall)


def parameters(rate_ref, gain_ref, rate_rows, gain_rows):
    tile = pl.program_id(0)

    @pl.when(tile == 0)
    def _():
        table_rows(rate_ref, rate_rows)
        table_rows(gain_ref, gain_rows)

    at = pl.ds(pl.multiple_of(tile * TILE_GROUPS, TILE_GROUPS), TILE_GROUPS)
    rates = rate_rows[at, :]
    return rates, gain_rows[at, :] * jnp.sqrt(2.0 * rates)


def per_mode(rows):
    own = iota(0, (TILE_GROUPS, LANES)) == iota(1, (TILE_GROUPS, LANES)) // MODES
    flat = jnp.sum(jnp.where(own, rows, 0.0), axis=0, keepdims=True)
    return jnp.transpose(jnp.broadcast_to(flat, (LANES, LANES)))


def per_member(rows):
    return jnp.concatenate(
        [jnp.broadcast_to(rows[g : g + 1], (MEMBERS, LANES)) for g in range(TILE_GROUPS)], axis=0
    )


def state_kernel(
    me_ref, feat_ref, tail_ref, taps_ref, cot_ref, rate_ref, gain_ref,
    z_ref, eh_ref, el_ref, carry_ref, state_ref, cross_ref,
    wide, own_all, table_all, rate_rows, gain_rows,
):
    tokens = feat_ref.shape[1]
    blocks = tokens // LANES
    rate_tile, _ = parameters(rate_ref, gain_ref, rate_rows, gain_rows)
    rates = per_mode(rate_tile)
    lag = iota(1, (LANES, LANES)).astype(f32)
    lane_at = iota(1, (LANES, LANES))
    lane_row = iota(1, (1, LANES))

    back = jnp.exp(-rates * (LANES - 1.0 - lag))
    after = jnp.exp(-rates * (lag + 1.0))
    s_parts = split(back)
    l_parts = split((LANES - 1.0 - lag) * back)
    m_parts = split(after)
    n_parts = split((lag + 1.0) * after)
    for g in range(TILE_GROUPS):
        of = slice(g * MODES, (g + 1) * MODES)
        for part in range(2):
            s_of, l_of = s_parts[part][of], l_parts[part][of]
            m_of, n_of = m_parts[part][of], n_parts[part][of]
            table_all[g, :, part * LANES : (part + 1) * LANES] = jnp.concatenate(
                [s_of, s_of, s_of, l_of, m_of, m_of, n_of, m_of], axis=0
            )

    widen(feat_ref, tail_ref, me_ref, wide, tokens)
    for b in range(blocks):
        query = short_block(wide, taps_ref, 0, b * LANES, LANES)
        key = short_block(wide, taps_ref, 1, b * LANES, LANES)
        value = short_block(wide, taps_ref, 2, b * LANES, LANES)
        z_t = jnp.transpose((key * value).astype(bf16))
        e_t = jnp.transpose(cot_ref[b * LANES : (b + 1) * LANES, :].astype(f32) * query)
        e_high, e_low = split(e_t)
        at = slice(b * MEMBERS, (b + 1) * MEMBERS)
        for g in range(TILE_GROUPS):
            of = slice(g * MEMBERS, (g + 1) * MEMBERS)
            z_ref[g, at, :] = z_t[of]
            eh_ref[g, at, :] = e_high[of]
            el_ref[g, at, :] = e_low[of]

    for g in range(TILE_GROUPS):
        of = slice(g * MEMBERS, (g + 1) * MEMBERS)
        z, eh, el = z_ref[g], eh_ref[g], el_ref[g]
        left = jnp.concatenate(
            [
                jnp.concatenate([z, z], axis=1),
                jnp.concatenate([eh, eh], axis=1),
                jnp.concatenate([el, jnp.zeros_like(el)], axis=1),
            ],
            axis=0,
        )
        got = dot_nt(left, table_all[g])
        rows = z.shape[0]
        own = jnp.where(
            iota(1, (rows, LANES)) < 64, got[:rows], got[rows : 2 * rows] + got[2 * rows :]
        )
        for b in range(blocks):
            own_all[b, of, :] = own[b * MEMBERS : (b + 1) * MEMBERS]

    span = per_member(jnp.exp(rate_tile * (-float(LANES))))
    in_x = jnp.where((lane_row >= 48) & (lane_row < 64), float(LANES), 0.0)
    in_y = jnp.where((lane_row >= 96) & (lane_row < 112), float(LANES), 0.0)
    x_now = jnp.zeros((LANES, LANES), f32)
    y_now = jnp.zeros((LANES, LANES), f32)
    x_lag = jnp.zeros((LANES, LANES), f32)
    y_lag = jnp.zeros((LANES, LANES), f32)
    cross = jnp.zeros((LANES, LANES), f32)
    for b in range(blocks):
        own = own_all[b]
        cross = cross + x_now * pltpu.roll(own, 4 * MODES, 1)
        carry_ref[0, b] = x_now
        x_now = span * (x_now + x_lag) + own
        x_lag = span * x_lag + in_x * pltpu.roll(own, MODES, 1)
    for b in reversed(range(blocks)):
        own = own_all[b]
        carry_ref[0, b] = jnp.where(lane_at < 64, carry_ref[0, b], y_now)
        y_now = span * (y_now + y_lag) + own
        y_lag = span * y_lag + in_y * pltpu.roll(own, MODES, 1)
    cross_ref[...] = jnp.sum(cross.reshape(TILE_GROUPS, MEMBERS, LANES), axis=1)
    turned = jnp.transpose(jnp.where(lane_at < 64, x_now, y_now))
    state_ref[0:16] = turned[0:16]
    state_ref[16:32] = turned[48:64]
    state_ref[32:48] = turned[64:80]
    state_ref[48:64] = turned[96:112]


def inside_kernel(
    z_ref, eh_ref, el_ref, rate_ref, gain_ref,
    inner_ref, grad_ref, diag_ref,
    toep_all, power_all, fold_all, rate_rows, gain_rows,
):
    rate_tile, coef_tile = parameters(rate_ref, gain_ref, rate_rows, gain_rows)
    rates, coefs = per_mode(rate_tile), per_mode(coef_tile)
    lag = iota(1, (LANES, LANES)).astype(f32)
    row_at = iota(0, (LANES, LANES))
    lane_at = iota(1, (LANES, LANES))
    power = jnp.exp(-rates * lag)
    power_all[...] = power
    taps = jnp.sum((coefs * power).reshape(TILE_GROUPS, MODES, LANES), axis=1)
    for g in range(TILE_GROUPS):
        high, low = split(jnp.where(lane_at >= row_at, circulant(taps[g : g + 1]), 0.0))
        toep_all[g, 0:LANES, :] = high
        toep_all[g, LANES:, :] = low
    for g in range(TILE_GROUPS):
        z, eh, el = z_ref[g], eh_ref[g], el_ref[g]
        high = toep_all[g, 0:LANES, :]
        inner_ref[g] = dot_nn(jnp.concatenate([z, z], axis=1), toep_all[g])
        grad_ref[g] = dot_nt(
            jnp.concatenate([eh, el, eh], axis=1),
            jnp.concatenate([high, high, toep_all[g, LANES:, :]], axis=1),
        )
        z_back = jnp.transpose(z)
        gram = dot_nn(jnp.concatenate([z_back, z_back], axis=1), jnp.concatenate([eh, el], axis=0))
        gram = jnp.where(lane_at >= row_at, gram, 0.0)
        folded = [gram[0:8]] + [
            pltpu.roll(gram[8 * r : 8 * r + 8], LANES - 8 * r, 1) for r in range(1, LANES // 8)
        ]
        while len(folded) > 1:
            folded = [folded[i] + folded[i + 1] for i in range(0, len(folded), 2)]
        fold_all[8 * g : 8 * g + 8, :] = folded[0]

    corr = jnp.sum(sheared(fold_all[...], 8).reshape(TILE_GROUPS, 8, LANES), axis=1)
    weighted = power_all[...] * per_member(corr)
    first_col = jnp.sum(weighted, axis=1, keepdims=True)
    lag_col = jnp.sum(lag * weighted, axis=1, keepdims=True)
    mode_at = row_at % MODES
    placed = jnp.where(lane_at == mode_at, first_col, 0.0) + jnp.where(
        lane_at == mode_at + 32, lag_col, 0.0
    )
    diag_ref[...] = jnp.sum(placed.reshape(TILE_GROUPS, MODES, LANES), axis=1)


def exact_dot(left, right, dims):
    return lax.dot_general(
        left, right, (dims, ((), ())), precision=lax.Precision.HIGHEST, preferred_element_type=f32
    )


def join_kernel(tokens, me_ref, state_ref, diag_ref, cross_ref, rate_ref, gain_ref, *refs):
    gots, (bound_ref, local_ref) = refs[:-2], refs[-2:]
    me = me_ref[0]
    channels = state_ref.shape[1]
    groups = rate_ref.shape[1]
    chosen = (iota(0, (groups, channels)) == iota(1, (groups, channels)) // MEMBERS).astype(f32)
    rates = rate_ref[...]
    rate_cols = exact_dot(rates, chosen, ((1,), (0,)))
    zero = jnp.zeros((MODES, channels), f32)
    s_prev, l_prev, e_next = zero, zero, zero
    ahead = jnp.zeros((8, channels), f32)
    for key, got in enumerate(gots, 1):
        other = me ^ key
        earlier = other < me
        away = ((jnp.abs(me - other) - 1) * tokens).astype(f32)
        weight = jnp.exp(-rate_cols * away)
        part = weight * got[0:16]
        s_prev = s_prev + jnp.where(earlier, part, 0.0)
        l_prev = l_prev + jnp.where(earlier, weight * got[16:32] + away * part, 0.0)
        e_next = e_next + jnp.where(earlier, 0.0, part)
        ahead = ahead + jnp.where(other == me + 1, got[32:40], 0.0)
    bound_ref[0:16] = s_prev
    bound_ref[16:32] = e_next
    bound_ref[32:48] = state_ref[0:16] + jnp.exp(-rate_cols * float(tokens)) * s_prev
    bound_ref[48:56] = ahead
    moment_0, moment_1 = state_ref[32:48], state_ref[48:64]
    terms = jnp.concatenate([moment_0 * s_prev, moment_1 * s_prev + moment_0 * l_prev], axis=0)
    sums = exact_dot(terms, chosen, ((1,), (1,)))
    own = jnp.transpose(cross_ref[...] + diag_ref[...])
    first = sums[0:16] + own[0:16]
    lagged = -(sums[16:32] + own[32:48] + own[48:64])
    root = jnp.sqrt(2.0 * rates)
    local_ref[0:16] = root * first
    local_ref[16:32] = gain_ref[...] * root * (0.5 * first + rates * lagged)


def output_kernel(
    me_ref, feat_ref, tail_ref, taps_ref, cot_ref, rate_ref, gain_ref,
    inner_ref, grad_ref, carry_ref, bound_ref,
    mixer_ref, fgrad_ref,
    wide, adj, inner_t, grad_t, left_all, rate_rows, gain_rows,
):
    tokens = feat_ref.shape[1]
    blocks = tokens // LANES
    widen(feat_ref, tail_ref, me_ref, wide, tokens)
    for i in range(3):
        wide[i, 8 + tokens : 16 + tokens, :] = jnp.zeros((8, LANES), f32)
        wide[i, 8 + tokens : 10 + tokens, :] = bound_ref[48 + 2 * i : 50 + 2 * i]
    rate_tile, coef_tile = parameters(rate_ref, gain_ref, rate_rows, gain_rows)
    rates, coefs = per_mode(rate_tile), per_mode(coef_tile)
    lag = iota(1, (LANES, LANES)).astype(f32)
    lane_row = iota(1, (1, LANES))
    lane_at = iota(1, (LANES, LANES))
    is_low = ((lane_at >= 16) & (lane_at < 32)) | ((lane_at >= 80) & (lane_at < 96))
    before = bound_ref[0:16]
    after = bound_ref[16:32]
    gap = jnp.zeros((MODES, LANES), f32)
    stacked = jnp.concatenate([before, before, before, gap, after, after, gap, after], axis=0)
    turned = jnp.transpose(stacked)
    none_16 = jnp.zeros((MODES, LANES), bf16)
    none_64 = jnp.zeros((4 * MODES, LANES), bf16)
    member_rates = per_member(rate_tile)
    for b in range(blocks):
        steps = jnp.where(lane_row < 64, float(b * LANES), float((blocks - 1 - b) * LANES))
        value = carry_ref[0, b] + turned * jnp.exp(-member_rates * steps)
        high = value.astype(bf16).astype(f32)
        mixed = jnp.where(is_low, value - high, value).astype(bf16)
        for g in range(TILE_GROUPS):
            left_all[g, b * MEMBERS : (b + 1) * MEMBERS, :] = mixed[
                g * MEMBERS : (g + 1) * MEMBERS
            ]
    cz_parts = split(coefs * jnp.exp(-rates * (lag + 1.0)))
    ce_parts = split(coefs * jnp.exp(-rates * (LANES - 1.0 - lag)))
    for g in range(TILE_GROUPS):
        of = slice(g * MODES, (g + 1) * MODES)
        cz_high, cz_low = cz_parts[0][of], cz_parts[1][of]
        ce_high, ce_low = ce_parts[0][of], ce_parts[1][of]
        right = jnp.concatenate(
            [
                jnp.concatenate([cz_high, cz_high, cz_low, none_16, none_64], axis=0),
                jnp.concatenate([none_64, ce_high, ce_high, none_16, ce_low], axis=0),
            ],
            axis=1,
        )
        carried = dot_nn(left_all[g], right)
        whole_inner = inner_ref[g] + carried[:, :LANES]
        whole_grad = grad_ref[g] + carried[:, LANES:]
        for b in range(blocks):
            at = slice(b * MEMBERS, (b + 1) * MEMBERS)
            inner_t[b, of, :] = whole_inner[at]
            grad_t[b, of, :] = whole_grad[at]
    for b in range(blocks):
        at = slice(b * LANES, (b + 1) * LANES)
        query = short_block(wide, taps_ref, 0, b * LANES, LANES)
        key = short_block(wide, taps_ref, 1, b * LANES, LANES)
        value = short_block(wide, taps_ref, 2, b * LANES, LANES)
        inner = jnp.transpose(inner_t[b])
        grad = jnp.transpose(grad_t[b])
        mixer_ref[at, :] = (query * inner).astype(bf16)
        adj[0, at, :] = cot_ref[at, :].astype(f32) * inner
        adj[1, at, :] = grad * value
        adj[2, at, :] = grad * key
    key = short_block(wide, taps_ref, 1, tokens, 8)
    value = short_block(wide, taps_ref, 2, tokens, 8)
    query = short_block(wide, taps_ref, 0, tokens, 8)
    z = (key * value).astype(bf16).astype(f32)
    upstream = jnp.concatenate([bound_ref[54:56], jnp.zeros((6, LANES), f32)], axis=0)
    e = upstream * query
    rates = jnp.transpose(member_rates)[0:MODES]
    coefs = jnp.transpose(per_member(coef_tile))[0:MODES]
    decay = jnp.exp(-rates)
    grow = jnp.exp(rates)
    state = bound_ref[32:48]
    sum_0 = jnp.sum(coefs, axis=0, keepdims=True)
    sum_1 = jnp.sum(coefs * decay, axis=0, keepdims=True)
    inner_0 = jnp.sum(coefs * decay * state, axis=0, keepdims=True) + sum_0 * z[0:1]
    inner_1 = (
        jnp.sum(coefs * decay * decay * state, axis=0, keepdims=True)
        + sum_1 * z[0:1]
        + sum_0 * z[1:2]
    )
    grad_0 = jnp.sum(coefs * grow * after, axis=0, keepdims=True)
    grad_1 = jnp.sum(coefs * grow * (grow * after - e[0:1]), axis=0, keepdims=True)
    which = iota(0, (8, LANES))
    inner_8 = jnp.where(which == 0, inner_0, jnp.where(which == 1, inner_1, 0.0))
    grad_8 = jnp.where(which == 0, grad_0, jnp.where(which == 1, grad_1, 0.0))
    adj[0, tokens : tokens + 8, :] = upstream * inner_8
    adj[1, tokens : tokens + 8, :] = grad_8 * value
    adj[2, tokens : tokens + 8, :] = grad_8 * key
    for b in range(blocks):
        start = b * LANES
        for i in range(3):
            fgrad_ref[i, start : start + LANES, :] = (
                taps_ref[i, 0:1, :] * adj[i, start : start + LANES, :]
                + taps_ref[i, 1:2, :] * adj[i, start + 1 : start + 1 + LANES, :]
                + taps_ref[i, 2:3, :] * adj[i, start + 2 : start + 2 + LANES, :]
            ).astype(bf16)


def far(*arrays):
    return [pltpu.with_memory_space_constraint(array, pltpu.HBM) for array in arrays]


def near(*arrays):
    return [pltpu.with_memory_space_constraint(array, pltpu.VMEM) for array in arrays]


def shifted(value, axis, steps):
    count = lax.axis_size(axis)
    return lax.ppermute(value, axis, [(i, (i + steps) % count) for i in range(count)])


def swapped(value, axis, key):
    count = lax.axis_size(axis)
    return lax.ppermute(value, axis, [(i, i ^ key) for i in range(count)])


def per_device(features, short_taps, decay_rates, mode_gains, cotangent):
    tokens = features.shape[1]
    channels = features.shape[2]
    groups = decay_rates.shape[0]
    tiles = channels // LANES
    blocks = tokens // LANES
    ctx_count = lax.axis_size("ctx")
    ctx_index = lax.axis_index("ctx")

    tail = shifted(features[:, tokens - 2 :, :], "ctx", 1)
    head = jnp.concatenate([features[:, :2, :], cotangent[None, :2, :]], axis=0)
    head = head.astype(f32).reshape(8, channels)
    me = ctx_index.astype(jnp.int32).reshape(1)
    rates, gains = decay_rates.T, mode_gains.T

    per_group = pl.BlockSpec((TILE_GROUPS, ROWS, LANES), lambda j: (j, 0, 0))
    feat_spec = pl.BlockSpec((3, tokens, LANES), lambda j: (0, 0, j))
    tail_spec = pl.BlockSpec((3, 2, LANES), lambda j: (0, 0, j))
    taps_spec = pl.BlockSpec((3, 3, LANES), lambda j: (0, 0, j))
    cot_spec = pl.BlockSpec((tokens, LANES), lambda j: (0, j))
    table_spec = pl.BlockSpec((MODES, groups), lambda j: (0, 0))
    carry_spec = pl.BlockSpec((1, blocks, LANES, LANES), lambda j: (j, 0, 0, 0))
    slot_spec = pl.BlockSpec((TILE_GROUPS, LANES), lambda j: (j, 0))
    me_spec = pl.BlockSpec(memory_space=pltpu.SMEM)
    rows = blocks * MEMBERS
    turned = pltpu.VMEM((groups, rows, LANES), bf16)
    wide_turned = pltpu.VMEM((groups, rows, LANES), f32)
    slots = jax.ShapeDtypeStruct((groups, LANES), f32)
    table_scratch = [pltpu.VMEM((LANES, LANES), f32), pltpu.VMEM((LANES, LANES), f32)]

    def room(mebibytes):
        return pltpu.CompilerParams(vmem_limit_bytes=mebibytes * 2**20)

    z, eh, el, carry, states, cross = pl.pallas_call(
        state_kernel,
        grid=(tiles,),
        in_specs=[me_spec, feat_spec, tail_spec, taps_spec, cot_spec, table_spec, table_spec],
        out_specs=[
            per_group,
            per_group,
            per_group,
            carry_spec,
            pl.BlockSpec((4 * MODES, LANES), lambda j: (0, j)),
            slot_spec,
        ],
        out_shape=[
            turned,
            turned,
            turned,
            pltpu.VMEM((tiles, blocks, LANES, LANES), f32),
            jax.ShapeDtypeStruct((4 * MODES, channels), f32),
            slots,
        ],
        scratch_shapes=[
            pltpu.VMEM((3, tokens + 8, LANES), f32),
            pltpu.VMEM((blocks, LANES, LANES), f32),
            pltpu.VMEM((TILE_GROUPS, LANES, 2 * LANES), bf16),
        ]
        + table_scratch,
        compiler_params=room(24),
        name="state_part",
    )(me, *far(features, tail, short_taps, cotangent, rates, gains))

    gots = []
    for key in range(1, ctx_count):
        earlier = (ctx_index ^ key) < ctx_index
        sent = jnp.where(earlier, states[32:64], states[0:32])
        gots.append(swapped(jnp.concatenate([sent, head], axis=0), "ctx", key))

    inner, grad, diag = pl.pallas_call(
        inside_kernel,
        grid=(tiles,),
        in_specs=[per_group, per_group, per_group, table_spec, table_spec],
        out_specs=[per_group, per_group, slot_spec],
        out_shape=[wide_turned, wide_turned, slots],
        scratch_shapes=[
            pltpu.VMEM((TILE_GROUPS, 2 * LANES, LANES), bf16),
            pltpu.VMEM((LANES, LANES), f32),
            pltpu.VMEM((8 * TILE_GROUPS, LANES), f32),
        ]
        + table_scratch,
        compiler_params=room(24),
        cost_estimate=pl.CostEstimate(
            flops=2 * groups * rows * LANES * LANES * 7, bytes_accessed=14 * 2**20, transcendentals=0
        ),
        name="inside_part",
    )(*near(z, eh, el), *far(rates, gains))

    whole = pl.BlockSpec(memory_space=pltpu.VMEM)
    bound, local = pl.pallas_call(
        functools.partial(join_kernel, tokens),
        in_specs=[me_spec] + [whole] * (5 + len(gots)),
        out_specs=[whole, whole],
        out_shape=[
            jax.ShapeDtypeStruct((56, channels), f32),
            jax.ShapeDtypeStruct((2 * MODES, groups), f32),
        ],
        compiler_params=room(24),
        name="join_part",
    )(me, states, diag, cross, rates, gains, *gots)

    terms = [local] + [swapped(local, "ctx", key) for key in range(1, ctx_count)]
    while len(terms) > 1:
        terms = [terms[i] + terms[i + 1] for i in range(0, len(terms), 2)]
    summed = terms[0]
    squares = jnp.broadcast_to(jnp.sum(summed * summed), (8, LANES))
    fsdp_count = lax.axis_size("fsdp")
    step = 1
    while step < fsdp_count:
        squares = squares + swapped(squares, "fsdp", step)
        step *= 2
    entry_count = 2 * groups * MODES * fsdp_count
    factor = jnp.minimum(1.0, lax.rsqrt(squares[0, 0] / entry_count + 1e-06))
    clipped = summed * factor

    mixer, feature_grads = pl.pallas_call(
        output_kernel,
        grid=(tiles,),
        in_specs=[
            me_spec,
            feat_spec,
            tail_spec,
            taps_spec,
            cot_spec,
            table_spec,
            table_spec,
            per_group,
            per_group,
            carry_spec,
            pl.BlockSpec((56, LANES), lambda j: (0, j)),
        ],
        out_specs=[cot_spec, feat_spec],
        out_shape=[
            jax.ShapeDtypeStruct((tokens, channels), bf16),
            jax.ShapeDtypeStruct((3, tokens, channels), bf16),
        ],
        scratch_shapes=[
            pltpu.VMEM((3, tokens + 16, LANES), f32),
            pltpu.VMEM((3, tokens + 8, LANES), f32),
            pltpu.VMEM((blocks, LANES, LANES), f32),
            pltpu.VMEM((blocks, LANES, LANES), f32),
            pltpu.VMEM((TILE_GROUPS, rows, LANES), bf16),
        ]
        + table_scratch,
        compiler_params=room(24),
        cost_estimate=pl.CostEstimate(
            flops=2 * groups * rows * LANES * LANES * 4, bytes_accessed=28 * 2**20, transcendentals=0
        ),
        name="output_part",
    )(me, *far(features, tail, short_taps, cotangent, rates, gains), *near(inner, grad, carry), bound)
    return (mixer, feature_grads, clipped[:MODES].T, clipped[MODES:].T)


def solution(mesh):
    return jax.shard_map(
        per_device,
        mesh=mesh,
        in_specs=(
            P(None, "ctx", "fsdp"),
            P(None, None, "fsdp"),
            P("fsdp", None),
            P("fsdp", None),
            P("ctx", "fsdp"),
        ),
        out_specs=(P("ctx", "fsdp"), P(None, "ctx", "fsdp"), P("fsdp", None), P("fsdp", None)),
        check_vma=False,
    )
```

```python
import functools

import jax
import jax.numpy as jnp
from jax import lax
from jax.experimental import pallas as pl
from jax.experimental.pallas import tpu as pltpu
from jax.sharding import PartitionSpec as P

LANES = 128
MODES = 16
MEMBERS = 16
TILE_GROUPS = LANES // MEMBERS
ROWS = LANES
f32 = jnp.float32
bf16 = jnp.bfloat16


def split(value):
    high = value.astype(bf16)
    return high, (value - high.astype(f32)).astype(bf16)


def dot_nt(left, right):
    return lax.dot_general(left, right, (((1,), (1,)), ((), ())), preferred_element_type=f32)


def dot_tn(left, right):
    return lax.dot_general(left, right, (((0,), (0,)), ((), ())), preferred_element_type=f32)


def dot_nn(left, right):
    return lax.dot_general(left, right, (((1,), (0,)), ((), ())), preferred_element_type=f32)


def iota(axis, shape):
    return lax.broadcasted_iota(jnp.int32, shape, axis)


def widen(feat_ref, tail_ref, me_ref, wide, tokens):
    for i in range(3):
        wide[i, 6:8, :] = jnp.where(me_ref[0] == 0, 0.0, tail_ref[i].astype(f32))
        wide[i, 8 : 8 + tokens, :] = feat_ref[i].astype(f32)


def short_block(wide, taps_ref, i, start, count):
    return (
        taps_ref[i, 0:1, :] * wide[i, start + 8 : start + 8 + count, :]
        + taps_ref[i, 1:2, :] * wide[i, start + 7 : start + 7 + count, :]
        + taps_ref[i, 2:3, :] * wide[i, start + 6 : start + 6 + count, :]
    )


def sheared(row8, period):
    which = iota(0, row8.shape) % period
    for bit in (1, 2, 4):
        row8 = jnp.where((which & bit) != 0, pltpu.roll(row8, LANES - bit, 1), row8)
    return row8


def circulant(row):
    return pltpu.roll(jnp.broadcast_to(row, (LANES, LANES)), 0, 1, stride=1, stride_axis=0)


def of_tile(whole, first=0):
    return whole.at[pl.ds((pl.program_id(0) + first) * TILE_GROUPS, TILE_GROUPS)]


def table_rows(source_ref, rows_ref):
    tall = jnp.concatenate([source_ref[...]] * (LANES // MODES), axis=0)
    missing = LANES - tall.shape[1]
    if missing:
        tall = jnp.concatenate([tall, jnp.zeros((LANES, missing), f32)], axis=1)
    rows_ref[...] = jnp.transpose(tall)


def parameters(rate_ref, gain_ref, rate_rows, gain_rows, first=0):
    tile = pl.program_id(0) + first

    @pl.when(pl.program_id(0) == 0)
    def _():
        table_rows(rate_ref, rate_rows)
        table_rows(gain_ref, gain_rows)

    at = pl.ds(pl.multiple_of(tile * TILE_GROUPS, TILE_GROUPS), TILE_GROUPS)
    rates = rate_rows[at, :]
    return rates, gain_rows[at, :] * jnp.sqrt(2.0 * rates)


def per_mode(rows):
    own = iota(0, (TILE_GROUPS, LANES)) == iota(1, (TILE_GROUPS, LANES)) // MODES
    flat = jnp.sum(jnp.where(own, rows, 0.0), axis=0, keepdims=True)
    return jnp.transpose(jnp.broadcast_to(flat, (LANES, LANES)))


def per_member(rows):
    return jnp.concatenate(
        [jnp.broadcast_to(rows[g : g + 1], (MEMBERS, LANES)) for g in range(TILE_GROUPS)], axis=0
    )


def state_kernel(
    me_ref, feat_ref, tail_ref, taps_ref, cot_ref, rate_ref, gain_ref,
    z_whole, eh_whole, el_whole, carry_whole, short_whole, state_ref, cross_ref,
    wide, own_all, table_all, rate_rows, gain_rows,
):
    z_ref, eh_ref, el_ref = of_tile(z_whole), of_tile(eh_whole), of_tile(el_whole)
    carry_ref = carry_whole.at[pl.program_id(0)]
    short_ref = short_whole.at[pl.program_id(0)]
    tokens = feat_ref.shape[1]
    blocks = tokens // LANES
    rate_tile, _ = parameters(rate_ref, gain_ref, rate_rows, gain_rows)
    rates = per_mode(rate_tile)
    lag = iota(1, (LANES, LANES)).astype(f32)
    lane_at = iota(1, (LANES, LANES))
    lane_row = iota(1, (1, LANES))

    back = jnp.exp(-rates * (LANES - 1.0 - lag))
    after = jnp.exp(-rates * (lag + 1.0))
    s_parts = split(back)
    l_parts = split((LANES - 1.0 - lag) * back)
    m_parts = split(after)
    n_parts = split((lag + 1.0) * after)
    for g in range(TILE_GROUPS):
        of = slice(g * MODES, (g + 1) * MODES)
        for part in range(2):
            s_of, l_of = s_parts[part][of], l_parts[part][of]
            m_of, n_of = m_parts[part][of], n_parts[part][of]
            table_all[g, :, part * LANES : (part + 1) * LANES] = jnp.concatenate(
                [s_of, s_of, s_of, l_of, m_of, m_of, n_of, m_of], axis=0
            )

    widen(feat_ref, tail_ref, me_ref, wide, tokens)
    for b in range(blocks):
        query = short_block(wide, taps_ref, 0, b * LANES, LANES)
        key = short_block(wide, taps_ref, 1, b * LANES, LANES)
        value = short_block(wide, taps_ref, 2, b * LANES, LANES)
        short_ref[0, b * LANES : (b + 1) * LANES, :] = query
        short_ref[1, b * LANES : (b + 1) * LANES, :] = key
        short_ref[2, b * LANES : (b + 1) * LANES, :] = value
        z_t = jnp.transpose((key * value).astype(bf16))
        e_t = jnp.transpose(cot_ref[b * LANES : (b + 1) * LANES, :].astype(f32) * query)
        e_high, e_low = split(e_t)
        at = slice(b * MEMBERS, (b + 1) * MEMBERS)
        for g in range(TILE_GROUPS):
            of = slice(g * MEMBERS, (g + 1) * MEMBERS)
            z_ref[g, at, :] = z_t[of]
            eh_ref[g, at, :] = e_high[of]
            el_ref[g, at, :] = e_low[of]

    for g in range(TILE_GROUPS):
        of = slice(g * MEMBERS, (g + 1) * MEMBERS)
        z, eh, el = z_ref[g], eh_ref[g], el_ref[g]
        left = jnp.concatenate(
            [
                jnp.concatenate([z, z], axis=1),
                jnp.concatenate([eh, eh], axis=1),
                jnp.concatenate([el, jnp.zeros_like(el)], axis=1),
            ],
            axis=0,
        )
        got = dot_nt(left, table_all[g])
        rows = z.shape[0]
        from_e = got[rows : 2 * rows] + got[2 * rows :]
        for b in range(blocks):
            at = slice(b * MEMBERS, (b + 1) * MEMBERS)
            opposite = slice((blocks - 1 - b) * MEMBERS, (blocks - b) * MEMBERS)
            own_all[b, of, :] = jnp.where(
                iota(1, (MEMBERS, LANES)) < 64, got[at], from_e[opposite]
            )

    span = per_member(jnp.exp(rate_tile * (-float(LANES))))
    in_lag = jnp.where(
        ((lane_row >= 48) & (lane_row < 64)) | ((lane_row >= 96) & (lane_row < 112)),
        float(LANES),
        0.0,
    )
    now = jnp.zeros((LANES, LANES), f32)
    lagged = jnp.zeros((LANES, LANES), f32)
    cross = jnp.zeros((LANES, LANES), f32)
    for b in range(blocks):
        own = own_all[b]
        cross = cross + now * pltpu.roll(own_all[blocks - 1 - b], 4 * MODES, 1)
        carry_ref[b] = now
        now = span * (now + lagged) + own
        if b < blocks - 1:
            lagged = span * lagged + in_lag * pltpu.roll(own, MODES, 1)
    cross_ref[...] = jnp.sum(cross.reshape(TILE_GROUPS, MEMBERS, LANES), axis=1)
    turned = jnp.transpose(now)
    state_ref[0:16] = turned[0:16]
    state_ref[16:32] = turned[48:64]
    state_ref[32:48] = turned[64:80]
    state_ref[48:64] = turned[96:112]


def inside_kernel(
    z_whole, eh_whole, el_whole, rate_ref, gain_ref,
    inner_whole, grad_whole, diag_ref,
    toep_all, power_all, fold_all, rate_rows, gain_rows,
):
    z_ref, eh_ref, el_ref = of_tile(z_whole), of_tile(eh_whole), of_tile(el_whole)
    inner_ref, grad_ref = of_tile(inner_whole), of_tile(grad_whole)
    rate_tile, coef_tile = parameters(rate_ref, gain_ref, rate_rows, gain_rows)
    rates, coefs = per_mode(rate_tile), per_mode(coef_tile)
    lag = iota(1, (LANES, LANES)).astype(f32)
    row_at = iota(0, (LANES, LANES))
    lane_at = iota(1, (LANES, LANES))
    power = jnp.exp(-rates * lag)
    power_all[...] = power
    taps = jnp.sum((coefs * power).reshape(TILE_GROUPS, MODES, LANES), axis=1)
    for g in range(TILE_GROUPS):
        high, low = split(jnp.where(lane_at >= row_at, circulant(taps[g : g + 1]), 0.0))
        toep_all[g, 0:LANES, :] = high
        toep_all[g, LANES:, :] = low
    for g in range(TILE_GROUPS):
        z, eh, el = z_ref[g], eh_ref[g], el_ref[g]
        high = toep_all[g, 0:LANES, :]
        inner_ref[g] = dot_nn(jnp.concatenate([z, z], axis=1), toep_all[g])
        grad_ref[g] = dot_nt(
            jnp.concatenate([eh, el, eh], axis=1),
            jnp.concatenate([high, high, toep_all[g, LANES:, :]], axis=1),
        )
        z_back = jnp.transpose(z)
        gram = dot_nn(jnp.concatenate([z_back, z_back], axis=1), jnp.concatenate([eh, el], axis=0))
        gram = jnp.where(lane_at >= row_at, gram, 0.0)
        folded = [gram[0:8]] + [
            pltpu.roll(gram[8 * r : 8 * r + 8], LANES - 8 * r, 1) for r in range(1, LANES // 8)
        ]
        while len(folded) > 1:
            folded = [folded[i] + folded[i + 1] for i in range(0, len(folded), 2)]
        fold_all[8 * g : 8 * g + 8, :] = folded[0]

    corr = jnp.sum(sheared(fold_all[...], 8).reshape(TILE_GROUPS, 8, LANES), axis=1)
    weighted = power_all[...] * per_member(corr)
    first_col = jnp.sum(weighted, axis=1, keepdims=True)
    lag_col = jnp.sum(lag * weighted, axis=1, keepdims=True)
    mode_at = row_at % MODES
    placed = jnp.where(lane_at == mode_at, first_col, 0.0) + jnp.where(
        lane_at == mode_at + 32, lag_col, 0.0
    )
    diag_ref[...] = jnp.sum(placed.reshape(TILE_GROUPS, MODES, LANES), axis=1)


def exact_dot(left, right, dims):
    return lax.dot_general(
        left, right, (dims, ((), ())), precision=lax.Precision.HIGHEST, preferred_element_type=f32
    )


def join_kernel(tokens, me_ref, state_ref, diag_ref, cross_ref, rate_ref, gain_ref, *refs):
    gots, (bound_ref, local_ref) = refs[:-2], refs[-2:]
    me = me_ref[0]
    channels = state_ref.shape[1]
    groups = rate_ref.shape[1]
    chosen = (iota(0, (groups, channels)) == iota(1, (groups, channels)) // MEMBERS).astype(f32)
    rates = rate_ref[...]
    rate_cols = exact_dot(rates, chosen, ((1,), (0,)))
    zero = jnp.zeros((MODES, channels), f32)
    s_prev, l_prev, e_next = zero, zero, zero
    ahead = jnp.zeros((8, channels), f32)
    for key, got in enumerate(gots, 1):
        other = me ^ key
        earlier = other < me
        away = ((jnp.abs(me - other) - 1) * tokens).astype(f32)
        weight = jnp.exp(-rate_cols * away)
        part = weight * got[0:16]
        s_prev = s_prev + jnp.where(earlier, part, 0.0)
        l_prev = l_prev + jnp.where(earlier, weight * got[16:32] + away * part, 0.0)
        e_next = e_next + jnp.where(earlier, 0.0, part)
        ahead = ahead + jnp.where(other == me + 1, got[32:40], 0.0)
    bound_ref[0:16] = s_prev
    bound_ref[16:32] = e_next
    bound_ref[32:48] = state_ref[0:16] + jnp.exp(-rate_cols * float(tokens)) * s_prev
    bound_ref[48:56] = ahead
    moment_0, moment_1 = state_ref[32:48], state_ref[48:64]
    terms = jnp.concatenate([moment_0 * s_prev, moment_1 * s_prev + moment_0 * l_prev], axis=0)
    sums = exact_dot(terms, chosen, ((1,), (1,)))
    own = jnp.transpose(cross_ref[...] + diag_ref[...])
    first = sums[0:16] + own[0:16]
    lagged = -(sums[16:32] + own[32:48] + own[48:64])
    root = jnp.sqrt(2.0 * rates)
    local_ref[0:16] = root * first
    local_ref[16:32] = gain_ref[...] * root * (0.5 * first + rates * lagged)


def output_kernel(
    first, edge_ref, taps_ref, cot_ref, rate_ref, gain_ref,
    inner_whole, grad_whole, carry_whole, short_whole, bound_ref,
    *refs,
):
    mixer_ref, fgrad_ref, wide, adj, inner_t, grad_t, left_all, rate_rows, gain_rows = refs[-9:]
    inner_ref, grad_ref = of_tile(inner_whole, first), of_tile(grad_whole, first)
    carry_ref = carry_whole.at[pl.program_id(0) + first]
    short_ref = short_whole.at[pl.program_id(0) + first]
    tokens = cot_ref.shape[0]
    blocks = tokens // LANES
    rate_tile, coef_tile = parameters(rate_ref, gain_ref, rate_rows, gain_rows, first)
    rates, coefs = per_mode(rate_tile), per_mode(coef_tile)
    lag = iota(1, (LANES, LANES)).astype(f32)
    lane_at = iota(1, (LANES, LANES))
    is_low = ((lane_at >= 16) & (lane_at < 32)) | ((lane_at >= 80) & (lane_at < 96))
    before = bound_ref[0:16]
    after = bound_ref[16:32]
    gap = jnp.zeros((MODES, LANES), f32)
    stacked = jnp.concatenate([before, before, before, gap, after, after, gap, after], axis=0)
    turned = jnp.transpose(stacked)
    none_16 = jnp.zeros((MODES, LANES), bf16)
    none_64 = jnp.zeros((4 * MODES, LANES), bf16)
    member_rates = per_member(rate_tile)
    span = jnp.exp(member_rates * (-float(LANES)))
    from_others = turned
    for b in range(blocks):
        value = carry_ref[b] + from_others
        from_others = from_others * span
        high = value.astype(bf16).astype(f32)
        mixed = jnp.where(is_low, value - high, value).astype(bf16)
        for g in range(TILE_GROUPS):
            left_all[g, b * MEMBERS : (b + 1) * MEMBERS, :] = mixed[
                g * MEMBERS : (g + 1) * MEMBERS
            ]
    cz_parts = split(coefs * jnp.exp(-rates * (lag + 1.0)))
    ce_parts = split(coefs * jnp.exp(-rates * (LANES - 1.0 - lag)))
    for g in range(TILE_GROUPS):
        of = slice(g * MODES, (g + 1) * MODES)
        cz_high, cz_low = cz_parts[0][of], cz_parts[1][of]
        ce_high, ce_low = ce_parts[0][of], ce_parts[1][of]
        right = jnp.concatenate(
            [
                jnp.concatenate([cz_high, cz_high, cz_low, none_16, none_64], axis=0),
                jnp.concatenate([none_64, ce_high, ce_high, none_16, ce_low], axis=0),
            ],
            axis=1,
        )
        carried = dot_nn(left_all[g], right)
        for b in range(blocks):
            at = slice(b * MEMBERS, (b + 1) * MEMBERS)
            opposite = slice((blocks - 1 - b) * MEMBERS, (blocks - b) * MEMBERS)
            inner_t[b, of, :] = inner_ref[g, at, :] + carried[at, :LANES]
            grad_t[b, of, :] = grad_ref[g, at, :] + carried[opposite, LANES:]
    for b in range(blocks):
        at = slice(b * LANES, (b + 1) * LANES)
        inner = jnp.transpose(inner_t[b])
        grad = jnp.transpose(grad_t[b])
        mixer_ref[at, :] = (short_ref[0, at, :] * inner).astype(bf16)
        adj[0, at, :] = cot_ref[at, :].astype(f32) * inner
        adj[1, at, :] = grad * short_ref[2, at, :]
        adj[2, at, :] = grad * short_ref[1, at, :]
    for i in range(3):
        wide[i, 0:8, :] = edge_ref[i, 8:16, :].astype(f32)
        wide[i, 8:16, :] = jnp.zeros((8, LANES), f32)
        wide[i, 8:10, :] = bound_ref[48 + 2 * i : 50 + 2 * i]
    query, key, value = [short_block(wide, taps_ref, i, 0, 8) for i in range(3)]
    z = (key * value).astype(bf16).astype(f32)
    upstream = jnp.concatenate([bound_ref[54:56], jnp.zeros((6, LANES), f32)], axis=0)
    e = upstream * query
    rates = jnp.transpose(member_rates)[0:MODES]
    coefs = jnp.transpose(per_member(coef_tile))[0:MODES]
    decay = jnp.exp(-rates)
    grow = jnp.exp(rates)
    state = bound_ref[32:48]
    sum_0 = jnp.sum(coefs, axis=0, keepdims=True)
    sum_1 = jnp.sum(coefs * decay, axis=0, keepdims=True)
    inner_0 = jnp.sum(coefs * decay * state, axis=0, keepdims=True) + sum_0 * z[0:1]
    inner_1 = (
        jnp.sum(coefs * decay * decay * state, axis=0, keepdims=True)
        + sum_1 * z[0:1]
        + sum_0 * z[1:2]
    )
    grad_0 = jnp.sum(coefs * grow * after, axis=0, keepdims=True)
    grad_1 = jnp.sum(coefs * grow * (grow * after - e[0:1]), axis=0, keepdims=True)
    which = iota(0, (8, LANES))
    inner_8 = jnp.where(which == 0, inner_0, jnp.where(which == 1, inner_1, 0.0))
    grad_8 = jnp.where(which == 0, grad_0, jnp.where(which == 1, grad_1, 0.0))
    adj[0, tokens : tokens + 8, :] = upstream * inner_8
    adj[1, tokens : tokens + 8, :] = grad_8 * value
    adj[2, tokens : tokens + 8, :] = grad_8 * key
    for b in range(blocks):
        start = b * LANES
        for i in range(3):
            fgrad_ref[i, start : start + LANES, :] = (
                taps_ref[i, 0:1, :] * adj[i, start : start + LANES, :]
                + taps_ref[i, 1:2, :] * adj[i, start + 1 : start + 1 + LANES, :]
                + taps_ref[i, 2:3, :] * adj[i, start + 2 : start + 2 + LANES, :]
            ).astype(bf16)


def resident(shape, dtype):
    return pltpu.VMEM(shape, dtype)


def sum_kernel(*refs):
    *terms, summed_ref, square_ref = refs
    terms = [term[...] for term in terms]
    while len(terms) > 1:
        terms = [terms[i] + terms[i + 1] for i in range(0, len(terms), 2)]
    summed_ref[...] = terms[0]
    square_ref[...] = jnp.broadcast_to(
        jnp.sum(jnp.sum(terms[0] * terms[0], axis=0, keepdims=True), axis=1, keepdims=True),
        square_ref.shape,
    )


def far(*arrays):
    return [pltpu.with_memory_space_constraint(array, pltpu.HBM) for array in arrays]


def near(*arrays):
    return [pltpu.with_memory_space_constraint(array, pltpu.VMEM) for array in arrays]


def shifted(value, axis, steps):
    count = lax.axis_size(axis)
    return lax.ppermute(value, axis, [(i, (i + steps) % count) for i in range(count)])


def swapped(value, axis, key):
    count = lax.axis_size(axis)
    return lax.ppermute(value, axis, [(i, i ^ key) for i in range(count)])


def per_device(features, short_taps, decay_rates, mode_gains, cotangent):
    tokens = features.shape[1]
    channels = features.shape[2]
    groups = decay_rates.shape[0]
    tiles = channels // LANES
    blocks = tokens // LANES
    ctx_count = lax.axis_size("ctx")
    ctx_index = lax.axis_index("ctx")

    tail = shifted(features[:, tokens - 2 :, :], "ctx", 1)
    head = jnp.concatenate([features[:, :2, :], cotangent[None, :2, :]], axis=0)
    head = head.astype(f32).reshape(8, channels)
    me = ctx_index.astype(jnp.int32).reshape(1)
    rates, gains = decay_rates.T, mode_gains.T

    whole = pl.BlockSpec(memory_space=pltpu.VMEM)
    feat_spec = pl.BlockSpec((3, tokens, LANES), lambda j: (0, 0, j))
    tail_spec = pl.BlockSpec((3, 2, LANES), lambda j: (0, 0, j))
    taps_spec = pl.BlockSpec((3, 3, LANES), lambda j: (0, 0, j))
    cot_spec = pl.BlockSpec((tokens, LANES), lambda j: (0, j))
    table_spec = pl.BlockSpec((MODES, groups), lambda j: (0, 0))
    slot_spec = pl.BlockSpec((TILE_GROUPS, LANES), lambda j: (j, 0))
    me_spec = pl.BlockSpec(memory_space=pltpu.SMEM)
    rows = blocks * MEMBERS
    turned = resident((groups, rows, LANES), bf16)
    wide_turned = resident((groups, rows, LANES), f32)
    slots = jax.ShapeDtypeStruct((groups, LANES), f32)
    table_scratch = [pltpu.VMEM((LANES, LANES), f32), pltpu.VMEM((LANES, LANES), f32)]

    def room(mebibytes):
        return pltpu.CompilerParams(vmem_limit_bytes=mebibytes * 2**20)

    z, eh, el, carry, short, states, cross = pl.pallas_call(
        state_kernel,
        grid=(tiles,),
        in_specs=[me_spec, feat_spec, tail_spec, taps_spec, cot_spec, table_spec, table_spec],
        out_specs=[
            whole,
            whole,
            whole,
            whole,
            whole,
            pl.BlockSpec((4 * MODES, LANES), lambda j: (0, j)),
            slot_spec,
        ],
        out_shape=[
            turned,
            turned,
            turned,
            resident((tiles, blocks, LANES, LANES), f32),
            resident((tiles, 3, tokens, LANES), f32),
            jax.ShapeDtypeStruct((4 * MODES, channels), f32),
            slots,
        ],
        scratch_shapes=[
            pltpu.VMEM((3, tokens + 8, LANES), f32),
            pltpu.VMEM((blocks, LANES, LANES), f32),
            pltpu.VMEM((TILE_GROUPS, LANES, 2 * LANES), bf16),
        ]
        + table_scratch,
        compiler_params=room(14),
        name="state_part",
    )(me, *far(features, tail, short_taps, cotangent, rates, gains))

    gots = []
    for key in range(1, ctx_count):
        earlier = (ctx_index ^ key) < ctx_index
        sent = jnp.where(earlier, states[32:64], states[0:32])
        gots.append(swapped(jnp.concatenate([sent, head], axis=0), "ctx", key))

    inner, grad, diag = pl.pallas_call(
        inside_kernel,
        grid=(tiles,),
        in_specs=[whole, whole, whole, table_spec, table_spec],
        out_specs=[whole, whole, slot_spec],
        out_shape=[wide_turned, wide_turned, slots],
        scratch_shapes=[
            pltpu.VMEM((TILE_GROUPS, 2 * LANES, LANES), bf16),
            pltpu.VMEM((LANES, LANES), f32),
            pltpu.VMEM((8 * TILE_GROUPS, LANES), f32),
        ]
        + table_scratch,
        compiler_params=room(14),
        cost_estimate=pl.CostEstimate(
            flops=2 * groups * rows * LANES * LANES * 7, bytes_accessed=14 * 2**20, transcendentals=0
        ),
        name="inside_part",
    )(*near(z, eh, el), *far(rates, gains))

    bound, local = pl.pallas_call(
        functools.partial(join_kernel, tokens),
        in_specs=[me_spec] + [whole] * (5 + len(gots)),
        out_specs=[whole, whole],
        out_shape=[
            jax.ShapeDtypeStruct((56, channels), f32),
            jax.ShapeDtypeStruct((2 * MODES, groups), f32),
        ],
        compiler_params=room(14),
        name="join_part",
    )(me, states, diag, cross, rates, gains, *gots)

    def outputs(first, count, *written):
        columns = lambda j: (0, j + first)
        layers = lambda j: (0, 0, j + first)
        mine = [pl.BlockSpec((tokens, LANES), columns), pl.BlockSpec((3, tokens, LANES), layers)]
        return pl.pallas_call(
            functools.partial(output_kernel, first),
            grid=(count,),
            in_specs=[
                pl.BlockSpec((3, 16, LANES), lambda j: (0, tokens // 16 - 1, j + first)),
                pl.BlockSpec((3, 3, LANES), layers),
                pl.BlockSpec((tokens, LANES), columns),
                table_spec,
                table_spec,
                whole,
                whole,
                whole,
                whole,
                pl.BlockSpec((56, LANES), columns),
            ]
            + [pl.BlockSpec(memory_space=pl.ANY)] * len(written),
            out_specs=mine,
            out_shape=[
                jax.ShapeDtypeStruct((tokens, channels), bf16),
                jax.ShapeDtypeStruct((3, tokens, channels), bf16),
            ],
            scratch_shapes=[
                pltpu.VMEM((3, 16, LANES), f32),
                pltpu.VMEM((3, tokens + 8, LANES), f32),
                pltpu.VMEM((blocks, LANES, LANES), f32),
                pltpu.VMEM((blocks, LANES, LANES), f32),
                pltpu.VMEM((TILE_GROUPS, rows, LANES), bf16),
            ]
            + table_scratch,
            compiler_params=room(14),
            input_output_aliases={10: 0, 11: 1} if written else {},
            cost_estimate=pl.CostEstimate(
                flops=2 * count * TILE_GROUPS * rows * LANES * LANES * 8,
                bytes_accessed=count * 4 * 2**20,
                transcendentals=0,
            ),
            name="output_part",
        )(
            *far(features, short_taps, cotangent, rates, gains),
            *near(inner, grad, carry, short),
            bound,
            *written,
        )

    half = tiles // 2
    terms = [local] + [swapped(local, "ctx", key) for key in range(1, ctx_count)]
    written = outputs(0, half)
    terms, written = lax.optimization_barrier((terms, written))
    summed, squares = pl.pallas_call(
        sum_kernel,
        in_specs=[whole] * len(terms),
        out_specs=[whole, whole],
        out_shape=[
            jax.ShapeDtypeStruct((2 * MODES, groups), f32),
            jax.ShapeDtypeStruct((1, groups), f32),
        ],
        compiler_params=room(14),
        name="sum_part",
    )(*terms)
    fsdp_count = lax.axis_size("fsdp")
    step = 1
    while step * 4 < fsdp_count:
        squares = squares + swapped(squares, "fsdp", step)
        step *= 2
    squares, written = lax.optimization_barrier((squares, written))
    parts = [squares] + [swapped(squares, "fsdp", key) for key in range(step, fsdp_count, step)]
    mixer, feature_grads = outputs(half, tiles - half, *written)
    while len(parts) > 1:
        parts = [parts[i] + parts[i + 1] for i in range(0, len(parts), 2)]
    entry_count = 2 * groups * MODES * fsdp_count
    clipped = summed * jnp.minimum(1.0, lax.rsqrt(parts[0] / entry_count + 1e-06))
    return (mixer, feature_grads, clipped[:MODES].T, clipped[MODES:].T)


def solution(mesh):
    return jax.shard_map(
        per_device,
        mesh=mesh,
        in_specs=(
            P(None, "ctx", "fsdp"),
            P(None, None, "fsdp"),
            P("fsdp", None),
            P("fsdp", None),
            P("ctx", "fsdp"),
        ),
        out_specs=(P("ctx", "fsdp"), P(None, "ctx", "fsdp"), P("fsdp", None), P("fsdp", None)),
        check_vma=False,
    )
```

```python
import functools

import jax
import jax.numpy as jnp
from jax import lax
from jax.experimental import pallas as pl
from jax.experimental.pallas import tpu as pltpu
from jax.sharding import PartitionSpec as P

LANES = 128
MODES = 16
MEMBERS = 16
TILE_GROUPS = LANES // MEMBERS
ROWS = LANES
f32 = jnp.float32
bf16 = jnp.bfloat16


def split(value):
    high = value.astype(bf16)
    return high, (value - high.astype(f32)).astype(bf16)


def dot_nt(left, right):
    return lax.dot_general(left, right, (((1,), (1,)), ((), ())), preferred_element_type=f32)


def dot_tn(left, right):
    return lax.dot_general(left, right, (((0,), (0,)), ((), ())), preferred_element_type=f32)


def dot_nn(left, right):
    return lax.dot_general(left, right, (((1,), (0,)), ((), ())), preferred_element_type=f32)


def iota(axis, shape):
    return lax.broadcasted_iota(jnp.int32, shape, axis)


def widen(feat_ref, wide, tokens):
    for i in range(3):
        wide[i, 0:8, :] = jnp.zeros((8, LANES), f32)
        wide[i, 8 : 8 + tokens, :] = feat_ref[i].astype(f32)


def short_block(wide, taps_ref, i, start, count):
    return (
        taps_ref[i, 0:1, :] * wide[i, start + 8 : start + 8 + count, :]
        + taps_ref[i, 1:2, :] * wide[i, start + 7 : start + 7 + count, :]
        + taps_ref[i, 2:3, :] * wide[i, start + 6 : start + 6 + count, :]
    )


def sheared(row8, period):
    which = iota(0, row8.shape) % period
    for bit in (1, 2, 4):
        row8 = jnp.where((which & bit) != 0, pltpu.roll(row8, LANES - bit, 1), row8)
    return row8


def circulant(row):
    return pltpu.roll(jnp.broadcast_to(row, (LANES, LANES)), 0, 1, stride=1, stride_axis=0)


def of_tile(whole, first=0):
    return whole.at[pl.ds((pl.program_id(0) + first) * TILE_GROUPS, TILE_GROUPS)]


def table_rows(source_ref, rows_ref):
    tall = jnp.concatenate([source_ref[...]] * (LANES // MODES), axis=0)
    missing = LANES - tall.shape[1]
    if missing:
        tall = jnp.concatenate([tall, jnp.zeros((LANES, missing), f32)], axis=1)
    rows_ref[...] = jnp.transpose(tall)


def parameters(rate_ref, gain_ref, rate_rows, gain_rows, first=0):
    tile = pl.program_id(0) + first

    @pl.when(pl.program_id(0) == 0)
    def _():
        table_rows(rate_ref, rate_rows)
        table_rows(gain_ref, gain_rows)

    at = pl.ds(pl.multiple_of(tile * TILE_GROUPS, TILE_GROUPS), TILE_GROUPS)
    rates = rate_rows[at, :]
    return rates, gain_rows[at, :] * jnp.sqrt(2.0 * rates)


def per_mode(rows):
    own = iota(0, (TILE_GROUPS, LANES)) == iota(1, (TILE_GROUPS, LANES)) // MODES
    flat = jnp.sum(jnp.where(own, rows, 0.0), axis=0, keepdims=True)
    return jnp.transpose(jnp.broadcast_to(flat, (LANES, LANES)))


def per_member(rows):
    return jnp.concatenate(
        [jnp.broadcast_to(rows[g : g + 1], (MEMBERS, LANES)) for g in range(TILE_GROUPS)], axis=0
    )


def state_kernel(
    feat_ref, taps_ref, cot_ref, rate_ref, gain_ref,
    z_whole, eh_whole, el_whole, carry_whole, short_whole, state_ref, cross_ref,
    later_ref, earlier_ref,
    wide, own_all, table_all, rate_rows, gain_rows,
):
    z_ref, eh_ref, el_ref = of_tile(z_whole), of_tile(eh_whole), of_tile(el_whole)
    carry_ref = carry_whole.at[pl.program_id(0)]
    short_ref = short_whole.at[pl.program_id(0)]
    tokens = feat_ref.shape[1]
    blocks = tokens // LANES
    rate_tile, _ = parameters(rate_ref, gain_ref, rate_rows, gain_rows)
    rates = per_mode(rate_tile)
    lag = iota(1, (LANES, LANES)).astype(f32)
    lane_at = iota(1, (LANES, LANES))
    lane_row = iota(1, (1, LANES))

    back = jnp.exp(-rates * (LANES - 1.0 - lag))
    after = jnp.exp(-rates * (lag + 1.0))
    s_parts = split(back)
    l_parts = split((LANES - 1.0 - lag) * back)
    m_parts = split(after)
    n_parts = split((lag + 1.0) * after)
    for g in range(TILE_GROUPS):
        of = slice(g * MODES, (g + 1) * MODES)
        for part in range(2):
            s_of, l_of = s_parts[part][of], l_parts[part][of]
            m_of, n_of = m_parts[part][of], n_parts[part][of]
            table_all[g, :, part * LANES : (part + 1) * LANES] = jnp.concatenate(
                [s_of, s_of, s_of, l_of, m_of, m_of, n_of, m_of], axis=0
            )

    widen(feat_ref, wide, tokens)
    for b in range(blocks):
        query = short_block(wide, taps_ref, 0, b * LANES, LANES)
        key = short_block(wide, taps_ref, 1, b * LANES, LANES)
        value = short_block(wide, taps_ref, 2, b * LANES, LANES)
        short_ref[0, b * LANES : (b + 1) * LANES, :] = query
        short_ref[1, b * LANES : (b + 1) * LANES, :] = key
        short_ref[2, b * LANES : (b + 1) * LANES, :] = value
        product = key * value
        adjoint = cot_ref[b * LANES : (b + 1) * LANES, :].astype(f32) * query
        if b == 0:
            inside = iota(0, (LANES, LANES)) >= 2
            product = jnp.where(inside, product, 0.0)
            adjoint = jnp.where(inside, adjoint, 0.0)
        z_t = jnp.transpose(product.astype(bf16))
        e_t = jnp.transpose(adjoint)
        e_high, e_low = split(e_t)
        at = slice(b * MEMBERS, (b + 1) * MEMBERS)
        for g in range(TILE_GROUPS):
            of = slice(g * MEMBERS, (g + 1) * MEMBERS)
            z_ref[g, at, :] = z_t[of]
            eh_ref[g, at, :] = e_high[of]
            el_ref[g, at, :] = e_low[of]

    for g in range(TILE_GROUPS):
        of = slice(g * MEMBERS, (g + 1) * MEMBERS)
        z, eh, el = z_ref[g], eh_ref[g], el_ref[g]
        left = jnp.concatenate(
            [
                jnp.concatenate([z, z], axis=1),
                jnp.concatenate([eh, eh], axis=1),
                jnp.concatenate([el, jnp.zeros_like(el)], axis=1),
            ],
            axis=0,
        )
        got = dot_nt(left, table_all[g])
        rows = z.shape[0]
        from_e = got[rows : 2 * rows] + got[2 * rows :]
        for b in range(blocks):
            at = slice(b * MEMBERS, (b + 1) * MEMBERS)
            opposite = slice((blocks - 1 - b) * MEMBERS, (blocks - b) * MEMBERS)
            own_all[b, of, :] = jnp.where(
                iota(1, (MEMBERS, LANES)) < 64, got[at], from_e[opposite]
            )

    span = per_member(jnp.exp(rate_tile * (-float(LANES))))
    in_lag = jnp.where(
        ((lane_row >= 48) & (lane_row < 64)) | ((lane_row >= 96) & (lane_row < 112)),
        float(LANES),
        0.0,
    )
    now = jnp.zeros((LANES, LANES), f32)
    lagged = jnp.zeros((LANES, LANES), f32)
    cross = jnp.zeros((LANES, LANES), f32)
    for b in range(blocks):
        own = own_all[b]
        cross = cross + now * pltpu.roll(own_all[blocks - 1 - b], 4 * MODES, 1)
        carry_ref[b] = now
        now = span * (now + lagged) + own
        if b < blocks - 1:
            lagged = span * lagged + in_lag * pltpu.roll(own, MODES, 1)
    cross_ref[...] = jnp.sum(cross.reshape(TILE_GROUPS, MEMBERS, LANES), axis=1)
    turned = jnp.transpose(now)
    state_ref[0:16] = turned[0:16]
    state_ref[16:32] = turned[48:64]
    state_ref[32:48] = turned[64:80]
    state_ref[48:64] = turned[96:112]

    tile = pl.program_id(0)
    half = later_ref.shape[1] // 2
    here = pl.ds(pl.multiple_of(tile * LANES, LANES), LANES)
    edges = jnp.concatenate(
        [wide[i, 8:10, :] for i in range(3)]
        + [cot_ref[0:2, :].astype(f32)]
        + [wide[i, 6 + tokens : 8 + tokens, :] for i in range(3)]
        + [jnp.zeros((2, LANES), f32)],
        axis=0,
    )
    for out_ref, main in ((later_ref, turned[0:16]), (earlier_ref, turned[64:80])):
        out_ref[0:16, here] = main
        out_ref[24:40, here] = edges

    def place(out_ref, lag_rows, start):
        for part in range(2):
            at = pl.ds(pl.multiple_of(start + part * half, LANES), LANES)
            out_ref[16:24, at] = lag_rows[8 * part : 8 * part + 8]

    @pl.when(tile * LANES < half)
    def _():
        place(later_ref, turned[48:64], tile * LANES)

    @pl.when(tile * LANES >= half)
    def _():
        place(earlier_ref, turned[96:112], tile * LANES - half)


def inside_kernel(
    z_whole, eh_whole, el_whole, rate_ref, gain_ref,
    inner_whole, grad_whole, diag_ref,
    toep_all, power_all, fold_all, rate_rows, gain_rows,
):
    z_ref, eh_ref, el_ref = of_tile(z_whole), of_tile(eh_whole), of_tile(el_whole)
    inner_ref, grad_ref = of_tile(inner_whole), of_tile(grad_whole)
    rate_tile, coef_tile = parameters(rate_ref, gain_ref, rate_rows, gain_rows)
    rates, coefs = per_mode(rate_tile), per_mode(coef_tile)
    lag = iota(1, (LANES, LANES)).astype(f32)
    row_at = iota(0, (LANES, LANES))
    lane_at = iota(1, (LANES, LANES))
    power = jnp.exp(-rates * lag)
    power_all[...] = power
    taps = jnp.sum((coefs * power).reshape(TILE_GROUPS, MODES, LANES), axis=1)
    for g in range(TILE_GROUPS):
        high, low = split(jnp.where(lane_at >= row_at, circulant(taps[g : g + 1]), 0.0))
        toep_all[g, 0:LANES, :] = high
        toep_all[g, LANES:, :] = low
    for g in range(TILE_GROUPS):
        z, eh, el = z_ref[g], eh_ref[g], el_ref[g]
        high = toep_all[g, 0:LANES, :]
        inner_ref[g] = dot_nn(jnp.concatenate([z, z], axis=1), toep_all[g])
        grad_ref[g] = dot_nt(
            jnp.concatenate([eh, el, eh], axis=1),
            jnp.concatenate([high, high, toep_all[g, LANES:, :]], axis=1),
        )
        z_back = jnp.transpose(z)
        gram = dot_nn(jnp.concatenate([z_back, z_back], axis=1), jnp.concatenate([eh, el], axis=0))
        gram = jnp.where(lane_at >= row_at, gram, 0.0)
        folded = [gram[0:8]] + [
            pltpu.roll(gram[8 * r : 8 * r + 8], LANES - 8 * r, 1) for r in range(1, LANES // 8)
        ]
        while len(folded) > 1:
            folded = [folded[i] + folded[i + 1] for i in range(0, len(folded), 2)]
        fold_all[8 * g : 8 * g + 8, :] = folded[0]

    corr = jnp.sum(sheared(fold_all[...], 8).reshape(TILE_GROUPS, 8, LANES), axis=1)
    weighted = power_all[...] * per_member(corr)
    first_col = jnp.sum(weighted, axis=1, keepdims=True)
    lag_col = jnp.sum(lag * weighted, axis=1, keepdims=True)
    mode_at = row_at % MODES
    placed = jnp.where(lane_at == mode_at, first_col, 0.0) + jnp.where(
        lane_at == mode_at + 32, lag_col, 0.0
    )
    diag_ref[...] = jnp.sum(placed.reshape(TILE_GROUPS, MODES, LANES), axis=1)


def exact_dot(left, right, dims):
    return lax.dot_general(
        left, right, (dims, ((), ())), precision=lax.Precision.HIGHEST, preferred_element_type=f32
    )


def join_kernel(
    tokens, me_ref, state_ref, own_ref, diag_ref, cross_ref, taps_ref, rate_ref, gain_ref, *refs
):
    gots, (bound_ref, local_ref, edges_all) = refs[:-3], refs[-3:]
    me = me_ref[0]
    channels = state_ref.shape[1]
    groups = rate_ref.shape[1]
    half = channels // 2
    chosen = (iota(0, (groups, channels)) == iota(1, (groups, channels)) // MEMBERS).astype(f32)
    rates = rate_ref[...]
    rate_cols = exact_dot(rates, chosen, ((1,), (0,)))
    edges_all[me] = own_ref[24:40]
    for key, got in enumerate(gots, 1):
        edges_all[me ^ key] = got[24:40]

    def tail_of(device):
        return jnp.where(device > 0, edges_all[jnp.maximum(device - 1, 0)][8:14], 0.0)

    def first_tokens(device):
        head, tail = edges_all[device], tail_of(device)
        shorts = []
        for i in range(3):
            tap = [taps_ref[i, j : j + 1, :] for j in range(3)]
            now, last = head[2 * i : 2 * i + 2], tail[2 * i : 2 * i + 2]
            shorts.append(
                (
                    tap[0] * now[0:1] + tap[1] * last[1:2] + tap[2] * last[0:1],
                    tap[0] * now[1:2] + tap[1] * now[0:1] + tap[2] * last[1:2],
                )
            )
        z = [(shorts[1][t] * shorts[2][t]).astype(bf16).astype(f32) for t in range(2)]
        e = [head[6 + t : 7 + t] * shorts[0][t] for t in range(2)]
        return z, e

    decay = jnp.exp(-rate_cols)
    decay_2 = decay * decay
    grow = jnp.exp(rate_cols)
    to_end = [jnp.exp(-rate_cols * float(tokens - 1)), jnp.exp(-rate_cols * float(tokens - 2))]
    from_start = [decay, decay_2]
    zero = jnp.zeros((MODES, channels), f32)
    zero_half = jnp.zeros((MODES, half), f32)
    s_prev, e_next = zero, zero
    s_lag, e_lag = zero_half, zero_half
    ahead = jnp.zeros((8, channels), f32)
    for key, got in enumerate(gots, 1):
        other = me ^ key
        earlier = other < me
        z, e = first_tokens(other)
        add = [
            jnp.where(earlier, to_end[t] * z[t], from_start[t] * e[t]) for t in range(2)
        ]
        steps = [
            jnp.where(earlier, tokens - 1 - t, t + 1).astype(f32) for t in range(2)
        ]
        added = steps[0] * add[0] + steps[1] * add[1]
        away = ((jnp.abs(me - other) - 1) * tokens).astype(f32)
        weight = jnp.exp(-rate_cols * away)
        part = weight * (got[0:16] + add[0] + add[1])

        def halved(value):
            return jnp.where(earlier, value[:, :half], value[:, half:])

        lagged = jnp.concatenate([got[16:24, :half], got[16:24, half:]], axis=0) + halved(added)
        lag_part = halved(weight) * lagged + away * halved(part)
        s_prev = s_prev + jnp.where(earlier, part, 0.0)
        s_lag = s_lag + jnp.where(earlier, lag_part, 0.0)
        e_next = e_next + jnp.where(earlier, 0.0, part)
        e_lag = e_lag + jnp.where(earlier, 0.0, lag_part)
        ahead = ahead + jnp.where(other == me + 1, got[24:32], 0.0)
    z, e = first_tokens(me)
    ends, lagged, moment_0, moment_1 = [state_ref[16 * i : 16 * i + 16] for i in range(4)]
    at_end = [to_end[t] * z[t] for t in range(2)]
    at_start = [from_start[t] * e[t] for t in range(2)]
    own_s = ends + at_end[0] + at_end[1]
    own_l = lagged + float(tokens - 1) * at_end[0] + float(tokens - 2) * at_end[1]
    own_m = moment_0 + at_start[0] + at_start[1]
    own_n = moment_1 + at_start[0] + 2.0 * at_start[1]
    early_0, early_1 = grow * z[0], grow * grow * z[1]
    early = early_0 + early_1
    bound_ref[0:16] = s_prev + early
    bound_ref[16:32] = e_next
    bound_ref[32:48] = own_s + jnp.exp(-rate_cols * float(tokens)) * s_prev
    bound_ref[48:56] = ahead
    bound_ref[56:62] = tail_of(me)
    bound_ref[62:64] = jnp.zeros((2, channels), f32)

    def joined(first_half, second_half):
        return jnp.concatenate([first_half[:, :half], second_half[:, half:]], axis=1)

    back = decay * e[1] * z[0]
    first_terms = (
        joined(own_m * s_prev, own_s * e_next) + moment_0 * early + e[0] * z[0] + e[1] * z[1] + back
    )
    lag_terms = (
        joined(own_n * s_prev, own_l * e_next)
        + jnp.concatenate([own_m[:, :half] * s_lag, own_s[:, half:] * e_lag], axis=1)
        + moment_1 * early
        - moment_0 * (early_0 + 2.0 * early_1)
        + back
    )
    sums = exact_dot(jnp.concatenate([first_terms, lag_terms], axis=0), chosen, ((1,), (1,)))
    own = jnp.transpose(cross_ref[...] + diag_ref[...])
    first = sums[0:16] + own[0:16]
    lag_sum = -(sums[16:32] + own[32:48] + own[48:64])
    root = jnp.sqrt(2.0 * rates)
    local_ref[0:16] = root * first
    local_ref[16:32] = gain_ref[...] * root * (0.5 * first + rates * lag_sum)


def output_kernel(
    first, start_ref, edge_ref, taps_ref, cot_ref, rate_ref, gain_ref,
    inner_whole, grad_whole, carry_whole, short_whole, bound_ref,
    *refs,
):
    mixer_ref, fgrad_ref, wide, adj, inner_t, grad_t, left_all, rate_rows, gain_rows = refs[-9:]
    inner_ref, grad_ref = of_tile(inner_whole, first), of_tile(grad_whole, first)
    carry_ref = carry_whole.at[pl.program_id(0) + first]
    short_ref = short_whole.at[pl.program_id(0) + first]
    tokens = cot_ref.shape[0]
    blocks = tokens // LANES
    rate_tile, coef_tile = parameters(rate_ref, gain_ref, rate_rows, gain_rows, first)
    rates, coefs = per_mode(rate_tile), per_mode(coef_tile)
    lag = iota(1, (LANES, LANES)).astype(f32)
    lane_at = iota(1, (LANES, LANES))
    is_low = ((lane_at >= 16) & (lane_at < 32)) | ((lane_at >= 80) & (lane_at < 96))
    before = bound_ref[0:16]
    after = bound_ref[16:32]
    gap = jnp.zeros((MODES, LANES), f32)
    stacked = jnp.concatenate([before, before, before, gap, after, after, gap, after], axis=0)
    turned = jnp.transpose(stacked)
    none_16 = jnp.zeros((MODES, LANES), bf16)
    none_64 = jnp.zeros((4 * MODES, LANES), bf16)
    member_rates = per_member(rate_tile)
    span = jnp.exp(member_rates * (-float(LANES)))
    from_others = turned
    for b in range(blocks):
        value = carry_ref[b] + from_others
        from_others = from_others * span
        high = value.astype(bf16).astype(f32)
        mixed = jnp.where(is_low, value - high, value).astype(bf16)
        for g in range(TILE_GROUPS):
            left_all[g, b * MEMBERS : (b + 1) * MEMBERS, :] = mixed[
                g * MEMBERS : (g + 1) * MEMBERS
            ]
    cz_parts = split(coefs * jnp.exp(-rates * (lag + 1.0)))
    ce_parts = split(coefs * jnp.exp(-rates * (LANES - 1.0 - lag)))
    for g in range(TILE_GROUPS):
        of = slice(g * MODES, (g + 1) * MODES)
        cz_high, cz_low = cz_parts[0][of], cz_parts[1][of]
        ce_high, ce_low = ce_parts[0][of], ce_parts[1][of]
        right = jnp.concatenate(
            [
                jnp.concatenate([cz_high, cz_high, cz_low, none_16, none_64], axis=0),
                jnp.concatenate([none_64, ce_high, ce_high, none_16, ce_low], axis=0),
            ],
            axis=1,
        )
        carried = dot_nn(left_all[g], right)
        for b in range(blocks):
            at = slice(b * MEMBERS, (b + 1) * MEMBERS)
            opposite = slice((blocks - 1 - b) * MEMBERS, (blocks - b) * MEMBERS)
            inner_t[b, of, :] = inner_ref[g, at, :] + carried[at, :LANES]
            grad_t[b, of, :] = grad_ref[g, at, :] + carried[opposite, LANES:]
    rates = jnp.transpose(member_rates)[0:MODES]
    coefs = jnp.transpose(per_member(coef_tile))[0:MODES]
    decay = jnp.exp(-rates)
    grow = jnp.exp(rates)
    state = bound_ref[32:48]
    sum_0 = jnp.sum(coefs, axis=0, keepdims=True)
    sum_1 = jnp.sum(coefs * decay, axis=0, keepdims=True)
    for i in range(3):
        wide[i, 0:8, :] = jnp.zeros((8, LANES), f32)
        wide[i, 6:8, :] = bound_ref[56 + 2 * i : 58 + 2 * i]
        wide[i, 8:16, :] = start_ref[i, 0:8, :].astype(f32)
    begun = [short_block(wide, taps_ref, i, 0, 8) for i in range(3)]
    z_own = (begun[1] * begun[2]).astype(bf16).astype(f32)
    e_own = cot_ref[0:8, :].astype(f32) * begun[0]
    sum_up = jnp.sum(coefs * grow, axis=0, keepdims=True)
    which = iota(0, (8, LANES))
    inner_fix = jnp.where(which == 0, -sum_up * z_own[1:2], 0.0)
    grad_fix = jnp.where(
        which == 0,
        sum_0 * e_own[0:1] + sum_1 * e_own[1:2],
        jnp.where(which == 1, sum_0 * e_own[1:2], 0.0),
    )
    for b in range(blocks):
        at = slice(b * LANES, (b + 1) * LANES)
        inner = jnp.transpose(inner_t[b])
        grad = jnp.transpose(grad_t[b])
        query, key, value = [short_ref[i, at, :] for i in range(3)]
        if b == 0:
            query, key, value = [
                jnp.concatenate([begun[i], short_ref[i, 8:LANES, :]], axis=0) for i in range(3)
            ]
            inner = jnp.concatenate([inner[0:8] + inner_fix, inner[8:]], axis=0)
            grad = jnp.concatenate([grad[0:8] + grad_fix, grad[8:]], axis=0)
        mixer_ref[at, :] = (query * inner).astype(bf16)
        adj[0, at, :] = cot_ref[at, :].astype(f32) * inner
        adj[1, at, :] = grad * value
        adj[2, at, :] = grad * key
    for i in range(3):
        wide[i, 0:8, :] = edge_ref[i, 8:16, :].astype(f32)
        wide[i, 8:16, :] = jnp.zeros((8, LANES), f32)
        wide[i, 8:10, :] = bound_ref[48 + 2 * i : 50 + 2 * i]
    query, key, value = [short_block(wide, taps_ref, i, 0, 8) for i in range(3)]
    z = (key * value).astype(bf16).astype(f32)
    upstream = jnp.concatenate([bound_ref[54:56], jnp.zeros((6, LANES), f32)], axis=0)
    e = upstream * query
    inner_0 = jnp.sum(coefs * decay * state, axis=0, keepdims=True) + sum_0 * z[0:1]
    inner_1 = (
        jnp.sum(coefs * decay * decay * state, axis=0, keepdims=True)
        + sum_1 * z[0:1]
        + sum_0 * z[1:2]
    )
    grad_0 = jnp.sum(coefs * grow * after, axis=0, keepdims=True)
    grad_1 = jnp.sum(coefs * grow * (grow * after - e[0:1]), axis=0, keepdims=True)
    inner_8 = jnp.where(which == 0, inner_0, jnp.where(which == 1, inner_1, 0.0))
    grad_8 = jnp.where(which == 0, grad_0, jnp.where(which == 1, grad_1, 0.0))
    adj[0, tokens : tokens + 8, :] = upstream * inner_8
    adj[1, tokens : tokens + 8, :] = grad_8 * value
    adj[2, tokens : tokens + 8, :] = grad_8 * key
    for b in range(blocks):
        start = b * LANES
        for i in range(3):
            fgrad_ref[i, start : start + LANES, :] = (
                taps_ref[i, 0:1, :] * adj[i, start : start + LANES, :]
                + taps_ref[i, 1:2, :] * adj[i, start + 1 : start + 1 + LANES, :]
                + taps_ref[i, 2:3, :] * adj[i, start + 2 : start + 2 + LANES, :]
            ).astype(bf16)


def resident(shape, dtype):
    return pltpu.VMEM(shape, dtype)


def sum_kernel(*refs):
    *terms, summed_ref, square_ref = refs
    terms = [term[...] for term in terms]
    while len(terms) > 1:
        terms = [terms[i] + terms[i + 1] for i in range(0, len(terms), 2)]
    summed_ref[...] = terms[0]
    square_ref[...] = jnp.broadcast_to(
        jnp.sum(jnp.sum(terms[0] * terms[0], axis=0, keepdims=True), axis=1, keepdims=True),
        square_ref.shape,
    )


def far(*arrays):
    return [pltpu.with_memory_space_constraint(array, pltpu.HBM) for array in arrays]


def near(*arrays):
    return [pltpu.with_memory_space_constraint(array, pltpu.VMEM) for array in arrays]


def swapped(value, axis, key):
    count = lax.axis_size(axis)
    return lax.ppermute(value, axis, [(i, i ^ key) for i in range(count)])


def per_device(features, short_taps, decay_rates, mode_gains, cotangent):
    tokens = features.shape[1]
    channels = features.shape[2]
    groups = decay_rates.shape[0]
    tiles = channels // LANES
    blocks = tokens // LANES
    ctx_count = lax.axis_size("ctx")
    ctx_index = lax.axis_index("ctx")

    me = ctx_index.astype(jnp.int32).reshape(1)
    rates, gains = decay_rates.T, mode_gains.T

    whole = pl.BlockSpec(memory_space=pltpu.VMEM)
    feat_spec = pl.BlockSpec((3, tokens, LANES), lambda j: (0, 0, j))
    taps_spec = pl.BlockSpec((3, 3, LANES), lambda j: (0, 0, j))
    cot_spec = pl.BlockSpec((tokens, LANES), lambda j: (0, j))
    table_spec = pl.BlockSpec((MODES, groups), lambda j: (0, 0))
    slot_spec = pl.BlockSpec((TILE_GROUPS, LANES), lambda j: (j, 0))
    me_spec = pl.BlockSpec(memory_space=pltpu.SMEM)
    rows = blocks * MEMBERS
    turned = resident((groups, rows, LANES), bf16)
    wide_turned = resident((groups, rows, LANES), f32)
    slots = jax.ShapeDtypeStruct((groups, LANES), f32)
    table_scratch = [pltpu.VMEM((LANES, LANES), f32), pltpu.VMEM((LANES, LANES), f32)]

    def room(mebibytes):
        return pltpu.CompilerParams(vmem_limit_bytes=mebibytes * 2**20)

    z, eh, el, carry, short, states, cross, later, early = pl.pallas_call(
        state_kernel,
        grid=(tiles,),
        in_specs=[feat_spec, taps_spec, cot_spec, table_spec, table_spec],
        out_specs=[
            whole,
            whole,
            whole,
            whole,
            whole,
            pl.BlockSpec((4 * MODES, LANES), lambda j: (0, j)),
            slot_spec,
            whole,
            whole,
        ],
        out_shape=[
            turned,
            turned,
            turned,
            resident((tiles, blocks, LANES, LANES), f32),
            resident((tiles, 3, tokens, LANES), f32),
            jax.ShapeDtypeStruct((4 * MODES, channels), f32),
            slots,
            resident((40, channels), f32),
            resident((40, channels), f32),
        ],
        scratch_shapes=[
            pltpu.VMEM((3, tokens + 8, LANES), f32),
            pltpu.VMEM((blocks, LANES, LANES), f32),
            pltpu.VMEM((TILE_GROUPS, LANES, 2 * LANES), bf16),
        ]
        + table_scratch,
        compiler_params=room(14),
        name="state_part",
    )(*far(features, short_taps, cotangent, rates, gains))

    gots = []
    for key in range(1, ctx_count):
        sent = jnp.where((ctx_index ^ key) < ctx_index, early, later)
        gots.append(swapped(sent, "ctx", key))

    inner, grad, diag = pl.pallas_call(
        inside_kernel,
        grid=(tiles,),
        in_specs=[whole, whole, whole, table_spec, table_spec],
        out_specs=[whole, whole, slot_spec],
        out_shape=[wide_turned, wide_turned, slots],
        scratch_shapes=[
            pltpu.VMEM((TILE_GROUPS, 2 * LANES, LANES), bf16),
            pltpu.VMEM((LANES, LANES), f32),
            pltpu.VMEM((8 * TILE_GROUPS, LANES), f32),
        ]
        + table_scratch,
        compiler_params=room(14),
        cost_estimate=pl.CostEstimate(
            flops=2 * groups * rows * LANES * LANES * 7, bytes_accessed=14 * 2**20, transcendentals=0
        ),
        name="inside_part",
    )(*near(z, eh, el), *far(rates, gains))

    bound, local = pl.pallas_call(
        functools.partial(join_kernel, tokens),
        in_specs=[me_spec] + [whole] * (7 + len(gots)),
        out_specs=[whole, whole],
        out_shape=[
            jax.ShapeDtypeStruct((64, channels), f32),
            jax.ShapeDtypeStruct((2 * MODES, groups), f32),
        ],
        scratch_shapes=[pltpu.VMEM((ctx_count, 16, channels), f32)],
        compiler_params=room(14),
        name="join_part",
    )(me, states, later, diag, cross, short_taps, rates, gains, *gots)

    def outputs(first, count, *written):
        columns = lambda j: (0, j + first)
        layers = lambda j: (0, 0, j + first)
        mine = [pl.BlockSpec((tokens, LANES), columns), pl.BlockSpec((3, tokens, LANES), layers)]
        return pl.pallas_call(
            functools.partial(output_kernel, first),
            grid=(count,),
            in_specs=[
                pl.BlockSpec((3, 16, LANES), layers),
                pl.BlockSpec((3, 16, LANES), lambda j: (0, tokens // 16 - 1, j + first)),
                pl.BlockSpec((3, 3, LANES), layers),
                pl.BlockSpec((tokens, LANES), columns),
                table_spec,
                table_spec,
                whole,
                whole,
                whole,
                whole,
                pl.BlockSpec((64, LANES), columns),
            ]
            + [pl.BlockSpec(memory_space=pl.ANY)] * len(written),
            out_specs=mine,
            out_shape=[
                jax.ShapeDtypeStruct((tokens, channels), bf16),
                jax.ShapeDtypeStruct((3, tokens, channels), bf16),
            ],
            scratch_shapes=[
                pltpu.VMEM((3, 16, LANES), f32),
                pltpu.VMEM((3, tokens + 8, LANES), f32),
                pltpu.VMEM((blocks, LANES, LANES), f32),
                pltpu.VMEM((blocks, LANES, LANES), f32),
                pltpu.VMEM((TILE_GROUPS, rows, LANES), bf16),
            ]
            + table_scratch,
            compiler_params=room(14),
            input_output_aliases={11: 0, 12: 1} if written else {},
            cost_estimate=pl.CostEstimate(
                flops=2 * count * TILE_GROUPS * rows * LANES * LANES * 8,
                bytes_accessed=count * 4 * 2**20,
                transcendentals=0,
            ),
            name="output_part",
        )(
            *far(features, features, short_taps, cotangent, rates, gains),
            *near(inner, grad, carry, short),
            bound,
            *written,
        )

    half = tiles // 2
    terms = [local] + [swapped(local, "ctx", key) for key in range(1, ctx_count)]
    written = outputs(0, half)
    terms, written = lax.optimization_barrier((terms, written))
    summed, squares = pl.pallas_call(
        sum_kernel,
        in_specs=[whole] * len(terms),
        out_specs=[whole, whole],
        out_shape=[
            jax.ShapeDtypeStruct((2 * MODES, groups), f32),
            jax.ShapeDtypeStruct((1, groups), f32),
        ],
        compiler_params=room(14),
        name="sum_part",
    )(*terms)
    fsdp_count = lax.axis_size("fsdp")
    step = 1
    while step * 4 < fsdp_count:
        squares = squares + swapped(squares, "fsdp", step)
        step *= 2
    squares, written = lax.optimization_barrier((squares, written))
    parts = [squares] + [swapped(squares, "fsdp", key) for key in range(step, fsdp_count, step)]
    mixer, feature_grads = outputs(half, tiles - half, *written)
    while len(parts) > 1:
        parts = [parts[i] + parts[i + 1] for i in range(0, len(parts), 2)]
    entry_count = 2 * groups * MODES * fsdp_count
    clipped = summed * jnp.minimum(1.0, lax.rsqrt(parts[0] / entry_count + 1e-06))
    return (mixer, feature_grads, clipped[:MODES].T, clipped[MODES:].T)


def solution(mesh):
    return jax.shard_map(
        per_device,
        mesh=mesh,
        in_specs=(
            P(None, "ctx", "fsdp"),
            P(None, None, "fsdp"),
            P("fsdp", None),
            P("fsdp", None),
            P("ctx", "fsdp"),
        ),
        out_specs=(P("ctx", "fsdp"), P(None, "ctx", "fsdp"), P("fsdp", None), P("fsdp", None)),
        check_vma=False,
    )
```

```python
import functools

import jax
import jax.numpy as jnp
from jax import lax
from jax.experimental import pallas as pl
from jax.experimental.pallas import tpu as pltpu
from jax.sharding import PartitionSpec as P

LANES = 128
MODES = 16
MEMBERS = 16
TILE_GROUPS = LANES // MEMBERS
ROWS = LANES
f32 = jnp.float32
bf16 = jnp.bfloat16


def split(value):
    high = value.astype(bf16)
    return high, (value - high.astype(f32)).astype(bf16)


def dot_nt(left, right):
    return lax.dot_general(left, right, (((1,), (1,)), ((), ())), preferred_element_type=f32)


def dot_tn(left, right):
    return lax.dot_general(left, right, (((0,), (0,)), ((), ())), preferred_element_type=f32)


def dot_nn(left, right):
    return lax.dot_general(left, right, (((1,), (0,)), ((), ())), preferred_element_type=f32)


def iota(axis, shape):
    return lax.broadcasted_iota(jnp.int32, shape, axis)


def widen(feat_ref, wide, tokens):
    for i in range(3):
        wide[i, 0:8, :] = jnp.zeros((8, LANES), f32)
        wide[i, 8 : 8 + tokens, :] = feat_ref[i].astype(f32)


def short_block(wide, taps_ref, i, start, count):
    return (
        taps_ref[i, 0:1, :] * wide[i, start + 8 : start + 8 + count, :]
        + taps_ref[i, 1:2, :] * wide[i, start + 7 : start + 7 + count, :]
        + taps_ref[i, 2:3, :] * wide[i, start + 6 : start + 6 + count, :]
    )


def sheared(row8, period):
    which = iota(0, row8.shape) % period
    for bit in (1, 2, 4):
        row8 = jnp.where((which & bit) != 0, pltpu.roll(row8, LANES - bit, 1), row8)
    return row8


def circulant(row):
    return pltpu.roll(jnp.broadcast_to(row, (LANES, LANES)), 0, 1, stride=1, stride_axis=0)


def of_tile(whole, first=0):
    return whole.at[pl.ds((pl.program_id(0) + first) * TILE_GROUPS, TILE_GROUPS)]


def table_rows(source_ref, rows_ref):
    tall = jnp.concatenate([source_ref[...]] * (LANES // MODES), axis=0)
    missing = LANES - tall.shape[1]
    if missing:
        tall = jnp.concatenate([tall, jnp.zeros((LANES, missing), f32)], axis=1)
    rows_ref[...] = jnp.transpose(tall)


def parameters(rate_ref, gain_ref, rate_rows, gain_rows, first=0):
    tile = pl.program_id(0) + first

    @pl.when(pl.program_id(0) == 0)
    def _():
        table_rows(rate_ref, rate_rows)
        table_rows(gain_ref, gain_rows)

    at = pl.ds(pl.multiple_of(tile * TILE_GROUPS, TILE_GROUPS), TILE_GROUPS)
    rates = rate_rows[at, :]
    return rates, gain_rows[at, :] * jnp.sqrt(2.0 * rates)


def per_mode(rows):
    own = iota(0, (TILE_GROUPS, LANES)) == iota(1, (TILE_GROUPS, LANES)) // MODES
    flat = jnp.sum(jnp.where(own, rows, 0.0), axis=0, keepdims=True)
    return jnp.transpose(jnp.broadcast_to(flat, (LANES, LANES)))


def per_member(rows):
    return jnp.concatenate(
        [jnp.broadcast_to(rows[g : g + 1], (MEMBERS, LANES)) for g in range(TILE_GROUPS)], axis=0
    )


def state_kernel(
    feat_ref, taps_ref, cot_ref, rate_ref, gain_ref,
    z_whole, eh_whole, el_whole, carry_whole, short_whole, state_ref, cross_ref,
    later_ref, earlier_ref,
    wide, own_all, table_all, rate_rows, gain_rows,
):
    z_ref, eh_ref, el_ref = of_tile(z_whole), of_tile(eh_whole), of_tile(el_whole)
    carry_ref = carry_whole.at[pl.program_id(0)]
    short_ref = short_whole.at[pl.program_id(0)]
    tokens = feat_ref.shape[1]
    blocks = tokens // LANES
    rate_tile, _ = parameters(rate_ref, gain_ref, rate_rows, gain_rows)
    rates = per_mode(rate_tile)
    lag = iota(1, (LANES, LANES)).astype(f32)
    lane_at = iota(1, (LANES, LANES))
    lane_row = iota(1, (1, LANES))

    back = jnp.exp(-rates * (LANES - 1.0 - lag))
    after = jnp.exp(-rates * (lag + 1.0))
    s_parts = split(back)
    l_parts = split((LANES - 1.0 - lag) * back)
    m_parts = split(after)
    n_parts = split((lag + 1.0) * after)
    for g in range(TILE_GROUPS):
        of = slice(g * MODES, (g + 1) * MODES)
        for part in range(2):
            s_of, l_of = s_parts[part][of], l_parts[part][of]
            m_of, n_of = m_parts[part][of], n_parts[part][of]
            table_all[g, :, part * LANES : (part + 1) * LANES] = jnp.concatenate(
                [s_of, s_of, s_of, l_of, m_of, m_of, n_of, m_of], axis=0
            )

    widen(feat_ref, wide, tokens)
    for b in range(blocks):
        query = short_block(wide, taps_ref, 0, b * LANES, LANES)
        key = short_block(wide, taps_ref, 1, b * LANES, LANES)
        value = short_block(wide, taps_ref, 2, b * LANES, LANES)
        short_ref[0, b * LANES : (b + 1) * LANES, :] = query
        short_ref[1, b * LANES : (b + 1) * LANES, :] = key
        short_ref[2, b * LANES : (b + 1) * LANES, :] = value
        product = key * value
        adjoint = cot_ref[b * LANES : (b + 1) * LANES, :].astype(f32) * query
        if b == 0:
            inside = iota(0, (LANES, LANES)) >= 2
            product = jnp.where(inside, product, 0.0)
            adjoint = jnp.where(inside, adjoint, 0.0)
        z_t = jnp.transpose(product.astype(bf16))
        e_t = jnp.transpose(adjoint)
        e_high, e_low = split(e_t)
        at = slice(b * MEMBERS, (b + 1) * MEMBERS)
        for g in range(TILE_GROUPS):
            of = slice(g * MEMBERS, (g + 1) * MEMBERS)
            z_ref[g, at, :] = z_t[of]
            eh_ref[g, at, :] = e_high[of]
            el_ref[g, at, :] = e_low[of]

    for g in range(TILE_GROUPS):
        of = slice(g * MEMBERS, (g + 1) * MEMBERS)
        z, eh, el = z_ref[g], eh_ref[g], el_ref[g]
        left = jnp.concatenate(
            [
                jnp.concatenate([z, z], axis=1),
                jnp.concatenate([eh, eh], axis=1),
                jnp.concatenate([el, jnp.zeros_like(el)], axis=1),
            ],
            axis=0,
        )
        got = dot_nt(left, table_all[g])
        rows = z.shape[0]
        from_e = got[rows : 2 * rows] + got[2 * rows :]
        for b in range(blocks):
            at = slice(b * MEMBERS, (b + 1) * MEMBERS)
            opposite = slice((blocks - 1 - b) * MEMBERS, (blocks - b) * MEMBERS)
            own_all[b, of, :] = jnp.where(
                iota(1, (MEMBERS, LANES)) < 64, got[at], from_e[opposite]
            )

    span = per_member(jnp.exp(rate_tile * (-float(LANES))))
    in_lag = jnp.where(
        ((lane_row >= 48) & (lane_row < 64)) | ((lane_row >= 96) & (lane_row < 112)),
        float(LANES),
        0.0,
    )
    now = jnp.zeros((LANES, LANES), f32)
    lagged = jnp.zeros((LANES, LANES), f32)
    cross = jnp.zeros((LANES, LANES), f32)
    for b in range(blocks):
        own = own_all[b]
        cross = cross + now * pltpu.roll(own_all[blocks - 1 - b], 4 * MODES, 1)
        carry_ref[b] = now
        now = span * (now + lagged) + own
        if b < blocks - 1:
            lagged = span * lagged + in_lag * pltpu.roll(own, MODES, 1)
    cross_ref[...] = jnp.sum(cross.reshape(TILE_GROUPS, MEMBERS, LANES), axis=1)
    turned = jnp.transpose(now)
    state_ref[0:16] = turned[0:16]
    state_ref[16:32] = turned[48:64]
    state_ref[32:48] = turned[64:80]
    state_ref[48:64] = turned[96:112]

    tile = pl.program_id(0)
    half = later_ref.shape[1] // 2
    here = pl.ds(pl.multiple_of(tile * LANES, LANES), LANES)
    edges = jnp.concatenate(
        [wide[i, 8:10, :] for i in range(3)]
        + [cot_ref[0:2, :].astype(f32)]
        + [wide[i, 6 + tokens : 8 + tokens, :] for i in range(3)]
        + [jnp.zeros((2, LANES), f32)],
        axis=0,
    )
    for out_ref, main in ((later_ref, turned[0:16]), (earlier_ref, turned[64:80])):
        out_ref[0:16, here] = main
        out_ref[24:40, here] = edges

    def place(out_ref, lag_rows, start):
        for part in range(2):
            at = pl.ds(pl.multiple_of(start + part * half, LANES), LANES)
            out_ref[16:24, at] = lag_rows[8 * part : 8 * part + 8]

    @pl.when(tile * LANES < half)
    def _():
        place(later_ref, turned[48:64], tile * LANES)

    @pl.when(tile * LANES >= half)
    def _():
        place(earlier_ref, turned[96:112], tile * LANES - half)


def inside_kernel(
    z_whole, eh_whole, el_whole, rate_ref, gain_ref,
    inner_whole, grad_whole, diag_ref,
    toep_all, power_all, fold_all, rate_rows, gain_rows,
):
    z_ref, eh_ref, el_ref = of_tile(z_whole), of_tile(eh_whole), of_tile(el_whole)
    inner_ref, grad_ref = of_tile(inner_whole), of_tile(grad_whole)
    rate_tile, coef_tile = parameters(rate_ref, gain_ref, rate_rows, gain_rows)
    rates, coefs = per_mode(rate_tile), per_mode(coef_tile)
    lag = iota(1, (LANES, LANES)).astype(f32)
    row_at = iota(0, (LANES, LANES))
    lane_at = iota(1, (LANES, LANES))
    power = jnp.exp(-rates * lag)
    power_all[...] = power
    taps = jnp.sum((coefs * power).reshape(TILE_GROUPS, MODES, LANES), axis=1)
    for g in range(TILE_GROUPS):
        z_back = jnp.transpose(z_ref[g])
        gram = dot_nn(
            jnp.concatenate([z_back, z_back], axis=1),
            jnp.concatenate([eh_ref[g], el_ref[g]], axis=0),
        )
        gram = jnp.where(lane_at >= row_at, gram, 0.0)
        folded = [gram[0:8]] + [
            pltpu.roll(gram[8 * r : 8 * r + 8], LANES - 8 * r, 1) for r in range(1, LANES // 8)
        ]
        while len(folded) > 1:
            folded = [folded[i] + folded[i + 1] for i in range(0, len(folded), 2)]
        fold_all[8 * g : 8 * g + 8, :] = folded[0]
    for g in range(TILE_GROUPS):
        high, low = split(jnp.where(lane_at >= row_at, circulant(taps[g : g + 1]), 0.0))
        toep_all[g, 0:LANES, :] = high
        toep_all[g, LANES:, :] = low
    for g in range(TILE_GROUPS):
        z, eh, el = z_ref[g], eh_ref[g], el_ref[g]
        high = toep_all[g, 0:LANES, :]
        inner_ref[g] = dot_nn(jnp.concatenate([z, z], axis=1), toep_all[g])
        grad_ref[g] = dot_nt(
            jnp.concatenate([eh, el, eh], axis=1),
            jnp.concatenate([high, high, toep_all[g, LANES:, :]], axis=1),
        )
    corr = jnp.sum(sheared(fold_all[...], 8).reshape(TILE_GROUPS, 8, LANES), axis=1)
    weighted = power_all[...] * per_member(corr)
    first_col = jnp.sum(weighted, axis=1, keepdims=True)
    lag_col = jnp.sum(lag * weighted, axis=1, keepdims=True)
    mode_at = row_at % MODES
    placed = jnp.where(lane_at == mode_at, first_col, 0.0) + jnp.where(
        lane_at == mode_at + 32, lag_col, 0.0
    )
    diag_ref[...] = jnp.sum(placed.reshape(TILE_GROUPS, MODES, LANES), axis=1)


def exact_dot(left, right, dims):
    return lax.dot_general(
        left, right, (dims, ((), ())), precision=lax.Precision.HIGHEST, preferred_element_type=f32
    )


def join_kernel(
    tokens, me_ref, state_ref, own_ref, diag_ref, cross_ref, taps_ref, rate_ref, gain_ref, *refs
):
    gots, (bound_ref, local_ref, edges_all) = refs[:-3], refs[-3:]
    me = me_ref[0]
    channels = state_ref.shape[1]
    groups = rate_ref.shape[1]
    half = channels // 2
    chosen = (iota(0, (groups, channels)) == iota(1, (groups, channels)) // MEMBERS).astype(f32)
    rates = rate_ref[...]
    rate_cols = exact_dot(rates, chosen, ((1,), (0,)))
    edges_all[me] = own_ref[24:40]
    for key, got in enumerate(gots, 1):
        edges_all[me ^ key] = got[24:40]

    def tail_of(device):
        return jnp.where(device > 0, edges_all[jnp.maximum(device - 1, 0)][8:14], 0.0)

    def first_tokens(device):
        head, tail = edges_all[device], tail_of(device)
        shorts = []
        for i in range(3):
            tap = [taps_ref[i, j : j + 1, :] for j in range(3)]
            now, last = head[2 * i : 2 * i + 2], tail[2 * i : 2 * i + 2]
            shorts.append(
                (
                    tap[0] * now[0:1] + tap[1] * last[1:2] + tap[2] * last[0:1],
                    tap[0] * now[1:2] + tap[1] * now[0:1] + tap[2] * last[1:2],
                )
            )
        z = [(shorts[1][t] * shorts[2][t]).astype(bf16).astype(f32) for t in range(2)]
        e = [head[6 + t : 7 + t] * shorts[0][t] for t in range(2)]
        return z, e

    decay = jnp.exp(-rate_cols)
    decay_2 = decay * decay
    grow = jnp.exp(rate_cols)
    to_end = [jnp.exp(-rate_cols * float(tokens - 1)), jnp.exp(-rate_cols * float(tokens - 2))]
    from_start = [decay, decay_2]
    zero = jnp.zeros((MODES, channels), f32)
    zero_half = jnp.zeros((MODES, half), f32)
    s_prev, e_next = zero, zero
    s_lag, e_lag = zero_half, zero_half
    ahead = jnp.zeros((8, channels), f32)
    for key, got in enumerate(gots, 1):
        other = me ^ key
        earlier = other < me
        z, e = first_tokens(other)
        add = [
            jnp.where(earlier, to_end[t] * z[t], from_start[t] * e[t]) for t in range(2)
        ]
        steps = [
            jnp.where(earlier, tokens - 1 - t, t + 1).astype(f32) for t in range(2)
        ]
        added = steps[0] * add[0] + steps[1] * add[1]
        away = ((jnp.abs(me - other) - 1) * tokens).astype(f32)
        weight = jnp.exp(-rate_cols * away)
        part = weight * (got[0:16] + add[0] + add[1])

        def halved(value):
            return jnp.where(earlier, value[:, :half], value[:, half:])

        lagged = jnp.concatenate([got[16:24, :half], got[16:24, half:]], axis=0) + halved(added)
        lag_part = halved(weight) * lagged + away * halved(part)
        s_prev = s_prev + jnp.where(earlier, part, 0.0)
        s_lag = s_lag + jnp.where(earlier, lag_part, 0.0)
        e_next = e_next + jnp.where(earlier, 0.0, part)
        e_lag = e_lag + jnp.where(earlier, 0.0, lag_part)
        ahead = ahead + jnp.where(other == me + 1, got[24:32], 0.0)
    z, e = first_tokens(me)
    ends, lagged, moment_0, moment_1 = [state_ref[16 * i : 16 * i + 16] for i in range(4)]
    at_end = [to_end[t] * z[t] for t in range(2)]
    at_start = [from_start[t] * e[t] for t in range(2)]
    own_s = ends + at_end[0] + at_end[1]
    own_l = lagged + float(tokens - 1) * at_end[0] + float(tokens - 2) * at_end[1]
    own_m = moment_0 + at_start[0] + at_start[1]
    own_n = moment_1 + at_start[0] + 2.0 * at_start[1]
    early_0, early_1 = grow * z[0], grow * grow * z[1]
    early = early_0 + early_1
    bound_ref[0:16] = s_prev + early
    bound_ref[16:32] = e_next
    bound_ref[32:48] = own_s + jnp.exp(-rate_cols * float(tokens)) * s_prev
    bound_ref[48:56] = ahead
    bound_ref[56:62] = tail_of(me)
    bound_ref[62:64] = jnp.zeros((2, channels), f32)

    def joined(first_half, second_half):
        return jnp.concatenate([first_half[:, :half], second_half[:, half:]], axis=1)

    back = decay * e[1] * z[0]
    first_terms = (
        joined(own_m * s_prev, own_s * e_next) + moment_0 * early + e[0] * z[0] + e[1] * z[1] + back
    )
    lag_terms = (
        joined(own_n * s_prev, own_l * e_next)
        + jnp.concatenate([own_m[:, :half] * s_lag, own_s[:, half:] * e_lag], axis=1)
        + moment_1 * early
        - moment_0 * (early_0 + 2.0 * early_1)
        + back
    )
    sums = exact_dot(jnp.concatenate([first_terms, lag_terms], axis=0), chosen, ((1,), (1,)))
    own = jnp.transpose(cross_ref[...] + diag_ref[...])
    first = sums[0:16] + own[0:16]
    lag_sum = -(sums[16:32] + own[32:48] + own[48:64])
    root = jnp.sqrt(2.0 * rates)
    local_ref[0:16] = root * first
    local_ref[16:32] = gain_ref[...] * root * (0.5 * first + rates * lag_sum)


def output_kernel(
    first, start_ref, edge_ref, taps_ref, cot_ref, rate_ref, gain_ref,
    inner_whole, grad_whole, carry_whole, short_whole, bound_ref,
    *refs,
):
    mixer_ref, fgrad_ref, wide, adj, inner_t, grad_t, left_all, rate_rows, gain_rows = refs[-9:]
    inner_ref, grad_ref = of_tile(inner_whole, first), of_tile(grad_whole, first)
    carry_ref = carry_whole.at[pl.program_id(0) + first]
    short_ref = short_whole.at[pl.program_id(0) + first]
    tokens = cot_ref.shape[0]
    blocks = tokens // LANES
    rate_tile, coef_tile = parameters(rate_ref, gain_ref, rate_rows, gain_rows, first)
    rates, coefs = per_mode(rate_tile), per_mode(coef_tile)
    lag = iota(1, (LANES, LANES)).astype(f32)
    lane_at = iota(1, (LANES, LANES))
    is_low = ((lane_at >= 16) & (lane_at < 32)) | ((lane_at >= 80) & (lane_at < 96))
    before = bound_ref[0:16]
    after = bound_ref[16:32]
    gap = jnp.zeros((MODES, LANES), f32)
    stacked = jnp.concatenate([before, before, before, gap, after, after, gap, after], axis=0)
    turned = jnp.transpose(stacked)
    none_16 = jnp.zeros((MODES, LANES), bf16)
    none_64 = jnp.zeros((4 * MODES, LANES), bf16)
    member_rates = per_member(rate_tile)
    span = jnp.exp(member_rates * (-float(LANES)))
    from_others = turned
    for b in range(blocks):
        value = carry_ref[b] + from_others
        from_others = from_others * span
        high = value.astype(bf16).astype(f32)
        mixed = jnp.where(is_low, value - high, value).astype(bf16)
        for g in range(TILE_GROUPS):
            left_all[g, b * MEMBERS : (b + 1) * MEMBERS, :] = mixed[
                g * MEMBERS : (g + 1) * MEMBERS
            ]
    cz_parts = split(coefs * jnp.exp(-rates * (lag + 1.0)))
    ce_parts = split(coefs * jnp.exp(-rates * (LANES - 1.0 - lag)))
    for g in range(TILE_GROUPS):
        of = slice(g * MODES, (g + 1) * MODES)
        cz_high, cz_low = cz_parts[0][of], cz_parts[1][of]
        ce_high, ce_low = ce_parts[0][of], ce_parts[1][of]
        right = jnp.concatenate(
            [
                jnp.concatenate([cz_high, cz_high, cz_low, none_16, none_64], axis=0),
                jnp.concatenate([none_64, ce_high, ce_high, none_16, ce_low], axis=0),
            ],
            axis=1,
        )
        carried = dot_nn(left_all[g], right)
        for b in range(blocks):
            at = slice(b * MEMBERS, (b + 1) * MEMBERS)
            opposite = slice((blocks - 1 - b) * MEMBERS, (blocks - b) * MEMBERS)
            inner_t[b, of, :] = inner_ref[g, at, :] + carried[at, :LANES]
            grad_t[b, of, :] = grad_ref[g, at, :] + carried[opposite, LANES:]
    rates = jnp.transpose(member_rates)[0:MODES]
    coefs = jnp.transpose(per_member(coef_tile))[0:MODES]
    decay = jnp.exp(-rates)
    grow = jnp.exp(rates)
    state = bound_ref[32:48]
    sum_0 = jnp.sum(coefs, axis=0, keepdims=True)
    sum_1 = jnp.sum(coefs * decay, axis=0, keepdims=True)
    for i in range(3):
        wide[i, 0:8, :] = jnp.zeros((8, LANES), f32)
        wide[i, 6:8, :] = bound_ref[56 + 2 * i : 58 + 2 * i]
        wide[i, 8:16, :] = start_ref[i, 0:8, :].astype(f32)
    begun = [short_block(wide, taps_ref, i, 0, 8) for i in range(3)]
    z_own = (begun[1] * begun[2]).astype(bf16).astype(f32)
    e_own = cot_ref[0:8, :].astype(f32) * begun[0]
    sum_up = jnp.sum(coefs * grow, axis=0, keepdims=True)
    which = iota(0, (8, LANES))
    inner_fix = jnp.where(which == 0, -sum_up * z_own[1:2], 0.0)
    grad_fix = jnp.where(
        which == 0,
        sum_0 * e_own[0:1] + sum_1 * e_own[1:2],
        jnp.where(which == 1, sum_0 * e_own[1:2], 0.0),
    )
    for b in range(blocks):
        at = slice(b * LANES, (b + 1) * LANES)
        inner = jnp.transpose(inner_t[b])
        grad = jnp.transpose(grad_t[b])
        query, key, value = [short_ref[i, at, :] for i in range(3)]
        if b == 0:
            query, key, value = [
                jnp.concatenate([begun[i], short_ref[i, 8:LANES, :]], axis=0) for i in range(3)
            ]
            inner = jnp.concatenate([inner[0:8] + inner_fix, inner[8:]], axis=0)
            grad = jnp.concatenate([grad[0:8] + grad_fix, grad[8:]], axis=0)
        mixer_ref[at, :] = (query * inner).astype(bf16)
        adj[0, at, :] = cot_ref[at, :].astype(f32) * inner
        adj[1, at, :] = grad * value
        adj[2, at, :] = grad * key
    for i in range(3):
        wide[i, 0:8, :] = edge_ref[i, 8:16, :].astype(f32)
        wide[i, 8:16, :] = jnp.zeros((8, LANES), f32)
        wide[i, 8:10, :] = bound_ref[48 + 2 * i : 50 + 2 * i]
    query, key, value = [short_block(wide, taps_ref, i, 0, 8) for i in range(3)]
    z = (key * value).astype(bf16).astype(f32)
    upstream = jnp.concatenate([bound_ref[54:56], jnp.zeros((6, LANES), f32)], axis=0)
    e = upstream * query
    inner_0 = jnp.sum(coefs * decay * state, axis=0, keepdims=True) + sum_0 * z[0:1]
    inner_1 = (
        jnp.sum(coefs * decay * decay * state, axis=0, keepdims=True)
        + sum_1 * z[0:1]
        + sum_0 * z[1:2]
    )
    grad_0 = jnp.sum(coefs * grow * after, axis=0, keepdims=True)
    grad_1 = jnp.sum(coefs * grow * (grow * after - e[0:1]), axis=0, keepdims=True)
    inner_8 = jnp.where(which == 0, inner_0, jnp.where(which == 1, inner_1, 0.0))
    grad_8 = jnp.where(which == 0, grad_0, jnp.where(which == 1, grad_1, 0.0))
    adj[0, tokens : tokens + 8, :] = upstream * inner_8
    adj[1, tokens : tokens + 8, :] = grad_8 * value
    adj[2, tokens : tokens + 8, :] = grad_8 * key
    for b in range(blocks):
        start = b * LANES
        for i in range(3):
            fgrad_ref[i, start : start + LANES, :] = (
                taps_ref[i, 0:1, :] * adj[i, start : start + LANES, :]
                + taps_ref[i, 1:2, :] * adj[i, start + 1 : start + 1 + LANES, :]
                + taps_ref[i, 2:3, :] * adj[i, start + 2 : start + 2 + LANES, :]
            ).astype(bf16)


def resident(shape, dtype):
    return pltpu.VMEM(shape, dtype)


def sum_kernel(*refs):
    *terms, summed_ref, square_ref = refs
    terms = [term[...] for term in terms]
    while len(terms) > 1:
        terms = [terms[i] + terms[i + 1] for i in range(0, len(terms), 2)]
    summed_ref[...] = terms[0]
    square_ref[...] = jnp.broadcast_to(
        jnp.sum(jnp.sum(terms[0] * terms[0], axis=0, keepdims=True), axis=1, keepdims=True),
        square_ref.shape,
    )


def far(*arrays):
    return [pltpu.with_memory_space_constraint(array, pltpu.HBM) for array in arrays]


def near(*arrays):
    return [pltpu.with_memory_space_constraint(array, pltpu.VMEM) for array in arrays]


def swapped(value, axis, key):
    count = lax.axis_size(axis)
    return lax.ppermute(value, axis, [(i, i ^ key) for i in range(count)])


def per_device(features, short_taps, decay_rates, mode_gains, cotangent):
    tokens = features.shape[1]
    channels = features.shape[2]
    groups = decay_rates.shape[0]
    tiles = channels // LANES
    blocks = tokens // LANES
    ctx_count = lax.axis_size("ctx")
    ctx_index = lax.axis_index("ctx")

    me = ctx_index.astype(jnp.int32).reshape(1)
    rates, gains = decay_rates.T, mode_gains.T

    whole = pl.BlockSpec(memory_space=pltpu.VMEM)
    feat_spec = pl.BlockSpec((3, tokens, LANES), lambda j: (0, 0, j))
    taps_spec = pl.BlockSpec((3, 3, LANES), lambda j: (0, 0, j))
    cot_spec = pl.BlockSpec((tokens, LANES), lambda j: (0, j))
    table_spec = pl.BlockSpec((MODES, groups), lambda j: (0, 0))
    slot_spec = pl.BlockSpec((TILE_GROUPS, LANES), lambda j: (j, 0))
    me_spec = pl.BlockSpec(memory_space=pltpu.SMEM)
    rows = blocks * MEMBERS
    turned = resident((groups, rows, LANES), bf16)
    wide_turned = resident((groups, rows, LANES), f32)
    slots = jax.ShapeDtypeStruct((groups, LANES), f32)
    table_scratch = [pltpu.VMEM((LANES, LANES), f32), pltpu.VMEM((LANES, LANES), f32)]

    def room(mebibytes):
        return pltpu.CompilerParams(vmem_limit_bytes=mebibytes * 2**20)

    z, eh, el, carry, short, states, cross, later, early = pl.pallas_call(
        state_kernel,
        grid=(tiles,),
        in_specs=[feat_spec, taps_spec, cot_spec, table_spec, table_spec],
        out_specs=[
            whole,
            whole,
            whole,
            whole,
            whole,
            pl.BlockSpec((4 * MODES, LANES), lambda j: (0, j)),
            slot_spec,
            whole,
            whole,
        ],
        out_shape=[
            turned,
            turned,
            turned,
            resident((tiles, blocks, LANES, LANES), f32),
            resident((tiles, 3, tokens, LANES), f32),
            jax.ShapeDtypeStruct((4 * MODES, channels), f32),
            slots,
            resident((40, channels), f32),
            resident((40, channels), f32),
        ],
        scratch_shapes=[
            pltpu.VMEM((3, tokens + 8, LANES), f32),
            pltpu.VMEM((blocks, LANES, LANES), f32),
            pltpu.VMEM((TILE_GROUPS, LANES, 2 * LANES), bf16),
        ]
        + table_scratch,
        compiler_params=room(14),
        name="state_part",
    )(*far(features, short_taps, cotangent, rates, gains))

    gots = []
    for key in range(1, ctx_count):
        sent = jnp.where((ctx_index ^ key) < ctx_index, early, later)
        gots.append(swapped(sent.astype(bf16), "ctx", key).astype(f32))

    inner, grad, diag = pl.pallas_call(
        inside_kernel,
        grid=(tiles,),
        in_specs=[whole, whole, whole, table_spec, table_spec],
        out_specs=[whole, whole, slot_spec],
        out_shape=[wide_turned, wide_turned, slots],
        scratch_shapes=[
            pltpu.VMEM((TILE_GROUPS, 2 * LANES, LANES), bf16),
            pltpu.VMEM((LANES, LANES), f32),
            pltpu.VMEM((8 * TILE_GROUPS, LANES), f32),
        ]
        + table_scratch,
        compiler_params=room(14),
        cost_estimate=pl.CostEstimate(
            flops=2 * groups * rows * LANES * LANES * 7, bytes_accessed=14 * 2**20, transcendentals=0
        ),
        name="inside_part",
    )(*near(z, eh, el), *far(rates, gains))

    bound, local = pl.pallas_call(
        functools.partial(join_kernel, tokens),
        in_specs=[me_spec] + [whole] * (7 + len(gots)),
        out_specs=[whole, whole],
        out_shape=[
            jax.ShapeDtypeStruct((64, channels), f32),
            jax.ShapeDtypeStruct((2 * MODES, groups), f32),
        ],
        scratch_shapes=[pltpu.VMEM((ctx_count, 16, channels), f32)],
        compiler_params=room(14),
        name="join_part",
    )(me, states, later, diag, cross, short_taps, rates, gains, *gots)

    def outputs(first, count, *written):
        columns = lambda j: (0, j + first)
        layers = lambda j: (0, 0, j + first)
        mine = [pl.BlockSpec((tokens, LANES), columns), pl.BlockSpec((3, tokens, LANES), layers)]
        return pl.pallas_call(
            functools.partial(output_kernel, first),
            grid=(count,),
            in_specs=[
                pl.BlockSpec((3, 16, LANES), layers),
                pl.BlockSpec((3, 16, LANES), lambda j: (0, tokens // 16 - 1, j + first)),
                pl.BlockSpec((3, 3, LANES), layers),
                pl.BlockSpec((tokens, LANES), columns),
                table_spec,
                table_spec,
                whole,
                whole,
                whole,
                whole,
                pl.BlockSpec((64, LANES), columns),
            ]
            + [pl.BlockSpec(memory_space=pl.ANY)] * len(written),
            out_specs=mine,
            out_shape=[
                jax.ShapeDtypeStruct((tokens, channels), bf16),
                jax.ShapeDtypeStruct((3, tokens, channels), bf16),
            ],
            scratch_shapes=[
                pltpu.VMEM((3, 16, LANES), f32),
                pltpu.VMEM((3, tokens + 8, LANES), f32),
                pltpu.VMEM((blocks, LANES, LANES), f32),
                pltpu.VMEM((blocks, LANES, LANES), f32),
                pltpu.VMEM((TILE_GROUPS, rows, LANES), bf16),
            ]
            + table_scratch,
            compiler_params=room(14),
            input_output_aliases={11: 0, 12: 1} if written else {},
            cost_estimate=pl.CostEstimate(
                flops=2 * count * TILE_GROUPS * rows * LANES * LANES * 8,
                bytes_accessed=count * 4 * 2**20,
                transcendentals=0,
            ),
            name="output_part",
        )(
            *far(features, features, short_taps, cotangent, rates, gains),
            *near(inner, grad, carry, short),
            bound,
            *written,
        )

    half = tiles // 2
    terms = [local] + [swapped(local, "ctx", key) for key in range(1, ctx_count)]
    written = outputs(0, half)
    terms, written = lax.optimization_barrier((terms, written))
    summed, squares = pl.pallas_call(
        sum_kernel,
        in_specs=[whole] * len(terms),
        out_specs=[whole, whole],
        out_shape=[
            jax.ShapeDtypeStruct((2 * MODES, groups), f32),
            jax.ShapeDtypeStruct((1, groups), f32),
        ],
        compiler_params=room(14),
        name="sum_part",
    )(*terms)
    fsdp_count = lax.axis_size("fsdp")
    step = 1
    while step * 4 < fsdp_count:
        squares = squares + swapped(squares, "fsdp", step)
        step *= 2
    squares, written = lax.optimization_barrier((squares, written))
    parts = [squares] + [swapped(squares, "fsdp", key) for key in range(step, fsdp_count, step)]
    mixer, feature_grads = outputs(half, tiles - half, *written)
    while len(parts) > 1:
        parts = [parts[i] + parts[i + 1] for i in range(0, len(parts), 2)]
    entry_count = 2 * groups * MODES * fsdp_count
    clipped = summed * jnp.minimum(1.0, lax.rsqrt(parts[0] / entry_count + 1e-06))
    return (mixer, feature_grads, clipped[:MODES].T, clipped[MODES:].T)


def solution(mesh):
    return jax.shard_map(
        per_device,
        mesh=mesh,
        in_specs=(
            P(None, "ctx", "fsdp"),
            P(None, None, "fsdp"),
            P("fsdp", None),
            P("fsdp", None),
            P("ctx", "fsdp"),
        ),
        out_specs=(P("ctx", "fsdp"), P(None, "ctx", "fsdp"), P("fsdp", None), P("fsdp", None)),
        check_vma=False,
    )
```

```python
import functools

import jax
import jax.numpy as jnp
from jax import lax
from jax.experimental import pallas as pl
from jax.experimental.pallas import tpu as pltpu
from jax.sharding import PartitionSpec as P

LANES = 128
MODES = 16
MEMBERS = 16
TILE_GROUPS = LANES // MEMBERS
ROWS = LANES
f32 = jnp.float32
bf16 = jnp.bfloat16
STATE_PER = 2
OUTPUT_PER = 2
STATE_ROOM = 18
OUTPUT_ROOM = 18


def split(value):
    high = value.astype(bf16)
    return high, (value - high.astype(f32)).astype(bf16)


def dot_nt(left, right):
    return lax.dot_general(left, right, (((1,), (1,)), ((), ())), preferred_element_type=f32)


def dot_tn(left, right):
    return lax.dot_general(left, right, (((0,), (0,)), ((), ())), preferred_element_type=f32)


def dot_nn(left, right):
    return lax.dot_general(left, right, (((1,), (0,)), ((), ())), preferred_element_type=f32)


def iota(axis, shape):
    return lax.broadcasted_iota(jnp.int32, shape, axis)


def widen(feat_ref, wide, tokens):
    for i in range(3):
        wide[i, 0:8, :] = jnp.zeros((8, LANES), f32)
        wide[i, 8 : 8 + tokens, :] = feat_ref[i].astype(f32)


def short_block(wide, taps_ref, i, start, count):
    return (
        taps_ref[i, 0:1, :] * wide[i, start + 8 : start + 8 + count, :]
        + taps_ref[i, 1:2, :] * wide[i, start + 7 : start + 7 + count, :]
        + taps_ref[i, 2:3, :] * wide[i, start + 6 : start + 6 + count, :]
    )


def sheared(row8, period):
    which = iota(0, row8.shape) % period
    for bit in (1, 2, 4):
        row8 = jnp.where((which & bit) != 0, pltpu.roll(row8, LANES - bit, 1), row8)
    return row8


def circulant(row):
    return pltpu.roll(jnp.broadcast_to(row, (LANES, LANES)), 0, 1, stride=1, stride_axis=0)


def of_tile(whole, tile):
    return whole.at[pl.ds(tile * TILE_GROUPS, TILE_GROUPS)]


def staggered(parts):
    phase = [0] * len(parts)
    open_parts = [True] * len(parts)
    while any(open_parts):
        for u, part in enumerate(parts):
            if not open_parts[u] or (u and open_parts[u - 1] and phase[u] >= phase[u - 1]):
                continue
            got = next(part, None)
            if got is None:
                open_parts[u] = False
            else:
                phase[u] = got


def table_rows(source_ref, rows_ref):
    tall = jnp.concatenate([source_ref[...]] * (LANES // MODES), axis=0)
    missing = LANES - tall.shape[1]
    if missing:
        tall = jnp.concatenate([tall, jnp.zeros((LANES, missing), f32)], axis=1)
    rows_ref[...] = jnp.transpose(tall)


def fill_tables(rate_ref, gain_ref, rate_rows, gain_rows):
    @pl.when(pl.program_id(0) == 0)
    def _():
        table_rows(rate_ref, rate_rows)
        table_rows(gain_ref, gain_rows)


def parameters(tile, rate_rows, gain_rows):
    at = pl.ds(pl.multiple_of(tile * TILE_GROUPS, TILE_GROUPS), TILE_GROUPS)
    rates = rate_rows[at, :]
    return rates, gain_rows[at, :] * jnp.sqrt(2.0 * rates)


def per_mode(rows):
    own = iota(0, (TILE_GROUPS, LANES)) == iota(1, (TILE_GROUPS, LANES)) // MODES
    flat = jnp.sum(jnp.where(own, rows, 0.0), axis=0, keepdims=True)
    return jnp.transpose(jnp.broadcast_to(flat, (LANES, LANES)))


def per_member(rows):
    return jnp.concatenate(
        [jnp.broadcast_to(rows[g : g + 1], (MEMBERS, LANES)) for g in range(TILE_GROUPS)], axis=0
    )


def state_kernel(
    feat_ref, taps_ref, cot_ref, rate_ref, gain_ref,
    z_whole, eh_whole, el_whole, carry_whole, short_whole, state_ref, cross_ref,
    later_ref, earlier_ref,
    wide, own_all, table_all, rate_rows, gain_rows,
):
    fill_tables(rate_ref, gain_ref, rate_rows, gain_rows)
    count = cot_ref.shape[1] // LANES
    parts = []
    for u in range(count):
        tile = pl.program_id(0) * count + u
        lanes = slice(u * LANES, (u + 1) * LANES)
        parts.append(
            state_tile(
                tile, feat_ref.at[:, :, lanes], taps_ref.at[:, :, lanes], cot_ref.at[:, lanes],
                of_tile(z_whole, tile), of_tile(eh_whole, tile), of_tile(el_whole, tile),
                carry_whole.at[tile], short_whole.at[tile], state_ref.at[:, lanes],
                cross_ref.at[u * TILE_GROUPS : (u + 1) * TILE_GROUPS], later_ref, earlier_ref,
                wide.at[u], own_all.at[u], table_all.at[u], rate_rows, gain_rows,
            )
        )
    staggered(parts)


def state_tile(
    tile, feat_ref, taps_ref, cot_ref,
    z_ref, eh_ref, el_ref, carry_ref, short_ref, state_ref, cross_ref, later_ref, earlier_ref,
    wide, own_all, table_all, rate_rows, gain_rows,
):
    tokens = feat_ref.shape[1]
    blocks = tokens // LANES
    rate_tile, _ = parameters(tile, rate_rows, gain_rows)
    rates = per_mode(rate_tile)
    lag = iota(1, (LANES, LANES)).astype(f32)
    lane_at = iota(1, (LANES, LANES))
    lane_row = iota(1, (1, LANES))

    back = jnp.exp(-rates * (LANES - 1.0 - lag))
    after = jnp.exp(-rates * (lag + 1.0))
    s_parts = split(back)
    l_parts = split((LANES - 1.0 - lag) * back)
    m_parts = split(after)
    n_parts = split((lag + 1.0) * after)
    for g in range(TILE_GROUPS):
        of = slice(g * MODES, (g + 1) * MODES)
        for part in range(2):
            s_of, l_of = s_parts[part][of], l_parts[part][of]
            m_of, n_of = m_parts[part][of], n_parts[part][of]
            table_all[g, :, part * LANES : (part + 1) * LANES] = jnp.concatenate(
                [s_of, s_of, s_of, l_of, m_of, m_of, n_of, m_of], axis=0
            )

    widen(feat_ref, wide, tokens)
    for b in range(blocks):
        query = short_block(wide, taps_ref, 0, b * LANES, LANES)
        key = short_block(wide, taps_ref, 1, b * LANES, LANES)
        value = short_block(wide, taps_ref, 2, b * LANES, LANES)
        short_ref[0, b * LANES : (b + 1) * LANES, :] = query
        short_ref[1, b * LANES : (b + 1) * LANES, :] = key
        short_ref[2, b * LANES : (b + 1) * LANES, :] = value
        product = key * value
        adjoint = cot_ref[b * LANES : (b + 1) * LANES, :].astype(f32) * query
        if b == 0:
            inside = iota(0, (LANES, LANES)) >= 2
            product = jnp.where(inside, product, 0.0)
            adjoint = jnp.where(inside, adjoint, 0.0)
        z_t = jnp.transpose(product.astype(bf16))
        e_t = jnp.transpose(adjoint)
        e_high, e_low = split(e_t)
        at = slice(b * MEMBERS, (b + 1) * MEMBERS)
        for g in range(TILE_GROUPS):
            of = slice(g * MEMBERS, (g + 1) * MEMBERS)
            z_ref[g, at, :] = z_t[of]
            eh_ref[g, at, :] = e_high[of]
            el_ref[g, at, :] = e_low[of]
        yield 1

    for g in range(TILE_GROUPS):
        of = slice(g * MEMBERS, (g + 1) * MEMBERS)
        z, eh, el = z_ref[g], eh_ref[g], el_ref[g]
        left = jnp.concatenate(
            [
                jnp.concatenate([z, z], axis=1),
                jnp.concatenate([eh, eh], axis=1),
                jnp.concatenate([el, jnp.zeros_like(el)], axis=1),
            ],
            axis=0,
        )
        got = dot_nt(left, table_all[g])
        rows = z.shape[0]
        from_e = got[rows : 2 * rows] + got[2 * rows :]
        for b in range(blocks):
            at = slice(b * MEMBERS, (b + 1) * MEMBERS)
            opposite = slice((blocks - 1 - b) * MEMBERS, (blocks - b) * MEMBERS)
            own_all[b, of, :] = jnp.where(
                iota(1, (MEMBERS, LANES)) < 64, got[at], from_e[opposite]
            )
        yield 2

    span = per_member(jnp.exp(rate_tile * (-float(LANES))))
    in_lag = jnp.where(
        ((lane_row >= 48) & (lane_row < 64)) | ((lane_row >= 96) & (lane_row < 112)),
        float(LANES),
        0.0,
    )
    now = jnp.zeros((LANES, LANES), f32)
    lagged = jnp.zeros((LANES, LANES), f32)
    cross = jnp.zeros((LANES, LANES), f32)
    for b in range(blocks):
        own = own_all[b]
        cross = cross + now * pltpu.roll(own_all[blocks - 1 - b], 4 * MODES, 1)
        carry_ref[b] = now
        now = span * (now + lagged) + own
        if b < blocks - 1:
            lagged = span * lagged + in_lag * pltpu.roll(own, MODES, 1)
        yield 3
    cross_ref[...] = jnp.sum(cross.reshape(TILE_GROUPS, MEMBERS, LANES), axis=1)
    turned = jnp.transpose(now)
    state_ref[0:16] = turned[0:16]
    state_ref[16:32] = turned[48:64]
    state_ref[32:48] = turned[64:80]
    state_ref[48:64] = turned[96:112]

    half = later_ref.shape[1] // 2
    here = pl.ds(pl.multiple_of(tile * LANES, LANES), LANES)
    edges = jnp.concatenate(
        [wide[i, 8:10, :] for i in range(3)]
        + [cot_ref[0:2, :].astype(f32)]
        + [wide[i, 6 + tokens : 8 + tokens, :] for i in range(3)]
        + [jnp.zeros((2, LANES), f32)],
        axis=0,
    )
    for out_ref, main in ((later_ref, turned[0:16]), (earlier_ref, turned[64:80])):
        out_ref[0:16, here] = main
        out_ref[24:40, here] = edges

    def place(out_ref, lag_rows, start):
        for part in range(2):
            at = pl.ds(pl.multiple_of(start + part * half, LANES), LANES)
            out_ref[16:24, at] = lag_rows[8 * part : 8 * part + 8]

    @pl.when(tile * LANES < half)
    def _():
        place(later_ref, turned[48:64], tile * LANES)

    @pl.when(tile * LANES >= half)
    def _():
        place(earlier_ref, turned[96:112], tile * LANES - half)


def inside_kernel(
    z_whole, eh_whole, el_whole, rate_ref, gain_ref,
    inner_whole, grad_whole, diag_ref,
    toep_all, power_all, fold_all, rate_rows, gain_rows,
):
    tile = pl.program_id(0)
    z_ref, eh_ref, el_ref = [of_tile(ref, tile) for ref in (z_whole, eh_whole, el_whole)]
    inner_ref, grad_ref = of_tile(inner_whole, tile), of_tile(grad_whole, tile)
    fill_tables(rate_ref, gain_ref, rate_rows, gain_rows)
    rate_tile, coef_tile = parameters(tile, rate_rows, gain_rows)
    rates, coefs = per_mode(rate_tile), per_mode(coef_tile)
    lag = iota(1, (LANES, LANES)).astype(f32)
    row_at = iota(0, (LANES, LANES))
    lane_at = iota(1, (LANES, LANES))
    power = jnp.exp(-rates * lag)
    power_all[...] = power
    taps = jnp.sum((coefs * power).reshape(TILE_GROUPS, MODES, LANES), axis=1)
    for g in range(TILE_GROUPS):
        z_back = jnp.transpose(z_ref[g])
        gram = dot_nn(
            jnp.concatenate([z_back, z_back], axis=1),
            jnp.concatenate([eh_ref[g], el_ref[g]], axis=0),
        )
        gram = jnp.where(lane_at >= row_at, gram, 0.0)
        folded = [gram[0:8]] + [
            pltpu.roll(gram[8 * r : 8 * r + 8], LANES - 8 * r, 1) for r in range(1, LANES // 8)
        ]
        while len(folded) > 1:
            folded = [folded[i] + folded[i + 1] for i in range(0, len(folded), 2)]
        fold_all[8 * g : 8 * g + 8, :] = folded[0]
    for g in range(TILE_GROUPS):
        high, low = split(jnp.where(lane_at >= row_at, circulant(taps[g : g + 1]), 0.0))
        toep_all[g, 0:LANES, :] = high
        toep_all[g, LANES:, :] = low
    for g in range(TILE_GROUPS):
        z, eh, el = z_ref[g], eh_ref[g], el_ref[g]
        high = toep_all[g, 0:LANES, :]
        inner_ref[g] = dot_nn(jnp.concatenate([z, z], axis=1), toep_all[g])
        grad_ref[g] = dot_nt(
            jnp.concatenate([eh, el, eh], axis=1),
            jnp.concatenate([high, high, toep_all[g, LANES:, :]], axis=1),
        )
    corr = jnp.sum(sheared(fold_all[...], 8).reshape(TILE_GROUPS, 8, LANES), axis=1)
    weighted = power_all[...] * per_member(corr)
    first_col = jnp.sum(weighted, axis=1, keepdims=True)
    lag_col = jnp.sum(lag * weighted, axis=1, keepdims=True)
    mode_at = row_at % MODES
    placed = jnp.where(lane_at == mode_at, first_col, 0.0) + jnp.where(
        lane_at == mode_at + 32, lag_col, 0.0
    )
    diag_ref[...] = jnp.sum(placed.reshape(TILE_GROUPS, MODES, LANES), axis=1)


def exact_dot(left, right, dims):
    return lax.dot_general(
        left, right, (dims, ((), ())), precision=lax.Precision.HIGHEST, preferred_element_type=f32
    )


def join_kernel(
    tokens, me_ref, state_ref, own_ref, diag_ref, cross_ref, taps_ref, rate_ref, gain_ref, *refs
):
    gots, (bound_ref, local_ref, edges_all) = refs[:-3], refs[-3:]
    me = me_ref[0]
    channels = state_ref.shape[1]
    groups = rate_ref.shape[1]
    half = channels // 2
    chosen = (iota(0, (groups, channels)) == iota(1, (groups, channels)) // MEMBERS).astype(f32)
    rates = rate_ref[...]
    rate_cols = exact_dot(rates, chosen, ((1,), (0,)))
    edges_all[me] = own_ref[24:40]
    for key, got in enumerate(gots, 1):
        edges_all[me ^ key] = got[24:40]

    def tail_of(device):
        return jnp.where(device > 0, edges_all[jnp.maximum(device - 1, 0)][8:14], 0.0)

    def first_tokens(device):
        head, tail = edges_all[device], tail_of(device)
        shorts = []
        for i in range(3):
            tap = [taps_ref[i, j : j + 1, :] for j in range(3)]
            now, last = head[2 * i : 2 * i + 2], tail[2 * i : 2 * i + 2]
            shorts.append(
                (
                    tap[0] * now[0:1] + tap[1] * last[1:2] + tap[2] * last[0:1],
                    tap[0] * now[1:2] + tap[1] * now[0:1] + tap[2] * last[1:2],
                )
            )
        z = [(shorts[1][t] * shorts[2][t]).astype(bf16).astype(f32) for t in range(2)]
        e = [head[6 + t : 7 + t] * shorts[0][t] for t in range(2)]
        return z, e

    decay = jnp.exp(-rate_cols)
    decay_2 = decay * decay
    grow = jnp.exp(rate_cols)
    to_end = [jnp.exp(-rate_cols * float(tokens - 1)), jnp.exp(-rate_cols * float(tokens - 2))]
    from_start = [decay, decay_2]
    zero = jnp.zeros((MODES, channels), f32)
    zero_half = jnp.zeros((MODES, half), f32)
    s_prev, e_next = zero, zero
    s_lag, e_lag = zero_half, zero_half
    ahead = jnp.zeros((8, channels), f32)
    for key, got in enumerate(gots, 1):
        other = me ^ key
        earlier = other < me
        z, e = first_tokens(other)
        add = [
            jnp.where(earlier, to_end[t] * z[t], from_start[t] * e[t]) for t in range(2)
        ]
        steps = [
            jnp.where(earlier, tokens - 1 - t, t + 1).astype(f32) for t in range(2)
        ]
        added = steps[0] * add[0] + steps[1] * add[1]
        away = ((jnp.abs(me - other) - 1) * tokens).astype(f32)
        weight = jnp.exp(-rate_cols * away)
        part = weight * (got[0:16] + add[0] + add[1])

        def halved(value):
            return jnp.where(earlier, value[:, :half], value[:, half:])

        lagged = jnp.concatenate([got[16:24, :half], got[16:24, half:]], axis=0) + halved(added)
        lag_part = halved(weight) * lagged + away * halved(part)
        s_prev = s_prev + jnp.where(earlier, part, 0.0)
        s_lag = s_lag + jnp.where(earlier, lag_part, 0.0)
        e_next = e_next + jnp.where(earlier, 0.0, part)
        e_lag = e_lag + jnp.where(earlier, 0.0, lag_part)
        ahead = ahead + jnp.where(other == me + 1, got[24:32], 0.0)
    z, e = first_tokens(me)
    ends, lagged, moment_0, moment_1 = [state_ref[16 * i : 16 * i + 16] for i in range(4)]
    at_end = [to_end[t] * z[t] for t in range(2)]
    at_start = [from_start[t] * e[t] for t in range(2)]
    own_s = ends + at_end[0] + at_end[1]
    own_l = lagged + float(tokens - 1) * at_end[0] + float(tokens - 2) * at_end[1]
    own_m = moment_0 + at_start[0] + at_start[1]
    own_n = moment_1 + at_start[0] + 2.0 * at_start[1]
    early_0, early_1 = grow * z[0], grow * grow * z[1]
    early = early_0 + early_1
    bound_ref[0:16] = s_prev + early
    bound_ref[16:32] = e_next
    bound_ref[32:48] = own_s + jnp.exp(-rate_cols * float(tokens)) * s_prev
    bound_ref[48:56] = ahead
    bound_ref[56:62] = tail_of(me)
    bound_ref[62:64] = jnp.zeros((2, channels), f32)

    def joined(first_half, second_half):
        return jnp.concatenate([first_half[:, :half], second_half[:, half:]], axis=1)

    back = decay * e[1] * z[0]
    first_terms = (
        joined(own_m * s_prev, own_s * e_next) + moment_0 * early + e[0] * z[0] + e[1] * z[1] + back
    )
    lag_terms = (
        joined(own_n * s_prev, own_l * e_next)
        + jnp.concatenate([own_m[:, :half] * s_lag, own_s[:, half:] * e_lag], axis=1)
        + moment_1 * early
        - moment_0 * (early_0 + 2.0 * early_1)
        + back
    )
    sums = exact_dot(jnp.concatenate([first_terms, lag_terms], axis=0), chosen, ((1,), (1,)))
    own = jnp.transpose(cross_ref[...] + diag_ref[...])
    first = sums[0:16] + own[0:16]
    lag_sum = -(sums[16:32] + own[32:48] + own[48:64])
    root = jnp.sqrt(2.0 * rates)
    local_ref[0:16] = root * first
    local_ref[16:32] = gain_ref[...] * root * (0.5 * first + rates * lag_sum)


def output_kernel(
    first, start_ref, edge_ref, taps_ref, cot_ref, rate_ref, gain_ref,
    inner_whole, grad_whole, carry_whole, short_whole, bound_ref,
    *refs,
):
    mixer_ref, fgrad_ref, wide, adj, inner_t, grad_t, left_all, rate_rows, gain_rows = refs[-9:]
    fill_tables(rate_ref, gain_ref, rate_rows, gain_rows)
    count = cot_ref.shape[1] // LANES
    parts = []
    for u in range(count):
        tile = pl.program_id(0) * count + u + first
        lanes = slice(u * LANES, (u + 1) * LANES)
        parts.append(
            output_tile(
                tile, start_ref.at[:, :, lanes], edge_ref.at[:, :, lanes],
                taps_ref.at[:, :, lanes], cot_ref.at[:, lanes],
                of_tile(inner_whole, tile), of_tile(grad_whole, tile),
                carry_whole.at[tile], short_whole.at[tile], bound_ref.at[:, lanes],
                mixer_ref.at[:, lanes], fgrad_ref.at[:, :, lanes],
                wide.at[u], adj.at[u], inner_t.at[u], grad_t.at[u], left_all.at[u],
                rate_rows, gain_rows,
            )
        )
    staggered(parts)


def output_tile(
    tile, start_ref, edge_ref, taps_ref, cot_ref,
    inner_ref, grad_ref, carry_ref, short_ref, bound_ref,
    mixer_ref, fgrad_ref,
    wide, adj, inner_t, grad_t, left_all, rate_rows, gain_rows,
):
    tokens = cot_ref.shape[0]
    blocks = tokens // LANES
    rate_tile, coef_tile = parameters(tile, rate_rows, gain_rows)
    rates, coefs = per_mode(rate_tile), per_mode(coef_tile)
    lag = iota(1, (LANES, LANES)).astype(f32)
    lane_at = iota(1, (LANES, LANES))
    is_low = ((lane_at >= 16) & (lane_at < 32)) | ((lane_at >= 80) & (lane_at < 96))
    before = bound_ref[0:16]
    after = bound_ref[16:32]
    gap = jnp.zeros((MODES, LANES), f32)
    stacked = jnp.concatenate([before, before, before, gap, after, after, gap, after], axis=0)
    turned = jnp.transpose(stacked)
    none_16 = jnp.zeros((MODES, LANES), bf16)
    none_64 = jnp.zeros((4 * MODES, LANES), bf16)
    member_rates = per_member(rate_tile)
    span = jnp.exp(member_rates * (-float(LANES)))
    from_others = turned
    for b in range(blocks):
        value = carry_ref[b] + from_others
        from_others = from_others * span
        high = value.astype(bf16).astype(f32)
        mixed = jnp.where(is_low, value - high, value).astype(bf16)
        for g in range(TILE_GROUPS):
            left_all[g, b * MEMBERS : (b + 1) * MEMBERS, :] = mixed[
                g * MEMBERS : (g + 1) * MEMBERS
            ]
    cz_parts = split(coefs * jnp.exp(-rates * (lag + 1.0)))
    ce_parts = split(coefs * jnp.exp(-rates * (LANES - 1.0 - lag)))
    for g in range(TILE_GROUPS):
        of = slice(g * MODES, (g + 1) * MODES)
        cz_high, cz_low = cz_parts[0][of], cz_parts[1][of]
        ce_high, ce_low = ce_parts[0][of], ce_parts[1][of]
        right = jnp.concatenate(
            [
                jnp.concatenate([cz_high, cz_high, cz_low, none_16, none_64], axis=0),
                jnp.concatenate([none_64, ce_high, ce_high, none_16, ce_low], axis=0),
            ],
            axis=1,
        )
        carried = dot_nn(left_all[g], right)
        for b in range(blocks):
            at = slice(b * MEMBERS, (b + 1) * MEMBERS)
            opposite = slice((blocks - 1 - b) * MEMBERS, (blocks - b) * MEMBERS)
            inner_t[b, of, :] = inner_ref[g, at, :] + carried[at, :LANES]
            grad_t[b, of, :] = grad_ref[g, at, :] + carried[opposite, LANES:]
        yield 1
    rates = jnp.transpose(member_rates)[0:MODES]
    coefs = jnp.transpose(per_member(coef_tile))[0:MODES]
    decay = jnp.exp(-rates)
    grow = jnp.exp(rates)
    state = bound_ref[32:48]
    sum_0 = jnp.sum(coefs, axis=0, keepdims=True)
    sum_1 = jnp.sum(coefs * decay, axis=0, keepdims=True)
    for i in range(3):
        wide[i, 0:8, :] = jnp.zeros((8, LANES), f32)
        wide[i, 6:8, :] = bound_ref[56 + 2 * i : 58 + 2 * i]
        wide[i, 8:16, :] = start_ref[i, 0:8, :].astype(f32)
    begun = [short_block(wide, taps_ref, i, 0, 8) for i in range(3)]
    z_own = (begun[1] * begun[2]).astype(bf16).astype(f32)
    e_own = cot_ref[0:8, :].astype(f32) * begun[0]
    sum_up = jnp.sum(coefs * grow, axis=0, keepdims=True)
    which = iota(0, (8, LANES))
    inner_fix = jnp.where(which == 0, -sum_up * z_own[1:2], 0.0)
    grad_fix = jnp.where(
        which == 0,
        sum_0 * e_own[0:1] + sum_1 * e_own[1:2],
        jnp.where(which == 1, sum_0 * e_own[1:2], 0.0),
    )
    for b in range(blocks):
        at = slice(b * LANES, (b + 1) * LANES)
        inner = jnp.transpose(inner_t[b])
        query = short_ref[0, at, :]
        if b == 0:
            query = jnp.concatenate([begun[0], short_ref[0, 8:LANES, :]], axis=0)
            inner = jnp.concatenate([inner[0:8] + inner_fix, inner[8:]], axis=0)
        mixer_ref[at, :] = (query * inner).astype(bf16)
        adj[0, at, :] = cot_ref[at, :].astype(f32) * inner
        yield 2
    for b in range(blocks):
        at = slice(b * LANES, (b + 1) * LANES)
        grad = jnp.transpose(grad_t[b])
        key, value = short_ref[1, at, :], short_ref[2, at, :]
        if b == 0:
            key = jnp.concatenate([begun[1], short_ref[1, 8:LANES, :]], axis=0)
            value = jnp.concatenate([begun[2], short_ref[2, 8:LANES, :]], axis=0)
            grad = jnp.concatenate([grad[0:8] + grad_fix, grad[8:]], axis=0)
        adj[1, at, :] = grad * value
        adj[2, at, :] = grad * key
        yield 2
    for i in range(3):
        wide[i, 0:8, :] = edge_ref[i, 8:16, :].astype(f32)
        wide[i, 8:16, :] = jnp.zeros((8, LANES), f32)
        wide[i, 8:10, :] = bound_ref[48 + 2 * i : 50 + 2 * i]
    query, key, value = [short_block(wide, taps_ref, i, 0, 8) for i in range(3)]
    z = (key * value).astype(bf16).astype(f32)
    upstream = jnp.concatenate([bound_ref[54:56], jnp.zeros((6, LANES), f32)], axis=0)
    e = upstream * query
    inner_0 = jnp.sum(coefs * decay * state, axis=0, keepdims=True) + sum_0 * z[0:1]
    inner_1 = (
        jnp.sum(coefs * decay * decay * state, axis=0, keepdims=True)
        + sum_1 * z[0:1]
        + sum_0 * z[1:2]
    )
    grad_0 = jnp.sum(coefs * grow * after, axis=0, keepdims=True)
    grad_1 = jnp.sum(coefs * grow * (grow * after - e[0:1]), axis=0, keepdims=True)
    inner_8 = jnp.where(which == 0, inner_0, jnp.where(which == 1, inner_1, 0.0))
    grad_8 = jnp.where(which == 0, grad_0, jnp.where(which == 1, grad_1, 0.0))
    adj[0, tokens : tokens + 8, :] = upstream * inner_8
    adj[1, tokens : tokens + 8, :] = grad_8 * value
    adj[2, tokens : tokens + 8, :] = grad_8 * key
    for i in range(3):
        for b in range(blocks):
            start = b * LANES
            fgrad_ref[i, start : start + LANES, :] = (
                taps_ref[i, 0:1, :] * adj[i, start : start + LANES, :]
                + taps_ref[i, 1:2, :] * adj[i, start + 1 : start + 1 + LANES, :]
                + taps_ref[i, 2:3, :] * adj[i, start + 2 : start + 2 + LANES, :]
            ).astype(bf16)
            yield 3


def resident(shape, dtype):
    return pltpu.VMEM(shape, dtype)


def sum_kernel(*refs):
    *terms, summed_ref, square_ref = refs
    terms = [term[...] for term in terms]
    while len(terms) > 1:
        terms = [terms[i] + terms[i + 1] for i in range(0, len(terms), 2)]
    summed_ref[...] = terms[0]
    square_ref[...] = jnp.broadcast_to(
        jnp.sum(jnp.sum(terms[0] * terms[0], axis=0, keepdims=True), axis=1, keepdims=True),
        square_ref.shape,
    )


def far(*arrays):
    return [pltpu.with_memory_space_constraint(array, pltpu.HBM) for array in arrays]


def near(*arrays):
    return [pltpu.with_memory_space_constraint(array, pltpu.VMEM) for array in arrays]


def swapped(value, axis, key):
    count = lax.axis_size(axis)
    return lax.ppermute(value, axis, [(i, i ^ key) for i in range(count)])


def per_device(features, short_taps, decay_rates, mode_gains, cotangent):
    tokens = features.shape[1]
    channels = features.shape[2]
    groups = decay_rates.shape[0]
    tiles = channels // LANES
    blocks = tokens // LANES
    ctx_count = lax.axis_size("ctx")
    ctx_index = lax.axis_index("ctx")

    me = ctx_index.astype(jnp.int32).reshape(1)
    rates, gains = decay_rates.T, mode_gains.T

    whole = pl.BlockSpec(memory_space=pltpu.VMEM)
    per = STATE_PER if tiles % STATE_PER == 0 else 1
    feat_spec = pl.BlockSpec((3, tokens, per * LANES), lambda j: (0, 0, j))
    taps_spec = pl.BlockSpec((3, 3, per * LANES), lambda j: (0, 0, j))
    cot_spec = pl.BlockSpec((tokens, per * LANES), lambda j: (0, j))
    table_spec = pl.BlockSpec((MODES, groups), lambda j: (0, 0))
    slot_spec = pl.BlockSpec((TILE_GROUPS, LANES), lambda j: (j, 0))
    me_spec = pl.BlockSpec(memory_space=pltpu.SMEM)
    rows = blocks * MEMBERS
    turned = resident((groups, rows, LANES), bf16)
    wide_turned = resident((groups, rows, LANES), f32)
    slots = jax.ShapeDtypeStruct((groups, LANES), f32)
    table_scratch = [pltpu.VMEM((LANES, LANES), f32), pltpu.VMEM((LANES, LANES), f32)]

    def room(mebibytes):
        return pltpu.CompilerParams(vmem_limit_bytes=mebibytes * 2**20)

    z, eh, el, carry, short, states, cross, later, early = pl.pallas_call(
        state_kernel,
        grid=(tiles // per,),
        in_specs=[feat_spec, taps_spec, cot_spec, table_spec, table_spec],
        out_specs=[
            whole,
            whole,
            whole,
            whole,
            whole,
            pl.BlockSpec((4 * MODES, per * LANES), lambda j: (0, j)),
            pl.BlockSpec((per * TILE_GROUPS, LANES), lambda j: (j, 0)),
            whole,
            whole,
        ],
        out_shape=[
            turned,
            turned,
            turned,
            resident((tiles, blocks, LANES, LANES), f32),
            resident((tiles, 3, tokens, LANES), f32),
            jax.ShapeDtypeStruct((4 * MODES, channels), f32),
            slots,
            resident((40, channels), f32),
            resident((40, channels), f32),
        ],
        scratch_shapes=[
            pltpu.VMEM((per, 3, tokens + 8, LANES), f32),
            pltpu.VMEM((per, blocks, LANES, LANES), f32),
            pltpu.VMEM((per, TILE_GROUPS, LANES, 2 * LANES), bf16),
        ]
        + table_scratch,
        compiler_params=room(STATE_ROOM),
        name="state_part",
    )(*far(features, short_taps, cotangent, rates, gains))

    gots = []
    for key in range(1, ctx_count):
        sent = jnp.where((ctx_index ^ key) < ctx_index, early, later)
        gots.append(swapped(sent.astype(bf16), "ctx", key).astype(f32))

    inner, grad, diag = pl.pallas_call(
        inside_kernel,
        grid=(tiles,),
        in_specs=[whole, whole, whole, table_spec, table_spec],
        out_specs=[whole, whole, slot_spec],
        out_shape=[wide_turned, wide_turned, slots],
        scratch_shapes=[
            pltpu.VMEM((TILE_GROUPS, 2 * LANES, LANES), bf16),
            pltpu.VMEM((LANES, LANES), f32),
            pltpu.VMEM((8 * TILE_GROUPS, LANES), f32),
        ]
        + table_scratch,
        compiler_params=room(14),
        cost_estimate=pl.CostEstimate(
            flops=2 * groups * rows * LANES * LANES * 7, bytes_accessed=14 * 2**20, transcendentals=0
        ),
        name="inside_part",
    )(*near(z, eh, el), *far(rates, gains))

    bound, local = pl.pallas_call(
        functools.partial(join_kernel, tokens),
        in_specs=[me_spec] + [whole] * (7 + len(gots)),
        out_specs=[whole, whole],
        out_shape=[
            jax.ShapeDtypeStruct((64, channels), f32),
            jax.ShapeDtypeStruct((2 * MODES, groups), f32),
        ],
        scratch_shapes=[pltpu.VMEM((ctx_count, 16, channels), f32)],
        compiler_params=room(14),
        name="join_part",
    )(me, states, later, diag, cross, short_taps, rates, gains, *gots)

    def outputs(first, count, *written):
        per = OUTPUT_PER if count % OUTPUT_PER == 0 and first % OUTPUT_PER == 0 else 1
        wide_lanes = per * LANES
        columns = lambda j: (0, j + first // per)
        layers = lambda j: (0, 0, j + first // per)
        mine = [pl.BlockSpec((tokens, wide_lanes), columns), pl.BlockSpec((3, tokens, wide_lanes), layers)]
        return pl.pallas_call(
            functools.partial(output_kernel, first),
            grid=(count // per,),
            in_specs=[
                pl.BlockSpec((3, 16, wide_lanes), layers),
                pl.BlockSpec((3, 16, wide_lanes), lambda j: (0, tokens // 16 - 1, j + first // per)),
                pl.BlockSpec((3, 3, wide_lanes), layers),
                pl.BlockSpec((tokens, wide_lanes), columns),
                table_spec,
                table_spec,
                whole,
                whole,
                whole,
                whole,
                pl.BlockSpec((64, wide_lanes), columns),
            ]
            + [pl.BlockSpec(memory_space=pl.ANY)] * len(written),
            out_specs=mine,
            out_shape=[
                jax.ShapeDtypeStruct((tokens, channels), bf16),
                jax.ShapeDtypeStruct((3, tokens, channels), bf16),
            ],
            scratch_shapes=[
                pltpu.VMEM((per, 3, 16, LANES), f32),
                pltpu.VMEM((per, 3, tokens + 8, LANES), f32),
                pltpu.VMEM((per, blocks, LANES, LANES), f32),
                pltpu.VMEM((per, blocks, LANES, LANES), f32),
                pltpu.VMEM((per, TILE_GROUPS, rows, LANES), bf16),
            ]
            + table_scratch,
            compiler_params=room(OUTPUT_ROOM),
            input_output_aliases={11: 0, 12: 1} if written else {},
            cost_estimate=pl.CostEstimate(
                flops=2 * count * TILE_GROUPS * rows * LANES * LANES * 8,
                bytes_accessed=count * 4 * 2**20,
                transcendentals=0,
            ),
            name="output_part",
        )(
            *far(features, features, short_taps, cotangent, rates, gains),
            *near(inner, grad, carry, short),
            bound,
            *written,
        )

    half = tiles // 2
    terms = [local] + [swapped(local, "ctx", key) for key in range(1, ctx_count)]
    written = outputs(0, half)
    terms, written = lax.optimization_barrier((terms, written))
    summed, squares = pl.pallas_call(
        sum_kernel,
        in_specs=[whole] * len(terms),
        out_specs=[whole, whole],
        out_shape=[
            jax.ShapeDtypeStruct((2 * MODES, groups), f32),
            jax.ShapeDtypeStruct((1, groups), f32),
        ],
        compiler_params=room(14),
        name="sum_part",
    )(*terms)
    fsdp_count = lax.axis_size("fsdp")
    step = 1
    while step * 4 < fsdp_count:
        squares = squares + swapped(squares, "fsdp", step)
        step *= 2
    squares, written = lax.optimization_barrier((squares, written))
    parts = [squares] + [swapped(squares, "fsdp", key) for key in range(step, fsdp_count, step)]
    mixer, feature_grads = outputs(half, tiles - half, *written)
    while len(parts) > 1:
        parts = [parts[i] + parts[i + 1] for i in range(0, len(parts), 2)]
    entry_count = 2 * groups * MODES * fsdp_count
    clipped = summed * jnp.minimum(1.0, lax.rsqrt(parts[0] / entry_count + 1e-06))
    return (mixer, feature_grads, clipped[:MODES].T, clipped[MODES:].T)


def solution(mesh):
    return jax.shard_map(
        per_device,
        mesh=mesh,
        in_specs=(
            P(None, "ctx", "fsdp"),
            P(None, None, "fsdp"),
            P("fsdp", None),
            P("fsdp", None),
            P("ctx", "fsdp"),
        ),
        out_specs=(P("ctx", "fsdp"), P(None, "ctx", "fsdp"), P("fsdp", None), P("fsdp", None)),
        check_vma=False,
    )
```

```python
import functools

import jax
import jax.numpy as jnp
from jax import lax
from jax.experimental import pallas as pl
from jax.experimental.pallas import tpu as pltpu
from jax.sharding import PartitionSpec as P

LANES = 128
MODES = 16
MEMBERS = 16
TILE_GROUPS = LANES // MEMBERS
ROWS = LANES
f32 = jnp.float32
bf16 = jnp.bfloat16
STATE_PER = 2
OUTPUT_PER = 2
INSIDE_PER = 2
STATE_ROOM = 18
OUTPUT_ROOM = 18


def split(value):
    high = value.astype(bf16)
    return high, (value - high.astype(f32)).astype(bf16)


def dot_nt(left, right):
    return lax.dot_general(left, right, (((1,), (1,)), ((), ())), preferred_element_type=f32)


def dot_tn(left, right):
    return lax.dot_general(left, right, (((0,), (0,)), ((), ())), preferred_element_type=f32)


def dot_nn(left, right):
    return lax.dot_general(left, right, (((1,), (0,)), ((), ())), preferred_element_type=f32)


def iota(axis, shape):
    return lax.broadcasted_iota(jnp.int32, shape, axis)


def widen(feat_ref, wide, tokens):
    for i in range(3):
        wide[i, 0:8, :] = jnp.zeros((8, LANES), f32)
        wide[i, 8 : 8 + tokens, :] = feat_ref[i].astype(f32)


def short_block(wide, taps_ref, i, start, count):
    return (
        taps_ref[i, 0:1, :] * wide[i, start + 8 : start + 8 + count, :]
        + taps_ref[i, 1:2, :] * wide[i, start + 7 : start + 7 + count, :]
        + taps_ref[i, 2:3, :] * wide[i, start + 6 : start + 6 + count, :]
    )


def sheared(row8, period):
    which = iota(0, row8.shape) % period
    for bit in (1, 2, 4):
        row8 = jnp.where((which & bit) != 0, pltpu.roll(row8, LANES - bit, 1), row8)
    return row8


def circulant(row):
    return pltpu.roll(jnp.broadcast_to(row, (LANES, LANES)), 0, 1, stride=1, stride_axis=0)


def of_tile(whole, tile):
    return whole.at[pl.ds(tile * TILE_GROUPS, TILE_GROUPS)]


def staggered(parts):
    phase = [0] * len(parts)
    open_parts = [True] * len(parts)
    while any(open_parts):
        for u, part in enumerate(parts):
            if not open_parts[u] or (u and open_parts[u - 1] and phase[u] >= phase[u - 1]):
                continue
            got = next(part, None)
            if got is None:
                open_parts[u] = False
            else:
                phase[u] = got


def table_rows(source_ref, rows_ref):
    tall = jnp.concatenate([source_ref[...]] * (LANES // MODES), axis=0)
    missing = LANES - tall.shape[1]
    if missing:
        tall = jnp.concatenate([tall, jnp.zeros((LANES, missing), f32)], axis=1)
    rows_ref[...] = jnp.transpose(tall)


def fill_tables(rate_ref, gain_ref, rate_rows, gain_rows):
    @pl.when(pl.program_id(0) == 0)
    def _():
        table_rows(rate_ref, rate_rows)
        table_rows(gain_ref, gain_rows)


def parameters(tile, rate_rows, gain_rows):
    at = pl.ds(pl.multiple_of(tile * TILE_GROUPS, TILE_GROUPS), TILE_GROUPS)
    rates = rate_rows[at, :]
    return rates, gain_rows[at, :] * jnp.sqrt(2.0 * rates)


def per_mode(rows):
    own = iota(0, (TILE_GROUPS, LANES)) == iota(1, (TILE_GROUPS, LANES)) // MODES
    flat = jnp.sum(jnp.where(own, rows, 0.0), axis=0, keepdims=True)
    return jnp.transpose(jnp.broadcast_to(flat, (LANES, LANES)))


def per_member(rows):
    return jnp.concatenate(
        [jnp.broadcast_to(rows[g : g + 1], (MEMBERS, LANES)) for g in range(TILE_GROUPS)], axis=0
    )


def state_kernel(
    feat_ref, taps_ref, cot_ref, rate_ref, gain_ref,
    z_whole, eh_whole, el_whole, carry_whole, short_whole, state_ref, cross_ref,
    later_ref, earlier_ref,
    wide, own_all, table_all, rate_rows, gain_rows,
):
    fill_tables(rate_ref, gain_ref, rate_rows, gain_rows)
    count = cot_ref.shape[1] // LANES
    parts = []
    for u in range(count):
        tile = pl.program_id(0) * count + u
        lanes = slice(u * LANES, (u + 1) * LANES)
        parts.append(
            state_tile(
                tile, feat_ref.at[:, :, lanes], taps_ref.at[:, :, lanes], cot_ref.at[:, lanes],
                of_tile(z_whole, tile), of_tile(eh_whole, tile), of_tile(el_whole, tile),
                carry_whole.at[tile], short_whole.at[tile], state_ref.at[:, lanes],
                cross_ref.at[u * TILE_GROUPS : (u + 1) * TILE_GROUPS], later_ref, earlier_ref,
                wide.at[u], own_all.at[u], table_all.at[u], rate_rows, gain_rows,
            )
        )
    staggered(parts)


def state_tile(
    tile, feat_ref, taps_ref, cot_ref,
    z_ref, eh_ref, el_ref, carry_ref, short_ref, state_ref, cross_ref, later_ref, earlier_ref,
    wide, own_all, table_all, rate_rows, gain_rows,
):
    tokens = feat_ref.shape[1]
    blocks = tokens // LANES
    rate_tile, _ = parameters(tile, rate_rows, gain_rows)
    rates = per_mode(rate_tile)
    lag = iota(1, (LANES, LANES)).astype(f32)
    lane_at = iota(1, (LANES, LANES))
    lane_row = iota(1, (1, LANES))

    back = jnp.exp(-rates * (LANES - 1.0 - lag))
    after = jnp.exp(-rates * (lag + 1.0))
    s_parts = split(back)
    l_parts = split((LANES - 1.0 - lag) * back)
    m_parts = split(after)
    n_parts = split((lag + 1.0) * after)
    for g in range(TILE_GROUPS):
        of = slice(g * MODES, (g + 1) * MODES)
        for part in range(2):
            s_of, l_of = s_parts[part][of], l_parts[part][of]
            m_of, n_of = m_parts[part][of], n_parts[part][of]
            table_all[g, :, part * LANES : (part + 1) * LANES] = jnp.concatenate(
                [s_of, s_of, s_of, l_of, m_of, m_of, n_of, m_of], axis=0
            )

    widen(feat_ref, wide, tokens)
    for b in range(blocks):
        query = short_block(wide, taps_ref, 0, b * LANES, LANES)
        key = short_block(wide, taps_ref, 1, b * LANES, LANES)
        value = short_block(wide, taps_ref, 2, b * LANES, LANES)
        short_ref[0, b * LANES : (b + 1) * LANES, :] = query
        short_ref[1, b * LANES : (b + 1) * LANES, :] = key
        short_ref[2, b * LANES : (b + 1) * LANES, :] = value
        product = key * value
        adjoint = cot_ref[b * LANES : (b + 1) * LANES, :].astype(f32) * query
        if b == 0:
            inside = iota(0, (LANES, LANES)) >= 2
            product = jnp.where(inside, product, 0.0)
            adjoint = jnp.where(inside, adjoint, 0.0)
        z_t = jnp.transpose(product.astype(bf16))
        e_t = jnp.transpose(adjoint)
        e_high, e_low = split(e_t)
        at = slice(b * MEMBERS, (b + 1) * MEMBERS)
        for g in range(TILE_GROUPS):
            of = slice(g * MEMBERS, (g + 1) * MEMBERS)
            z_ref[g, at, :] = z_t[of]
            eh_ref[g, at, :] = e_high[of]
            el_ref[g, at, :] = e_low[of]
        yield 1

    for g in range(TILE_GROUPS):
        of = slice(g * MEMBERS, (g + 1) * MEMBERS)
        z, eh, el = z_ref[g], eh_ref[g], el_ref[g]
        left = jnp.concatenate(
            [
                jnp.concatenate([z, z], axis=1),
                jnp.concatenate([eh, eh], axis=1),
                jnp.concatenate([el, jnp.zeros_like(el)], axis=1),
            ],
            axis=0,
        )
        got = dot_nt(left, table_all[g])
        rows = z.shape[0]
        from_e = got[rows : 2 * rows] + got[2 * rows :]
        for b in range(blocks):
            at = slice(b * MEMBERS, (b + 1) * MEMBERS)
            opposite = slice((blocks - 1 - b) * MEMBERS, (blocks - b) * MEMBERS)
            own_all[b, of, :] = jnp.where(
                iota(1, (MEMBERS, LANES)) < 64, got[at], from_e[opposite]
            )
        yield 2

    span = per_member(jnp.exp(rate_tile * (-float(LANES))))
    in_lag = jnp.where(
        ((lane_row >= 48) & (lane_row < 64)) | ((lane_row >= 96) & (lane_row < 112)),
        float(LANES),
        0.0,
    )
    now = jnp.zeros((LANES, LANES), f32)
    lagged = jnp.zeros((LANES, LANES), f32)
    cross = jnp.zeros((LANES, LANES), f32)
    for b in range(blocks):
        own = own_all[b]
        cross = cross + now * pltpu.roll(own_all[blocks - 1 - b], 4 * MODES, 1)
        carry_ref[b] = now
        now = span * (now + lagged) + own
        if b < blocks - 1:
            lagged = span * lagged + in_lag * pltpu.roll(own, MODES, 1)
        yield 3
    cross_ref[...] = jnp.sum(cross.reshape(TILE_GROUPS, MEMBERS, LANES), axis=1)
    turned = jnp.transpose(now)
    state_ref[0:16] = turned[0:16]
    state_ref[16:32] = turned[48:64]
    state_ref[32:48] = turned[64:80]
    state_ref[48:64] = turned[96:112]

    half = later_ref.shape[1] // 2
    here = pl.ds(pl.multiple_of(tile * LANES, LANES), LANES)
    edges = jnp.concatenate(
        [wide[i, 8:10, :] for i in range(3)]
        + [cot_ref[0:2, :].astype(f32)]
        + [wide[i, 6 + tokens : 8 + tokens, :] for i in range(3)]
        + [jnp.zeros((2, LANES), f32)],
        axis=0,
    )
    for out_ref, main in ((later_ref, turned[0:16]), (earlier_ref, turned[64:80])):
        out_ref[0:16, here] = main
        out_ref[24:40, here] = edges

    def place(out_ref, lag_rows, start):
        for part in range(2):
            at = pl.ds(pl.multiple_of(start + part * half, LANES), LANES)
            out_ref[16:24, at] = lag_rows[8 * part : 8 * part + 8]

    @pl.when(tile * LANES < half)
    def _():
        place(later_ref, turned[48:64], tile * LANES)

    @pl.when(tile * LANES >= half)
    def _():
        place(earlier_ref, turned[96:112], tile * LANES - half)


def inside_kernel(
    z_whole, eh_whole, el_whole, rate_ref, gain_ref,
    inner_whole, grad_whole, diag_ref,
    toep_all, power_all, fold_all, rate_rows, gain_rows,
):
    fill_tables(rate_ref, gain_ref, rate_rows, gain_rows)
    count = diag_ref.shape[0] // TILE_GROUPS
    parts = []
    for u in range(count):
        tile = pl.program_id(0) * count + u
        parts.append(
            inside_tile(
                tile, of_tile(z_whole, tile), of_tile(eh_whole, tile), of_tile(el_whole, tile),
                of_tile(inner_whole, tile), of_tile(grad_whole, tile),
                diag_ref.at[u * TILE_GROUPS : (u + 1) * TILE_GROUPS],
                toep_all.at[u], power_all.at[u], fold_all.at[u], rate_rows, gain_rows,
            )
        )
    staggered(parts)


def inside_tile(
    tile, z_ref, eh_ref, el_ref, inner_ref, grad_ref, diag_ref,
    toep_all, power_all, fold_all, rate_rows, gain_rows,
):
    rate_tile, coef_tile = parameters(tile, rate_rows, gain_rows)
    rates, coefs = per_mode(rate_tile), per_mode(coef_tile)
    lag = iota(1, (LANES, LANES)).astype(f32)
    row_at = iota(0, (LANES, LANES))
    lane_at = iota(1, (LANES, LANES))
    power = jnp.exp(-rates * lag)
    power_all[...] = power
    taps = jnp.sum((coefs * power).reshape(TILE_GROUPS, MODES, LANES), axis=1)
    for g in range(TILE_GROUPS):
        z_back = jnp.transpose(z_ref[g])
        gram = dot_nn(
            jnp.concatenate([z_back, z_back], axis=1),
            jnp.concatenate([eh_ref[g], el_ref[g]], axis=0),
        )
        gram = jnp.where(lane_at >= row_at, gram, 0.0)
        folded = [gram[0:8]] + [
            pltpu.roll(gram[8 * r : 8 * r + 8], LANES - 8 * r, 1) for r in range(1, LANES // 8)
        ]
        while len(folded) > 1:
            folded = [folded[i] + folded[i + 1] for i in range(0, len(folded), 2)]
        fold_all[8 * g : 8 * g + 8, :] = folded[0]
        yield 1
    for g in range(TILE_GROUPS):
        high, low = split(jnp.where(lane_at >= row_at, circulant(taps[g : g + 1]), 0.0))
        toep_all[g, 0:LANES, :] = high
        toep_all[g, LANES:, :] = low
        yield 2
    for g in range(TILE_GROUPS):
        z, eh, el = z_ref[g], eh_ref[g], el_ref[g]
        high = toep_all[g, 0:LANES, :]
        inner_ref[g] = dot_nn(jnp.concatenate([z, z], axis=1), toep_all[g])
        grad_ref[g] = dot_nt(
            jnp.concatenate([eh, el, eh], axis=1),
            jnp.concatenate([high, high, toep_all[g, LANES:, :]], axis=1),
        )
        yield 3
    corr = jnp.sum(sheared(fold_all[...], 8).reshape(TILE_GROUPS, 8, LANES), axis=1)
    weighted = power_all[...] * per_member(corr)
    first_col = jnp.sum(weighted, axis=1, keepdims=True)
    lag_col = jnp.sum(lag * weighted, axis=1, keepdims=True)
    mode_at = row_at % MODES
    placed = jnp.where(lane_at == mode_at, first_col, 0.0) + jnp.where(
        lane_at == mode_at + 32, lag_col, 0.0
    )
    diag_ref[...] = jnp.sum(placed.reshape(TILE_GROUPS, MODES, LANES), axis=1)


def exact_dot(left, right, dims):
    return lax.dot_general(
        left, right, (dims, ((), ())), precision=lax.Precision.HIGHEST, preferred_element_type=f32
    )


def join_kernel(
    tokens, me_ref, state_ref, own_ref, diag_ref, cross_ref, taps_ref, rate_ref, gain_ref, *refs
):
    gots, (bound_ref, local_ref, edges_all) = refs[:-3], refs[-3:]
    me = me_ref[0]
    channels = state_ref.shape[1]
    groups = rate_ref.shape[1]
    half = channels // 2
    chosen = (iota(0, (groups, channels)) == iota(1, (groups, channels)) // MEMBERS).astype(f32)
    rates = rate_ref[...]
    rate_cols = exact_dot(rates, chosen, ((1,), (0,)))
    edges_all[me] = own_ref[24:40]
    for key, got in enumerate(gots, 1):
        edges_all[me ^ key] = got[24:40]

    def tail_of(device):
        return jnp.where(device > 0, edges_all[jnp.maximum(device - 1, 0)][8:14], 0.0)

    def first_tokens(device):
        head, tail = edges_all[device], tail_of(device)
        shorts = []
        for i in range(3):
            tap = [taps_ref[i, j : j + 1, :] for j in range(3)]
            now, last = head[2 * i : 2 * i + 2], tail[2 * i : 2 * i + 2]
            shorts.append(
                (
                    tap[0] * now[0:1] + tap[1] * last[1:2] + tap[2] * last[0:1],
                    tap[0] * now[1:2] + tap[1] * now[0:1] + tap[2] * last[1:2],
                )
            )
        z = [(shorts[1][t] * shorts[2][t]).astype(bf16).astype(f32) for t in range(2)]
        e = [head[6 + t : 7 + t] * shorts[0][t] for t in range(2)]
        return z, e

    decay = jnp.exp(-rate_cols)
    decay_2 = decay * decay
    grow = jnp.exp(rate_cols)
    to_end = [jnp.exp(-rate_cols * float(tokens - 1)), jnp.exp(-rate_cols * float(tokens - 2))]
    from_start = [decay, decay_2]
    zero = jnp.zeros((MODES, channels), f32)
    zero_half = jnp.zeros((MODES, half), f32)
    s_prev, e_next = zero, zero
    s_lag, e_lag = zero_half, zero_half
    ahead = jnp.zeros((8, channels), f32)
    for key, got in enumerate(gots, 1):
        other = me ^ key
        earlier = other < me
        z, e = first_tokens(other)
        add = [
            jnp.where(earlier, to_end[t] * z[t], from_start[t] * e[t]) for t in range(2)
        ]
        steps = [
            jnp.where(earlier, tokens - 1 - t, t + 1).astype(f32) for t in range(2)
        ]
        added = steps[0] * add[0] + steps[1] * add[1]
        away = ((jnp.abs(me - other) - 1) * tokens).astype(f32)
        weight = jnp.exp(-rate_cols * away)
        part = weight * (got[0:16] + add[0] + add[1])

        def halved(value):
            return jnp.where(earlier, value[:, :half], value[:, half:])

        lagged = jnp.concatenate([got[16:24, :half], got[16:24, half:]], axis=0) + halved(added)
        lag_part = halved(weight) * lagged + away * halved(part)
        s_prev = s_prev + jnp.where(earlier, part, 0.0)
        s_lag = s_lag + jnp.where(earlier, lag_part, 0.0)
        e_next = e_next + jnp.where(earlier, 0.0, part)
        e_lag = e_lag + jnp.where(earlier, 0.0, lag_part)
        ahead = ahead + jnp.where(other == me + 1, got[24:32], 0.0)
    z, e = first_tokens(me)
    ends, lagged, moment_0, moment_1 = [state_ref[16 * i : 16 * i + 16] for i in range(4)]
    at_end = [to_end[t] * z[t] for t in range(2)]
    at_start = [from_start[t] * e[t] for t in range(2)]
    own_s = ends + at_end[0] + at_end[1]
    own_l = lagged + float(tokens - 1) * at_end[0] + float(tokens - 2) * at_end[1]
    own_m = moment_0 + at_start[0] + at_start[1]
    own_n = moment_1 + at_start[0] + 2.0 * at_start[1]
    early_0, early_1 = grow * z[0], grow * grow * z[1]
    early = early_0 + early_1
    bound_ref[0:16] = s_prev + early
    bound_ref[16:32] = e_next
    bound_ref[32:48] = own_s + jnp.exp(-rate_cols * float(tokens)) * s_prev
    bound_ref[48:56] = ahead
    bound_ref[56:62] = tail_of(me)
    bound_ref[62:64] = jnp.zeros((2, channels), f32)

    def joined(first_half, second_half):
        return jnp.concatenate([first_half[:, :half], second_half[:, half:]], axis=1)

    back = decay * e[1] * z[0]
    first_terms = (
        joined(own_m * s_prev, own_s * e_next) + moment_0 * early + e[0] * z[0] + e[1] * z[1] + back
    )
    lag_terms = (
        joined(own_n * s_prev, own_l * e_next)
        + jnp.concatenate([own_m[:, :half] * s_lag, own_s[:, half:] * e_lag], axis=1)
        + moment_1 * early
        - moment_0 * (early_0 + 2.0 * early_1)
        + back
    )
    sums = exact_dot(jnp.concatenate([first_terms, lag_terms], axis=0), chosen, ((1,), (1,)))
    own = jnp.transpose(cross_ref[...] + diag_ref[...])
    first = sums[0:16] + own[0:16]
    lag_sum = -(sums[16:32] + own[32:48] + own[48:64])
    root = jnp.sqrt(2.0 * rates)
    local_ref[0:16] = root * first
    local_ref[16:32] = gain_ref[...] * root * (0.5 * first + rates * lag_sum)


def output_kernel(
    first, start_ref, edge_ref, taps_ref, cot_ref, rate_ref, gain_ref,
    inner_whole, grad_whole, carry_whole, short_whole, bound_ref,
    *refs,
):
    mixer_ref, fgrad_ref, wide, adj, inner_t, grad_t, left_all, rate_rows, gain_rows = refs[-9:]
    fill_tables(rate_ref, gain_ref, rate_rows, gain_rows)
    count = cot_ref.shape[1] // LANES
    parts = []
    for u in range(count):
        tile = pl.program_id(0) * count + u + first
        lanes = slice(u * LANES, (u + 1) * LANES)
        parts.append(
            output_tile(
                tile, start_ref.at[:, :, lanes], edge_ref.at[:, :, lanes],
                taps_ref.at[:, :, lanes], cot_ref.at[:, lanes],
                of_tile(inner_whole, tile), of_tile(grad_whole, tile),
                carry_whole.at[tile], short_whole.at[tile], bound_ref.at[:, lanes],
                mixer_ref.at[:, lanes], fgrad_ref.at[:, :, lanes],
                wide.at[u], adj.at[u], inner_t.at[u], grad_t.at[u], left_all.at[u],
                rate_rows, gain_rows,
            )
        )
    staggered(parts)


def output_tile(
    tile, start_ref, edge_ref, taps_ref, cot_ref,
    inner_ref, grad_ref, carry_ref, short_ref, bound_ref,
    mixer_ref, fgrad_ref,
    wide, adj, inner_t, grad_t, left_all, rate_rows, gain_rows,
):
    tokens = cot_ref.shape[0]
    blocks = tokens // LANES
    rate_tile, coef_tile = parameters(tile, rate_rows, gain_rows)
    rates, coefs = per_mode(rate_tile), per_mode(coef_tile)
    lag = iota(1, (LANES, LANES)).astype(f32)
    lane_at = iota(1, (LANES, LANES))
    is_low = ((lane_at >= 16) & (lane_at < 32)) | ((lane_at >= 80) & (lane_at < 96))
    before = bound_ref[0:16]
    after = bound_ref[16:32]
    gap = jnp.zeros((MODES, LANES), f32)
    stacked = jnp.concatenate([before, before, before, gap, after, after, gap, after], axis=0)
    turned = jnp.transpose(stacked)
    none_16 = jnp.zeros((MODES, LANES), bf16)
    none_64 = jnp.zeros((4 * MODES, LANES), bf16)
    member_rates = per_member(rate_tile)
    span = jnp.exp(member_rates * (-float(LANES)))
    from_others = turned
    for b in range(blocks):
        value = carry_ref[b] + from_others
        from_others = from_others * span
        high = value.astype(bf16).astype(f32)
        mixed = jnp.where(is_low, value - high, value).astype(bf16)
        for g in range(TILE_GROUPS):
            left_all[g, b * MEMBERS : (b + 1) * MEMBERS, :] = mixed[
                g * MEMBERS : (g + 1) * MEMBERS
            ]
    cz_parts = split(coefs * jnp.exp(-rates * (lag + 1.0)))
    ce_parts = split(coefs * jnp.exp(-rates * (LANES - 1.0 - lag)))
    for g in range(TILE_GROUPS):
        of = slice(g * MODES, (g + 1) * MODES)
        cz_high, cz_low = cz_parts[0][of], cz_parts[1][of]
        ce_high, ce_low = ce_parts[0][of], ce_parts[1][of]
        right = jnp.concatenate(
            [
                jnp.concatenate([cz_high, cz_high, cz_low, none_16, none_64], axis=0),
                jnp.concatenate([none_64, ce_high, ce_high, none_16, ce_low], axis=0),
            ],
            axis=1,
        )
        carried = dot_nn(left_all[g], right)
        for b in range(blocks):
            at = slice(b * MEMBERS, (b + 1) * MEMBERS)
            opposite = slice((blocks - 1 - b) * MEMBERS, (blocks - b) * MEMBERS)
            inner_t[b, of, :] = inner_ref[g, at, :] + carried[at, :LANES]
            grad_t[b, of, :] = grad_ref[g, at, :] + carried[opposite, LANES:]
        yield 1
    rates = jnp.transpose(member_rates)[0:MODES]
    coefs = jnp.transpose(per_member(coef_tile))[0:MODES]
    decay = jnp.exp(-rates)
    grow = jnp.exp(rates)
    state = bound_ref[32:48]
    sum_0 = jnp.sum(coefs, axis=0, keepdims=True)
    sum_1 = jnp.sum(coefs * decay, axis=0, keepdims=True)
    for i in range(3):
        wide[i, 0:8, :] = jnp.zeros((8, LANES), f32)
        wide[i, 6:8, :] = bound_ref[56 + 2 * i : 58 + 2 * i]
        wide[i, 8:16, :] = start_ref[i, 0:8, :].astype(f32)
    begun = [short_block(wide, taps_ref, i, 0, 8) for i in range(3)]
    z_own = (begun[1] * begun[2]).astype(bf16).astype(f32)
    e_own = cot_ref[0:8, :].astype(f32) * begun[0]
    sum_up = jnp.sum(coefs * grow, axis=0, keepdims=True)
    which = iota(0, (8, LANES))
    inner_fix = jnp.where(which == 0, -sum_up * z_own[1:2], 0.0)
    grad_fix = jnp.where(
        which == 0,
        sum_0 * e_own[0:1] + sum_1 * e_own[1:2],
        jnp.where(which == 1, sum_0 * e_own[1:2], 0.0),
    )
    for b in range(blocks):
        at = slice(b * LANES, (b + 1) * LANES)
        inner = jnp.transpose(inner_t[b])
        query = short_ref[0, at, :]
        if b == 0:
            query = jnp.concatenate([begun[0], short_ref[0, 8:LANES, :]], axis=0)
            inner = jnp.concatenate([inner[0:8] + inner_fix, inner[8:]], axis=0)
        mixer_ref[at, :] = (query * inner).astype(bf16)
        adj[0, at, :] = cot_ref[at, :].astype(f32) * inner
        yield 2
    for b in range(blocks):
        at = slice(b * LANES, (b + 1) * LANES)
        grad = jnp.transpose(grad_t[b])
        key, value = short_ref[1, at, :], short_ref[2, at, :]
        if b == 0:
            key = jnp.concatenate([begun[1], short_ref[1, 8:LANES, :]], axis=0)
            value = jnp.concatenate([begun[2], short_ref[2, 8:LANES, :]], axis=0)
            grad = jnp.concatenate([grad[0:8] + grad_fix, grad[8:]], axis=0)
        adj[1, at, :] = grad * value
        adj[2, at, :] = grad * key
        yield 2
    for i in range(3):
        wide[i, 0:8, :] = edge_ref[i, 8:16, :].astype(f32)
        wide[i, 8:16, :] = jnp.zeros((8, LANES), f32)
        wide[i, 8:10, :] = bound_ref[48 + 2 * i : 50 + 2 * i]
    query, key, value = [short_block(wide, taps_ref, i, 0, 8) for i in range(3)]
    z = (key * value).astype(bf16).astype(f32)
    upstream = jnp.concatenate([bound_ref[54:56], jnp.zeros((6, LANES), f32)], axis=0)
    e = upstream * query
    inner_0 = jnp.sum(coefs * decay * state, axis=0, keepdims=True) + sum_0 * z[0:1]
    inner_1 = (
        jnp.sum(coefs * decay * decay * state, axis=0, keepdims=True)
        + sum_1 * z[0:1]
        + sum_0 * z[1:2]
    )
    grad_0 = jnp.sum(coefs * grow * after, axis=0, keepdims=True)
    grad_1 = jnp.sum(coefs * grow * (grow * after - e[0:1]), axis=0, keepdims=True)
    inner_8 = jnp.where(which == 0, inner_0, jnp.where(which == 1, inner_1, 0.0))
    grad_8 = jnp.where(which == 0, grad_0, jnp.where(which == 1, grad_1, 0.0))
    adj[0, tokens : tokens + 8, :] = upstream * inner_8
    adj[1, tokens : tokens + 8, :] = grad_8 * value
    adj[2, tokens : tokens + 8, :] = grad_8 * key
    for i in range(3):
        for b in range(blocks):
            start = b * LANES
            fgrad_ref[i, start : start + LANES, :] = (
                taps_ref[i, 0:1, :] * adj[i, start : start + LANES, :]
                + taps_ref[i, 1:2, :] * adj[i, start + 1 : start + 1 + LANES, :]
                + taps_ref[i, 2:3, :] * adj[i, start + 2 : start + 2 + LANES, :]
            ).astype(bf16)
            yield 3


def resident(shape, dtype):
    return pltpu.VMEM(shape, dtype)


def sum_kernel(*refs):
    *terms, summed_ref, square_ref = refs
    terms = [term[...] for term in terms]
    while len(terms) > 1:
        terms = [terms[i] + terms[i + 1] for i in range(0, len(terms), 2)]
    summed_ref[...] = terms[0]
    square_ref[...] = jnp.broadcast_to(
        jnp.sum(jnp.sum(terms[0] * terms[0], axis=0, keepdims=True), axis=1, keepdims=True),
        square_ref.shape,
    )


def far(*arrays):
    return [pltpu.with_memory_space_constraint(array, pltpu.HBM) for array in arrays]


def near(*arrays):
    return [pltpu.with_memory_space_constraint(array, pltpu.VMEM) for array in arrays]


def swapped(value, axis, key):
    count = lax.axis_size(axis)
    return lax.ppermute(value, axis, [(i, i ^ key) for i in range(count)])


def per_device(features, short_taps, decay_rates, mode_gains, cotangent):
    tokens = features.shape[1]
    channels = features.shape[2]
    groups = decay_rates.shape[0]
    tiles = channels // LANES
    blocks = tokens // LANES
    ctx_count = lax.axis_size("ctx")
    ctx_index = lax.axis_index("ctx")

    me = ctx_index.astype(jnp.int32).reshape(1)
    rates, gains = decay_rates.T, mode_gains.T

    whole = pl.BlockSpec(memory_space=pltpu.VMEM)
    per = STATE_PER if tiles % STATE_PER == 0 else 1
    feat_spec = pl.BlockSpec((3, tokens, per * LANES), lambda j: (0, 0, j))
    taps_spec = pl.BlockSpec((3, 3, per * LANES), lambda j: (0, 0, j))
    cot_spec = pl.BlockSpec((tokens, per * LANES), lambda j: (0, j))
    table_spec = pl.BlockSpec((MODES, groups), lambda j: (0, 0))
    me_spec = pl.BlockSpec(memory_space=pltpu.SMEM)
    rows = blocks * MEMBERS
    turned = resident((groups, rows, LANES), bf16)
    wide_turned = resident((groups, rows, LANES), f32)
    slots = jax.ShapeDtypeStruct((groups, LANES), f32)
    table_scratch = [pltpu.VMEM((LANES, LANES), f32), pltpu.VMEM((LANES, LANES), f32)]

    def room(mebibytes):
        return pltpu.CompilerParams(vmem_limit_bytes=mebibytes * 2**20)

    z, eh, el, carry, short, states, cross, later, early = pl.pallas_call(
        state_kernel,
        grid=(tiles // per,),
        in_specs=[feat_spec, taps_spec, cot_spec, table_spec, table_spec],
        out_specs=[
            whole,
            whole,
            whole,
            whole,
            whole,
            pl.BlockSpec((4 * MODES, per * LANES), lambda j: (0, j)),
            pl.BlockSpec((per * TILE_GROUPS, LANES), lambda j: (j, 0)),
            whole,
            whole,
        ],
        out_shape=[
            turned,
            turned,
            turned,
            resident((tiles, blocks, LANES, LANES), f32),
            resident((tiles, 3, tokens, LANES), f32),
            jax.ShapeDtypeStruct((4 * MODES, channels), f32),
            slots,
            resident((40, channels), f32),
            resident((40, channels), f32),
        ],
        scratch_shapes=[
            pltpu.VMEM((per, 3, tokens + 8, LANES), f32),
            pltpu.VMEM((per, blocks, LANES, LANES), f32),
            pltpu.VMEM((per, TILE_GROUPS, LANES, 2 * LANES), bf16),
        ]
        + table_scratch,
        compiler_params=room(STATE_ROOM),
        name="state_part",
    )(*far(features, short_taps, cotangent, rates, gains))

    gots = []
    for key in range(1, ctx_count):
        sent = jnp.where((ctx_index ^ key) < ctx_index, early, later)
        gots.append(swapped(sent.astype(bf16), "ctx", key).astype(f32))

    inside_per = INSIDE_PER if tiles % INSIDE_PER == 0 else 1
    inner, grad, diag = pl.pallas_call(
        inside_kernel,
        grid=(tiles // inside_per,),
        in_specs=[whole, whole, whole, table_spec, table_spec],
        out_specs=[
            whole,
            whole,
            pl.BlockSpec((inside_per * TILE_GROUPS, LANES), lambda j: (j, 0)),
        ],
        out_shape=[wide_turned, wide_turned, slots],
        scratch_shapes=[
            pltpu.VMEM((inside_per, TILE_GROUPS, 2 * LANES, LANES), bf16),
            pltpu.VMEM((inside_per, LANES, LANES), f32),
            pltpu.VMEM((inside_per, 8 * TILE_GROUPS, LANES), f32),
        ]
        + table_scratch,
        compiler_params=room(14),
        cost_estimate=pl.CostEstimate(
            flops=2 * groups * rows * LANES * LANES * 7, bytes_accessed=14 * 2**20, transcendentals=0
        ),
        name="inside_part",
    )(*near(z, eh, el), *far(rates, gains))

    bound, local = pl.pallas_call(
        functools.partial(join_kernel, tokens),
        in_specs=[me_spec] + [whole] * (7 + len(gots)),
        out_specs=[whole, whole],
        out_shape=[
            jax.ShapeDtypeStruct((64, channels), f32),
            jax.ShapeDtypeStruct((2 * MODES, groups), f32),
        ],
        scratch_shapes=[pltpu.VMEM((ctx_count, 16, channels), f32)],
        compiler_params=room(14),
        name="join_part",
    )(me, states, later, diag, cross, short_taps, rates, gains, *gots)

    def outputs(first, count, *written):
        per = OUTPUT_PER if count % OUTPUT_PER == 0 and first % OUTPUT_PER == 0 else 1
        wide_lanes = per * LANES
        columns = lambda j: (0, j + first // per)
        layers = lambda j: (0, 0, j + first // per)
        mine = [pl.BlockSpec((tokens, wide_lanes), columns), pl.BlockSpec((3, tokens, wide_lanes), layers)]
        return pl.pallas_call(
            functools.partial(output_kernel, first),
            grid=(count // per,),
            in_specs=[
                pl.BlockSpec((3, 16, wide_lanes), layers),
                pl.BlockSpec((3, 16, wide_lanes), lambda j: (0, tokens // 16 - 1, j + first // per)),
                pl.BlockSpec((3, 3, wide_lanes), layers),
                pl.BlockSpec((tokens, wide_lanes), columns),
                table_spec,
                table_spec,
                whole,
                whole,
                whole,
                whole,
                pl.BlockSpec((64, wide_lanes), columns),
            ]
            + [pl.BlockSpec(memory_space=pl.ANY)] * len(written),
            out_specs=mine,
            out_shape=[
                jax.ShapeDtypeStruct((tokens, channels), bf16),
                jax.ShapeDtypeStruct((3, tokens, channels), bf16),
            ],
            scratch_shapes=[
                pltpu.VMEM((per, 3, 16, LANES), f32),
                pltpu.VMEM((per, 3, tokens + 8, LANES), f32),
                pltpu.VMEM((per, blocks, LANES, LANES), f32),
                pltpu.VMEM((per, blocks, LANES, LANES), f32),
                pltpu.VMEM((per, TILE_GROUPS, rows, LANES), bf16),
            ]
            + table_scratch,
            compiler_params=room(OUTPUT_ROOM),
            input_output_aliases={11: 0, 12: 1} if written else {},
            cost_estimate=pl.CostEstimate(
                flops=2 * count * TILE_GROUPS * rows * LANES * LANES * 8,
                bytes_accessed=count * 4 * 2**20,
                transcendentals=0,
            ),
            name="output_part",
        )(
            *far(features, features, short_taps, cotangent, rates, gains),
            *near(inner, grad, carry, short),
            bound,
            *written,
        )

    half = tiles // 2
    terms = [local] + [swapped(local, "ctx", key) for key in range(1, ctx_count)]
    written = outputs(0, half)
    terms, written = lax.optimization_barrier((terms, written))
    summed, squares = pl.pallas_call(
        sum_kernel,
        in_specs=[whole] * len(terms),
        out_specs=[whole, whole],
        out_shape=[
            jax.ShapeDtypeStruct((2 * MODES, groups), f32),
            jax.ShapeDtypeStruct((1, groups), f32),
        ],
        compiler_params=room(14),
        name="sum_part",
    )(*terms)
    fsdp_count = lax.axis_size("fsdp")
    step = 1
    while step * 4 < fsdp_count:
        squares = squares + swapped(squares, "fsdp", step)
        step *= 2
    squares, written = lax.optimization_barrier((squares, written))
    parts = [squares] + [swapped(squares, "fsdp", key) for key in range(step, fsdp_count, step)]
    mixer, feature_grads = outputs(half, tiles - half, *written)
    while len(parts) > 1:
        parts = [parts[i] + parts[i + 1] for i in range(0, len(parts), 2)]
    entry_count = 2 * groups * MODES * fsdp_count
    clipped = summed * jnp.minimum(1.0, lax.rsqrt(parts[0] / entry_count + 1e-06))
    return (mixer, feature_grads, clipped[:MODES].T, clipped[MODES:].T)


def solution(mesh):
    return jax.shard_map(
        per_device,
        mesh=mesh,
        in_specs=(
            P(None, "ctx", "fsdp"),
            P(None, None, "fsdp"),
            P("fsdp", None),
            P("fsdp", None),
            P("ctx", "fsdp"),
        ),
        out_specs=(P("ctx", "fsdp"), P(None, "ctx", "fsdp"), P("fsdp", None), P("fsdp", None)),
        check_vma=False,
    )
```

```python
import functools

import jax
import jax.numpy as jnp
from jax import lax
from jax.experimental import pallas as pl
from jax.experimental.pallas import tpu as pltpu
from jax.sharding import PartitionSpec as P

LANES = 128
MODES = 16
MEMBERS = 16
TILE_GROUPS = LANES // MEMBERS
ROWS = LANES
f32 = jnp.float32
bf16 = jnp.bfloat16
STATE_PER = 2
OUTPUT_PER = 2
INSIDE_PER = 2
STATE_ROOM = 18
OUTPUT_ROOM = 18


def split(value):
    high = value.astype(bf16)
    return high, (value - high.astype(f32)).astype(bf16)


def dot_nt(left, right):
    return lax.dot_general(left, right, (((1,), (1,)), ((), ())), preferred_element_type=f32)


def dot_tn(left, right):
    return lax.dot_general(left, right, (((0,), (0,)), ((), ())), preferred_element_type=f32)


def dot_nn(left, right):
    return lax.dot_general(left, right, (((1,), (0,)), ((), ())), preferred_element_type=f32)


def iota(axis, shape):
    return lax.broadcasted_iota(jnp.int32, shape, axis)


def widen(feat_ref, wide, tokens):
    for i in range(3):
        wide[i, 0:8, :] = jnp.zeros((8, LANES), f32)
        wide[i, 8 : 8 + tokens, :] = feat_ref[i].astype(f32)


def short_block(wide, taps_ref, i, start, count):
    return (
        taps_ref[i, 0:1, :] * wide[i, start + 8 : start + 8 + count, :]
        + taps_ref[i, 1:2, :] * wide[i, start + 7 : start + 7 + count, :]
        + taps_ref[i, 2:3, :] * wide[i, start + 6 : start + 6 + count, :]
    )


def sheared(row8, period):
    which = iota(0, row8.shape) % period
    for bit in (1, 2, 4):
        row8 = jnp.where((which & bit) != 0, pltpu.roll(row8, LANES - bit, 1), row8)
    return row8


def circulant(row):
    return pltpu.roll(jnp.broadcast_to(row, (LANES, LANES)), 0, 1, stride=1, stride_axis=0)


def of_tile(whole, tile):
    return whole.at[pl.ds(tile * TILE_GROUPS, TILE_GROUPS)]


def staggered(parts):
    phase = [0] * len(parts)
    open_parts = [True] * len(parts)
    while any(open_parts):
        for u, part in enumerate(parts):
            if not open_parts[u] or (u and open_parts[u - 1] and phase[u] >= phase[u - 1]):
                continue
            got = next(part, None)
            if got is None:
                open_parts[u] = False
            else:
                phase[u] = got


def table_rows(source_ref, rows_ref):
    tall = jnp.concatenate([source_ref[...]] * (LANES // MODES), axis=0)
    missing = LANES - tall.shape[1]
    if missing:
        tall = jnp.concatenate([tall, jnp.zeros((LANES, missing), f32)], axis=1)
    rows_ref[...] = jnp.transpose(tall)


def fill_tables(rate_ref, gain_ref, rate_rows, gain_rows):
    @pl.when(pl.program_id(0) == 0)
    def _():
        table_rows(rate_ref, rate_rows)
        table_rows(gain_ref, gain_rows)


def parameters(tile, rate_rows, gain_rows):
    at = pl.ds(pl.multiple_of(tile * TILE_GROUPS, TILE_GROUPS), TILE_GROUPS)
    rates = rate_rows[at, :]
    return rates, gain_rows[at, :] * jnp.sqrt(2.0 * rates)


def per_mode(rows):
    own = iota(0, (TILE_GROUPS, LANES)) == iota(1, (TILE_GROUPS, LANES)) // MODES
    flat = jnp.sum(jnp.where(own, rows, 0.0), axis=0, keepdims=True)
    return jnp.transpose(jnp.broadcast_to(flat, (LANES, LANES)))


def per_member(rows):
    return jnp.concatenate(
        [jnp.broadcast_to(rows[g : g + 1], (MEMBERS, LANES)) for g in range(TILE_GROUPS)], axis=0
    )


def state_kernel(
    feat_ref, taps_ref, cot_ref, rate_ref, gain_ref,
    z_whole, eh_whole, el_whole, carry_whole, short_whole, state_ref, cross_ref,
    later_ref, earlier_ref,
    wide, own_all, table_all, rate_rows, gain_rows,
):
    fill_tables(rate_ref, gain_ref, rate_rows, gain_rows)
    count = cot_ref.shape[1] // LANES
    parts = []
    for u in range(count):
        tile = pl.program_id(0) * count + u
        lanes = slice(u * LANES, (u + 1) * LANES)
        parts.append(
            state_tile(
                tile, feat_ref.at[:, :, lanes], taps_ref.at[:, :, lanes], cot_ref.at[:, lanes],
                of_tile(z_whole, tile), of_tile(eh_whole, tile), of_tile(el_whole, tile),
                carry_whole.at[tile], short_whole.at[tile], state_ref.at[:, lanes],
                cross_ref.at[u * TILE_GROUPS : (u + 1) * TILE_GROUPS], later_ref, earlier_ref,
                wide.at[u], own_all.at[u], table_all.at[u], rate_rows, gain_rows,
            )
        )
    staggered(parts)


def state_tile(
    tile, feat_ref, taps_ref, cot_ref,
    z_ref, eh_ref, el_ref, carry_ref, short_ref, state_ref, cross_ref, later_ref, earlier_ref,
    wide, own_all, table_all, rate_rows, gain_rows,
):
    tokens = feat_ref.shape[1]
    blocks = tokens // LANES
    rate_tile, _ = parameters(tile, rate_rows, gain_rows)
    rates = per_mode(rate_tile)
    lag = iota(1, (LANES, LANES)).astype(f32)
    lane_at = iota(1, (LANES, LANES))
    lane_row = iota(1, (1, LANES))

    back = jnp.exp(-rates * (LANES - 1.0 - lag))
    after = jnp.exp(-rates * (lag + 1.0))
    s_parts = split(back)
    l_parts = split((LANES - 1.0 - lag) * back)
    m_parts = split(after)
    n_parts = split((lag + 1.0) * after)
    for g in range(TILE_GROUPS):
        of = slice(g * MODES, (g + 1) * MODES)
        for part in range(2):
            s_of, l_of = s_parts[part][of], l_parts[part][of]
            m_of, n_of = m_parts[part][of], n_parts[part][of]
            table_all[g, :, part * LANES : (part + 1) * LANES] = jnp.concatenate(
                [s_of, s_of, s_of, l_of, m_of, m_of, n_of, m_of], axis=0
            )

    widen(feat_ref, wide, tokens)
    for b in range(blocks):
        query = short_block(wide, taps_ref, 0, b * LANES, LANES)
        key = short_block(wide, taps_ref, 1, b * LANES, LANES)
        value = short_block(wide, taps_ref, 2, b * LANES, LANES)
        short_ref[0, b * LANES : (b + 1) * LANES, :] = query
        short_ref[1, b * LANES : (b + 1) * LANES, :] = key
        short_ref[2, b * LANES : (b + 1) * LANES, :] = value
        product = key * value
        adjoint = cot_ref[b * LANES : (b + 1) * LANES, :].astype(f32) * query
        if b == 0:
            inside = iota(0, (LANES, LANES)) >= 2
            product = jnp.where(inside, product, 0.0)
            adjoint = jnp.where(inside, adjoint, 0.0)
        z_t = jnp.transpose(product.astype(bf16))
        e_t = jnp.transpose(adjoint)
        e_high, e_low = split(e_t)
        at = slice(b * MEMBERS, (b + 1) * MEMBERS)
        for g in range(TILE_GROUPS):
            of = slice(g * MEMBERS, (g + 1) * MEMBERS)
            z_ref[g, at, :] = z_t[of]
            eh_ref[g, at, :] = e_high[of]
            el_ref[g, at, :] = e_low[of]
        yield 1

    for g in range(TILE_GROUPS):
        of = slice(g * MEMBERS, (g + 1) * MEMBERS)
        z, eh, el = z_ref[g], eh_ref[g], el_ref[g]
        left = jnp.concatenate(
            [
                jnp.concatenate([z, z], axis=1),
                jnp.concatenate([eh, eh], axis=1),
                jnp.concatenate([el, jnp.zeros_like(el)], axis=1),
            ],
            axis=0,
        )
        got = dot_nt(left, table_all[g])
        rows = z.shape[0]
        from_e = got[rows : 2 * rows] + got[2 * rows :]
        for b in range(blocks):
            at = slice(b * MEMBERS, (b + 1) * MEMBERS)
            opposite = slice((blocks - 1 - b) * MEMBERS, (blocks - b) * MEMBERS)
            own_all[b, of, :] = jnp.where(
                iota(1, (MEMBERS, LANES)) < 64, got[at], from_e[opposite]
            )
        yield 2

    span = per_member(jnp.exp(rate_tile * (-float(LANES))))
    in_lag = jnp.where(
        ((lane_row >= 48) & (lane_row < 64)) | ((lane_row >= 96) & (lane_row < 112)),
        float(LANES),
        0.0,
    )
    now = jnp.zeros((LANES, LANES), f32)
    lagged = jnp.zeros((LANES, LANES), f32)
    cross = jnp.zeros((LANES, LANES), f32)
    for b in range(blocks):
        own = own_all[b]
        cross = cross + now * pltpu.roll(own_all[blocks - 1 - b], 4 * MODES, 1)
        carry_ref[b] = now
        now = span * (now + lagged) + own
        if b < blocks - 1:
            lagged = span * lagged + in_lag * pltpu.roll(own, MODES, 1)
        yield 3
    cross_ref[...] = jnp.sum(cross.reshape(TILE_GROUPS, MEMBERS, LANES), axis=1)
    turned = jnp.transpose(now)
    state_ref[0:16] = turned[0:16]
    state_ref[16:32] = turned[48:64]
    state_ref[32:48] = turned[64:80]
    state_ref[48:64] = turned[96:112]

    half = later_ref.shape[1] // 2
    here = pl.ds(pl.multiple_of(tile * LANES, LANES), LANES)
    edges = jnp.concatenate(
        [wide[i, 8:10, :] for i in range(3)]
        + [cot_ref[0:2, :].astype(f32)]
        + [wide[i, 6 + tokens : 8 + tokens, :] for i in range(3)]
        + [jnp.zeros((2, LANES), f32)],
        axis=0,
    )
    for out_ref, main in ((later_ref, turned[0:16]), (earlier_ref, turned[64:80])):
        out_ref[0:16, here] = main
        out_ref[24:40, here] = edges

    def place(out_ref, lag_rows, start):
        for part in range(2):
            at = pl.ds(pl.multiple_of(start + part * half, LANES), LANES)
            out_ref[16:24, at] = lag_rows[8 * part : 8 * part + 8]

    @pl.when(tile * LANES < half)
    def _():
        place(later_ref, turned[48:64], tile * LANES)

    @pl.when(tile * LANES >= half)
    def _():
        place(earlier_ref, turned[96:112], tile * LANES - half)


def inside_kernel(
    z_whole, eh_whole, el_whole, rate_ref, gain_ref,
    inner_whole, grad_whole, diag_ref,
    toep_all, power_all, fold_all, rate_rows, gain_rows,
):
    fill_tables(rate_ref, gain_ref, rate_rows, gain_rows)
    count = diag_ref.shape[0] // TILE_GROUPS
    parts = []
    for u in range(count):
        tile = pl.program_id(0) * count + u
        parts.append(
            inside_tile(
                tile, of_tile(z_whole, tile), of_tile(eh_whole, tile), of_tile(el_whole, tile),
                of_tile(inner_whole, tile), of_tile(grad_whole, tile),
                diag_ref.at[u * TILE_GROUPS : (u + 1) * TILE_GROUPS],
                toep_all.at[u], power_all.at[u], fold_all.at[u], rate_rows, gain_rows,
            )
        )
    staggered(parts)


def inside_tile(
    tile, z_ref, eh_ref, el_ref, inner_ref, grad_ref, diag_ref,
    toep_all, power_all, fold_all, rate_rows, gain_rows,
):
    rate_tile, coef_tile = parameters(tile, rate_rows, gain_rows)
    rates, coefs = per_mode(rate_tile), per_mode(coef_tile)
    lag = iota(1, (LANES, LANES)).astype(f32)
    row_at = iota(0, (LANES, LANES))
    lane_at = iota(1, (LANES, LANES))
    power = jnp.exp(-rates * lag)
    power_all[...] = power
    taps = jnp.sum((coefs * power).reshape(TILE_GROUPS, MODES, LANES), axis=1)
    for g in range(TILE_GROUPS):
        z_back = jnp.transpose(z_ref[g])
        gram = dot_nn(
            jnp.concatenate([z_back, z_back], axis=1),
            jnp.concatenate([eh_ref[g], el_ref[g]], axis=0),
        )
        gram = jnp.where(lane_at >= row_at, gram, 0.0)
        folded = [gram[0:8]] + [
            pltpu.roll(gram[8 * r : 8 * r + 8], LANES - 8 * r, 1) for r in range(1, LANES // 8)
        ]
        while len(folded) > 1:
            folded = [folded[i] + folded[i + 1] for i in range(0, len(folded), 2)]
        fold_all[8 * g : 8 * g + 8, :] = folded[0]
        yield 1
    for g in range(TILE_GROUPS):
        high, low = split(jnp.where(lane_at >= row_at, circulant(taps[g : g + 1]), 0.0))
        toep_all[g, 0:LANES, :] = high
        toep_all[g, LANES:, :] = low
        yield 2
    for g in range(TILE_GROUPS):
        z, eh, el = z_ref[g], eh_ref[g], el_ref[g]
        high = toep_all[g, 0:LANES, :]
        inner_ref[g] = dot_nn(jnp.concatenate([z, z], axis=1), toep_all[g])
        grad_ref[g] = dot_nt(
            jnp.concatenate([eh, el, eh], axis=1),
            jnp.concatenate([high, high, toep_all[g, LANES:, :]], axis=1),
        )
        yield 3
    corr = jnp.sum(sheared(fold_all[...], 8).reshape(TILE_GROUPS, 8, LANES), axis=1)
    weighted = power_all[...] * per_member(corr)
    first_col = jnp.sum(weighted, axis=1, keepdims=True)
    lag_col = jnp.sum(lag * weighted, axis=1, keepdims=True)
    mode_at = row_at % MODES
    placed = jnp.where(lane_at == mode_at, first_col, 0.0) + jnp.where(
        lane_at == mode_at + 32, lag_col, 0.0
    )
    diag_ref[...] = jnp.sum(placed.reshape(TILE_GROUPS, MODES, LANES), axis=1)


def exact_dot(left, right, dims):
    return lax.dot_general(
        left, right, (dims, ((), ())), precision=lax.Precision.HIGHEST, preferred_element_type=f32
    )


def join_kernel(
    tokens, me_ref, state_ref, own_ref, diag_ref, cross_ref, taps_ref, rate_ref, gain_ref, *refs
):
    gots, (bound_ref, local_ref, edges_all) = refs[:-3], refs[-3:]
    me = me_ref[0]
    channels = state_ref.shape[1]
    groups = rate_ref.shape[1]
    half = channels // 2
    chosen = (iota(0, (groups, channels)) == iota(1, (groups, channels)) // MEMBERS).astype(f32)
    rates = rate_ref[...]
    rate_cols = exact_dot(rates, chosen, ((1,), (0,)))
    edges_all[me] = own_ref[24:40]
    for key, got in enumerate(gots, 1):
        edges_all[me ^ key] = got[24:40]

    def tail_of(device):
        return jnp.where(device > 0, edges_all[jnp.maximum(device - 1, 0)][8:14], 0.0)

    def first_tokens(device):
        head, tail = edges_all[device], tail_of(device)
        shorts = []
        for i in range(3):
            tap = [taps_ref[i, j : j + 1, :] for j in range(3)]
            now, last = head[2 * i : 2 * i + 2], tail[2 * i : 2 * i + 2]
            shorts.append(
                (
                    tap[0] * now[0:1] + tap[1] * last[1:2] + tap[2] * last[0:1],
                    tap[0] * now[1:2] + tap[1] * now[0:1] + tap[2] * last[1:2],
                )
            )
        z = [(shorts[1][t] * shorts[2][t]).astype(bf16).astype(f32) for t in range(2)]
        e = [head[6 + t : 7 + t] * shorts[0][t] for t in range(2)]
        return z, e

    decay = jnp.exp(-rate_cols)
    decay_2 = decay * decay
    grow = jnp.exp(rate_cols)
    to_end = [jnp.exp(-rate_cols * float(tokens - 1)), jnp.exp(-rate_cols * float(tokens - 2))]
    from_start = [decay, decay_2]
    zero = jnp.zeros((MODES, channels), f32)
    zero_half = jnp.zeros((MODES, half), f32)
    s_prev, e_next = zero, zero
    s_lag, e_lag = zero_half, zero_half
    ahead = jnp.zeros((8, channels), f32)
    for key, got in enumerate(gots, 1):
        other = me ^ key
        earlier = other < me
        z, e = first_tokens(other)
        add = [
            jnp.where(earlier, to_end[t] * z[t], from_start[t] * e[t]) for t in range(2)
        ]
        steps = [
            jnp.where(earlier, tokens - 1 - t, t + 1).astype(f32) for t in range(2)
        ]
        added = steps[0] * add[0] + steps[1] * add[1]
        away = ((jnp.abs(me - other) - 1) * tokens).astype(f32)
        weight = jnp.exp(-rate_cols * away)
        part = weight * (got[0:16] + add[0] + add[1])

        def halved(value):
            return jnp.where(earlier, value[:, :half], value[:, half:])

        lagged = jnp.concatenate([got[16:24, :half], got[16:24, half:]], axis=0) + halved(added)
        lag_part = halved(weight) * lagged + away * halved(part)
        s_prev = s_prev + jnp.where(earlier, part, 0.0)
        s_lag = s_lag + jnp.where(earlier, lag_part, 0.0)
        e_next = e_next + jnp.where(earlier, 0.0, part)
        e_lag = e_lag + jnp.where(earlier, 0.0, lag_part)
        ahead = ahead + jnp.where(other == me + 1, got[24:32], 0.0)
    z, e = first_tokens(me)
    ends, lagged, moment_0, moment_1 = [state_ref[16 * i : 16 * i + 16] for i in range(4)]
    at_end = [to_end[t] * z[t] for t in range(2)]
    at_start = [from_start[t] * e[t] for t in range(2)]
    own_s = ends + at_end[0] + at_end[1]
    own_l = lagged + float(tokens - 1) * at_end[0] + float(tokens - 2) * at_end[1]
    own_m = moment_0 + at_start[0] + at_start[1]
    own_n = moment_1 + at_start[0] + 2.0 * at_start[1]
    early_0, early_1 = grow * z[0], grow * grow * z[1]
    early = early_0 + early_1
    bound_ref[0:16] = s_prev + early
    bound_ref[16:32] = e_next
    bound_ref[32:48] = own_s + jnp.exp(-rate_cols * float(tokens)) * s_prev
    bound_ref[48:56] = ahead
    bound_ref[56:62] = tail_of(me)
    bound_ref[62:64] = jnp.zeros((2, channels), f32)

    def joined(first_half, second_half):
        return jnp.concatenate([first_half[:, :half], second_half[:, half:]], axis=1)

    back = decay * e[1] * z[0]
    first_terms = (
        joined(own_m * s_prev, own_s * e_next) + moment_0 * early + e[0] * z[0] + e[1] * z[1] + back
    )
    lag_terms = (
        joined(own_n * s_prev, own_l * e_next)
        + jnp.concatenate([own_m[:, :half] * s_lag, own_s[:, half:] * e_lag], axis=1)
        + moment_1 * early
        - moment_0 * (early_0 + 2.0 * early_1)
        + back
    )
    sums = exact_dot(jnp.concatenate([first_terms, lag_terms], axis=0), chosen, ((1,), (1,)))
    own = jnp.transpose(cross_ref[...] + diag_ref[...])
    first = sums[0:16] + own[0:16]
    lag_sum = -(sums[16:32] + own[32:48] + own[48:64])
    root = jnp.sqrt(2.0 * rates)
    local_ref[0:16] = root * first
    local_ref[16:32] = gain_ref[...] * root * (0.5 * first + rates * lag_sum)


def output_kernel(
    first, start_ref, edge_ref, taps_ref, cot_ref, rate_ref, gain_ref,
    inner_whole, grad_whole, carry_whole, short_whole, bound_ref,
    *refs,
):
    (
        mixer_hbm, fgrad_hbm, mixer_all, fgrad_all, sems,
        wide, adj, inner_t, grad_t, left_all, rate_rows, gain_rows,
    ) = refs[-12:]
    fill_tables(rate_ref, gain_ref, rate_rows, gain_rows)
    count = cot_ref.shape[1] // LANES
    total = mixer_all.shape[0]

    def copies(local):
        lanes = pl.ds(pl.multiple_of((local + first) * LANES, LANES), LANES)
        return [
            pltpu.make_async_copy(mixer_all.at[local], mixer_hbm.at[:, lanes], sems.at[local, 3])
        ] + [
            pltpu.make_async_copy(
                fgrad_all.at[local, i], fgrad_hbm.at[i, :, lanes], sems.at[local, i]
            )
            for i in range(3)
        ]

    parts = []
    for u in range(count):
        tile = pl.program_id(0) * count + u + first
        lanes = slice(u * LANES, (u + 1) * LANES)
        parts.append(
            output_tile(
                tile, start_ref.at[:, :, lanes], edge_ref.at[:, :, lanes],
                taps_ref.at[:, :, lanes], cot_ref.at[:, lanes],
                of_tile(inner_whole, tile), of_tile(grad_whole, tile),
                carry_whole.at[tile], short_whole.at[tile], bound_ref.at[:, lanes],
                mixer_all.at[tile - first], fgrad_all.at[tile - first], copies(tile - first),
                wide.at[u], adj.at[u], inner_t.at[u], grad_t.at[u], left_all.at[u],
                rate_rows, gain_rows,
            )
        )
    staggered(parts)

    @pl.when(pl.program_id(0) == pl.num_programs(0) - 1)
    def _():
        for local in range(total):
            for copy in copies(local):
                copy.wait()


def output_tile(
    tile, start_ref, edge_ref, taps_ref, cot_ref,
    inner_ref, grad_ref, carry_ref, short_ref, bound_ref,
    mixer_ref, fgrad_ref, copies,
    wide, adj, inner_t, grad_t, left_all, rate_rows, gain_rows,
):
    tokens = cot_ref.shape[0]
    blocks = tokens // LANES
    rate_tile, coef_tile = parameters(tile, rate_rows, gain_rows)
    rates, coefs = per_mode(rate_tile), per_mode(coef_tile)
    lag = iota(1, (LANES, LANES)).astype(f32)
    lane_at = iota(1, (LANES, LANES))
    is_low = ((lane_at >= 16) & (lane_at < 32)) | ((lane_at >= 80) & (lane_at < 96))
    before = bound_ref[0:16]
    after = bound_ref[16:32]
    gap = jnp.zeros((MODES, LANES), f32)
    stacked = jnp.concatenate([before, before, before, gap, after, after, gap, after], axis=0)
    turned = jnp.transpose(stacked)
    none_16 = jnp.zeros((MODES, LANES), bf16)
    none_64 = jnp.zeros((4 * MODES, LANES), bf16)
    member_rates = per_member(rate_tile)
    span = jnp.exp(member_rates * (-float(LANES)))
    from_others = turned
    for b in range(blocks):
        value = carry_ref[b] + from_others
        from_others = from_others * span
        high = value.astype(bf16).astype(f32)
        mixed = jnp.where(is_low, value - high, value).astype(bf16)
        for g in range(TILE_GROUPS):
            left_all[g, b * MEMBERS : (b + 1) * MEMBERS, :] = mixed[
                g * MEMBERS : (g + 1) * MEMBERS
            ]
        yield 0.5
    cz_parts = split(coefs * jnp.exp(-rates * (lag + 1.0)))
    ce_parts = split(coefs * jnp.exp(-rates * (LANES - 1.0 - lag)))
    for g in range(TILE_GROUPS):
        of = slice(g * MODES, (g + 1) * MODES)
        cz_high, cz_low = cz_parts[0][of], cz_parts[1][of]
        ce_high, ce_low = ce_parts[0][of], ce_parts[1][of]
        right = jnp.concatenate(
            [
                jnp.concatenate([cz_high, cz_high, cz_low, none_16, none_64], axis=0),
                jnp.concatenate([none_64, ce_high, ce_high, none_16, ce_low], axis=0),
            ],
            axis=1,
        )
        carried = dot_nn(left_all[g], right)
        for b in range(blocks):
            at = slice(b * MEMBERS, (b + 1) * MEMBERS)
            opposite = slice((blocks - 1 - b) * MEMBERS, (blocks - b) * MEMBERS)
            inner_t[b, of, :] = inner_ref[g, at, :] + carried[at, :LANES]
            grad_t[b, of, :] = grad_ref[g, at, :] + carried[opposite, LANES:]
        yield 1
    rates = jnp.transpose(member_rates)[0:MODES]
    coefs = jnp.transpose(per_member(coef_tile))[0:MODES]
    decay = jnp.exp(-rates)
    grow = jnp.exp(rates)
    state = bound_ref[32:48]
    sum_0 = jnp.sum(coefs, axis=0, keepdims=True)
    sum_1 = jnp.sum(coefs * decay, axis=0, keepdims=True)
    for i in range(3):
        wide[i, 0:8, :] = jnp.zeros((8, LANES), f32)
        wide[i, 6:8, :] = bound_ref[56 + 2 * i : 58 + 2 * i]
        wide[i, 8:16, :] = start_ref[i, 0:8, :].astype(f32)
    begun = [short_block(wide, taps_ref, i, 0, 8) for i in range(3)]
    z_own = (begun[1] * begun[2]).astype(bf16).astype(f32)
    e_own = cot_ref[0:8, :].astype(f32) * begun[0]
    sum_up = jnp.sum(coefs * grow, axis=0, keepdims=True)
    which = iota(0, (8, LANES))
    inner_fix = jnp.where(which == 0, -sum_up * z_own[1:2], 0.0)
    grad_fix = jnp.where(
        which == 0,
        sum_0 * e_own[0:1] + sum_1 * e_own[1:2],
        jnp.where(which == 1, sum_0 * e_own[1:2], 0.0),
    )
    for b in range(blocks):
        at = slice(b * LANES, (b + 1) * LANES)
        inner = jnp.transpose(inner_t[b])
        query = short_ref[0, at, :]
        if b == 0:
            query = jnp.concatenate([begun[0], short_ref[0, 8:LANES, :]], axis=0)
            inner = jnp.concatenate([inner[0:8] + inner_fix, inner[8:]], axis=0)
        mixer_ref[at, :] = (query * inner).astype(bf16)
        adj[0, at, :] = cot_ref[at, :].astype(f32) * inner
        yield 2
    copies[0].start()
    for b in range(blocks):
        at = slice(b * LANES, (b + 1) * LANES)
        grad = jnp.transpose(grad_t[b])
        key, value = short_ref[1, at, :], short_ref[2, at, :]
        if b == 0:
            key = jnp.concatenate([begun[1], short_ref[1, 8:LANES, :]], axis=0)
            value = jnp.concatenate([begun[2], short_ref[2, 8:LANES, :]], axis=0)
            grad = jnp.concatenate([grad[0:8] + grad_fix, grad[8:]], axis=0)
        adj[1, at, :] = grad * value
        adj[2, at, :] = grad * key
        yield 2
    for i in range(3):
        wide[i, 0:8, :] = edge_ref[i, 8:16, :].astype(f32)
        wide[i, 8:16, :] = jnp.zeros((8, LANES), f32)
        wide[i, 8:10, :] = bound_ref[48 + 2 * i : 50 + 2 * i]
    query, key, value = [short_block(wide, taps_ref, i, 0, 8) for i in range(3)]
    z = (key * value).astype(bf16).astype(f32)
    upstream = jnp.concatenate([bound_ref[54:56], jnp.zeros((6, LANES), f32)], axis=0)
    e = upstream * query
    inner_0 = jnp.sum(coefs * decay * state, axis=0, keepdims=True) + sum_0 * z[0:1]
    inner_1 = (
        jnp.sum(coefs * decay * decay * state, axis=0, keepdims=True)
        + sum_1 * z[0:1]
        + sum_0 * z[1:2]
    )
    grad_0 = jnp.sum(coefs * grow * after, axis=0, keepdims=True)
    grad_1 = jnp.sum(coefs * grow * (grow * after - e[0:1]), axis=0, keepdims=True)
    inner_8 = jnp.where(which == 0, inner_0, jnp.where(which == 1, inner_1, 0.0))
    grad_8 = jnp.where(which == 0, grad_0, jnp.where(which == 1, grad_1, 0.0))
    adj[0, tokens : tokens + 8, :] = upstream * inner_8
    adj[1, tokens : tokens + 8, :] = grad_8 * value
    adj[2, tokens : tokens + 8, :] = grad_8 * key
    for i in range(3):
        for b in range(blocks):
            start = b * LANES
            fgrad_ref[i, start : start + LANES, :] = (
                taps_ref[i, 0:1, :] * adj[i, start : start + LANES, :]
                + taps_ref[i, 1:2, :] * adj[i, start + 1 : start + 1 + LANES, :]
                + taps_ref[i, 2:3, :] * adj[i, start + 2 : start + 2 + LANES, :]
            ).astype(bf16)
            yield 3
        copies[1 + i].start()


def resident(shape, dtype):
    return pltpu.VMEM(shape, dtype)


def sum_kernel(*refs):
    *terms, summed_ref, square_ref = refs
    terms = [term[...] for term in terms]
    while len(terms) > 1:
        terms = [terms[i] + terms[i + 1] for i in range(0, len(terms), 2)]
    summed_ref[...] = terms[0]
    square_ref[...] = jnp.broadcast_to(
        jnp.sum(jnp.sum(terms[0] * terms[0], axis=0, keepdims=True), axis=1, keepdims=True),
        square_ref.shape,
    )


def far(*arrays):
    return [pltpu.with_memory_space_constraint(array, pltpu.HBM) for array in arrays]


def near(*arrays):
    return [pltpu.with_memory_space_constraint(array, pltpu.VMEM) for array in arrays]


def swapped(value, axis, key):
    count = lax.axis_size(axis)
    return lax.ppermute(value, axis, [(i, i ^ key) for i in range(count)])


def per_device(features, short_taps, decay_rates, mode_gains, cotangent):
    tokens = features.shape[1]
    channels = features.shape[2]
    groups = decay_rates.shape[0]
    tiles = channels // LANES
    blocks = tokens // LANES
    ctx_count = lax.axis_size("ctx")
    ctx_index = lax.axis_index("ctx")

    me = ctx_index.astype(jnp.int32).reshape(1)
    rates, gains = decay_rates.T, mode_gains.T

    whole = pl.BlockSpec(memory_space=pltpu.VMEM)
    per = STATE_PER if tiles % STATE_PER == 0 else 1
    feat_spec = pl.BlockSpec((3, tokens, per * LANES), lambda j: (0, 0, j))
    taps_spec = pl.BlockSpec((3, 3, per * LANES), lambda j: (0, 0, j))
    cot_spec = pl.BlockSpec((tokens, per * LANES), lambda j: (0, j))
    table_spec = pl.BlockSpec((MODES, groups), lambda j: (0, 0))
    me_spec = pl.BlockSpec(memory_space=pltpu.SMEM)
    rows = blocks * MEMBERS
    turned = resident((groups, rows, LANES), bf16)
    wide_turned = resident((groups, rows, LANES), f32)
    slots = jax.ShapeDtypeStruct((groups, LANES), f32)
    table_scratch = [pltpu.VMEM((LANES, LANES), f32), pltpu.VMEM((LANES, LANES), f32)]

    def room(mebibytes):
        return pltpu.CompilerParams(vmem_limit_bytes=mebibytes * 2**20)

    z, eh, el, carry, short, states, cross, later, early = pl.pallas_call(
        state_kernel,
        grid=(tiles // per,),
        in_specs=[feat_spec, taps_spec, cot_spec, table_spec, table_spec],
        out_specs=[
            whole,
            whole,
            whole,
            whole,
            whole,
            pl.BlockSpec((4 * MODES, per * LANES), lambda j: (0, j)),
            pl.BlockSpec((per * TILE_GROUPS, LANES), lambda j: (j, 0)),
            whole,
            whole,
        ],
        out_shape=[
            turned,
            turned,
            turned,
            resident((tiles, blocks, LANES, LANES), f32),
            resident((tiles, 3, tokens, LANES), f32),
            jax.ShapeDtypeStruct((4 * MODES, channels), f32),
            slots,
            resident((40, channels), f32),
            resident((40, channels), f32),
        ],
        scratch_shapes=[
            pltpu.VMEM((per, 3, tokens + 8, LANES), f32),
            pltpu.VMEM((per, blocks, LANES, LANES), f32),
            pltpu.VMEM((per, TILE_GROUPS, LANES, 2 * LANES), bf16),
        ]
        + table_scratch,
        compiler_params=room(STATE_ROOM),
        name="state_part",
    )(*far(features, short_taps, cotangent, rates, gains))

    gots = []
    for key in range(1, ctx_count):
        sent = jnp.where((ctx_index ^ key) < ctx_index, early, later)
        gots.append(swapped(sent.astype(bf16), "ctx", key).astype(f32))

    inside_per = INSIDE_PER if tiles % INSIDE_PER == 0 else 1
    inner, grad, diag = pl.pallas_call(
        inside_kernel,
        grid=(tiles // inside_per,),
        in_specs=[whole, whole, whole, table_spec, table_spec],
        out_specs=[
            whole,
            whole,
            pl.BlockSpec((inside_per * TILE_GROUPS, LANES), lambda j: (j, 0)),
        ],
        out_shape=[wide_turned, wide_turned, slots],
        scratch_shapes=[
            pltpu.VMEM((inside_per, TILE_GROUPS, 2 * LANES, LANES), bf16),
            pltpu.VMEM((inside_per, LANES, LANES), f32),
            pltpu.VMEM((inside_per, 8 * TILE_GROUPS, LANES), f32),
        ]
        + table_scratch,
        compiler_params=room(14),
        cost_estimate=pl.CostEstimate(
            flops=2 * groups * rows * LANES * LANES * 7, bytes_accessed=14 * 2**20, transcendentals=0
        ),
        name="inside_part",
    )(*near(z, eh, el), *far(rates, gains))

    bound, local = pl.pallas_call(
        functools.partial(join_kernel, tokens),
        in_specs=[me_spec] + [whole] * (7 + len(gots)),
        out_specs=[whole, whole],
        out_shape=[
            jax.ShapeDtypeStruct((64, channels), f32),
            jax.ShapeDtypeStruct((2 * MODES, groups), f32),
        ],
        scratch_shapes=[pltpu.VMEM((ctx_count, 16, channels), f32)],
        compiler_params=room(14),
        name="join_part",
    )(me, states, later, diag, cross, short_taps, rates, gains, *gots)

    def outputs(first, count, *written):
        per = OUTPUT_PER if count % OUTPUT_PER == 0 and first % OUTPUT_PER == 0 else 1
        wide_lanes = per * LANES
        columns = lambda j: (0, j + first // per)
        layers = lambda j: (0, 0, j + first // per)
        return pl.pallas_call(
            functools.partial(output_kernel, first),
            grid=(count // per,),
            in_specs=[
                pl.BlockSpec((3, 16, wide_lanes), layers),
                pl.BlockSpec((3, 16, wide_lanes), lambda j: (0, tokens // 16 - 1, j + first // per)),
                pl.BlockSpec((3, 3, wide_lanes), layers),
                pl.BlockSpec((tokens, wide_lanes), columns),
                table_spec,
                table_spec,
                whole,
                whole,
                whole,
                whole,
                pl.BlockSpec((64, wide_lanes), columns),
            ]
            + [pl.BlockSpec(memory_space=pl.ANY)] * len(written),
            out_specs=[pl.BlockSpec(memory_space=pl.ANY)] * 2,
            out_shape=[
                jax.ShapeDtypeStruct((tokens, channels), bf16),
                jax.ShapeDtypeStruct((3, tokens, channels), bf16),
            ],
            scratch_shapes=[
                pltpu.VMEM((count, tokens, LANES), bf16),
                pltpu.VMEM((count, 3, tokens, LANES), bf16),
                pltpu.SemaphoreType.DMA((count, 4)),
                pltpu.VMEM((per, 3, 16, LANES), f32),
                pltpu.VMEM((per, 3, tokens + 8, LANES), f32),
                pltpu.VMEM((per, blocks, LANES, LANES), f32),
                pltpu.VMEM((per, blocks, LANES, LANES), f32),
                pltpu.VMEM((per, TILE_GROUPS, rows, LANES), bf16),
            ]
            + table_scratch,
            compiler_params=room(OUTPUT_ROOM),
            input_output_aliases={11: 0, 12: 1} if written else {},
            cost_estimate=pl.CostEstimate(
                flops=2 * count * TILE_GROUPS * rows * LANES * LANES * 8,
                bytes_accessed=count * 4 * 2**20,
                transcendentals=0,
            ),
            name="output_part",
        )(
            *far(features, features, short_taps, cotangent, rates, gains),
            *near(inner, grad, carry, short),
            bound,
            *written,
        )

    half = tiles // 2
    terms = [local] + [swapped(local, "ctx", key) for key in range(1, ctx_count)]
    written = outputs(0, half)
    terms, written = lax.optimization_barrier((terms, written))
    summed, squares = pl.pallas_call(
        sum_kernel,
        in_specs=[whole] * len(terms),
        out_specs=[whole, whole],
        out_shape=[
            jax.ShapeDtypeStruct((2 * MODES, groups), f32),
            jax.ShapeDtypeStruct((1, groups), f32),
        ],
        compiler_params=room(14),
        name="sum_part",
    )(*terms)
    fsdp_count = lax.axis_size("fsdp")
    step = 1
    while step * 4 < fsdp_count:
        squares = squares + swapped(squares, "fsdp", step)
        step *= 2
    squares, written = lax.optimization_barrier((squares, written))
    parts = [squares] + [swapped(squares, "fsdp", key) for key in range(step, fsdp_count, step)]
    mixer, feature_grads = outputs(half, tiles - half, *written)
    while len(parts) > 1:
        parts = [parts[i] + parts[i + 1] for i in range(0, len(parts), 2)]
    entry_count = 2 * groups * MODES * fsdp_count
    clipped = summed * jnp.minimum(1.0, lax.rsqrt(parts[0] / entry_count + 1e-06))
    return (mixer, feature_grads, clipped[:MODES].T, clipped[MODES:].T)


def solution(mesh):
    return jax.shard_map(
        per_device,
        mesh=mesh,
        in_specs=(
            P(None, "ctx", "fsdp"),
            P(None, None, "fsdp"),
            P("fsdp", None),
            P("fsdp", None),
            P("ctx", "fsdp"),
        ),
        out_specs=(P("ctx", "fsdp"), P(None, "ctx", "fsdp"), P("fsdp", None), P("fsdp", None)),
        check_vma=False,
    )
```

```python
import functools

import jax
import jax.numpy as jnp
from jax import lax
from jax.experimental import pallas as pl
from jax.experimental.pallas import tpu as pltpu
from jax.sharding import PartitionSpec as P

LANES = 128
MODES = 16
MEMBERS = 16
TILE_GROUPS = LANES // MEMBERS
ROWS = LANES
f32 = jnp.float32
bf16 = jnp.bfloat16
STATE_PER = 2
OUTPUT_PER = 2
INSIDE_PER = 2
STATE_ROOM = 18
OUTPUT_ROOM = 18


def split(value):
    high = value.astype(bf16)
    return high, (value - high.astype(f32)).astype(bf16)


def dot_nt(left, right):
    return lax.dot_general(left, right, (((1,), (1,)), ((), ())), preferred_element_type=f32)


def dot_tn(left, right):
    return lax.dot_general(left, right, (((0,), (0,)), ((), ())), preferred_element_type=f32)


def dot_nn(left, right):
    return lax.dot_general(left, right, (((1,), (0,)), ((), ())), preferred_element_type=f32)


def iota(axis, shape):
    return lax.broadcasted_iota(jnp.int32, shape, axis)


def widen(feat_ref, wide, tokens):
    for i in range(3):
        wide[i, 0:8, :] = jnp.zeros((8, LANES), f32)
        wide[i, 8 : 8 + tokens, :] = feat_ref[i].astype(f32)


def short_block(wide, taps_ref, i, start, count):
    return (
        taps_ref[i, 0:1, :] * wide[i, start + 8 : start + 8 + count, :]
        + taps_ref[i, 1:2, :] * wide[i, start + 7 : start + 7 + count, :]
        + taps_ref[i, 2:3, :] * wide[i, start + 6 : start + 6 + count, :]
    )


def sheared(row8, period):
    which = iota(0, row8.shape) % period
    for bit in (1, 2, 4):
        row8 = jnp.where((which & bit) != 0, pltpu.roll(row8, LANES - bit, 1), row8)
    return row8


def circulant(row):
    return pltpu.roll(jnp.broadcast_to(row, (LANES, LANES)), 0, 1, stride=1, stride_axis=0)


def of_tile(whole, tile):
    return whole.at[pl.ds(tile * TILE_GROUPS, TILE_GROUPS)]


def staggered(parts):
    phase = [0] * len(parts)
    open_parts = [True] * len(parts)
    while any(open_parts):
        for u, part in enumerate(parts):
            if not open_parts[u] or (u and open_parts[u - 1] and phase[u] >= phase[u - 1]):
                continue
            got = next(part, None)
            if got is None:
                open_parts[u] = False
            else:
                phase[u] = got


def table_rows(source_ref, rows_ref):
    tall = jnp.concatenate([source_ref[...]] * (LANES // MODES), axis=0)
    missing = LANES - tall.shape[1]
    if missing:
        tall = jnp.concatenate([tall, jnp.zeros((LANES, missing), f32)], axis=1)
    rows_ref[...] = jnp.transpose(tall)


def fill_tables(rate_ref, gain_ref, rate_rows, gain_rows):
    @pl.when(pl.program_id(0) == 0)
    def _():
        table_rows(rate_ref, rate_rows)
        table_rows(gain_ref, gain_rows)


def parameters(tile, rate_rows, gain_rows):
    at = pl.ds(pl.multiple_of(tile * TILE_GROUPS, TILE_GROUPS), TILE_GROUPS)
    rates = rate_rows[at, :]
    return rates, gain_rows[at, :] * jnp.sqrt(2.0 * rates)


def per_mode(rows):
    own = iota(0, (TILE_GROUPS, LANES)) == iota(1, (TILE_GROUPS, LANES)) // MODES
    flat = jnp.sum(jnp.where(own, rows, 0.0), axis=0, keepdims=True)
    return jnp.transpose(jnp.broadcast_to(flat, (LANES, LANES)))


def per_member(rows):
    return jnp.concatenate(
        [jnp.broadcast_to(rows[g : g + 1], (MEMBERS, LANES)) for g in range(TILE_GROUPS)], axis=0
    )


def state_kernel(
    feat_ref, taps_ref, cot_ref, rate_ref, gain_ref,
    z_whole, eh_whole, el_whole, carry_whole, short_whole, state_ref, cross_ref,
    later_ref, earlier_ref,
    wide, own_all, table_all, rate_rows, gain_rows,
):
    fill_tables(rate_ref, gain_ref, rate_rows, gain_rows)
    count = cot_ref.shape[1] // LANES
    parts = []
    for u in range(count):
        tile = pl.program_id(0) * count + u
        lanes = slice(u * LANES, (u + 1) * LANES)
        parts.append(
            state_tile(
                tile, feat_ref.at[:, :, lanes], taps_ref.at[:, :, lanes], cot_ref.at[:, lanes],
                of_tile(z_whole, tile), of_tile(eh_whole, tile), of_tile(el_whole, tile),
                carry_whole.at[tile], short_whole.at[tile], state_ref.at[:, lanes],
                cross_ref.at[u * TILE_GROUPS : (u + 1) * TILE_GROUPS], later_ref, earlier_ref,
                wide.at[u], own_all.at[u], table_all.at[u], rate_rows, gain_rows,
            )
        )
    staggered(parts)


def state_tile(
    tile, feat_ref, taps_ref, cot_ref,
    z_ref, eh_ref, el_ref, carry_ref, short_ref, state_ref, cross_ref, later_ref, earlier_ref,
    wide, own_all, table_all, rate_rows, gain_rows,
):
    tokens = feat_ref.shape[1]
    blocks = tokens // LANES
    rate_tile, _ = parameters(tile, rate_rows, gain_rows)
    rates = per_mode(rate_tile)
    lag = iota(1, (LANES, LANES)).astype(f32)
    lane_at = iota(1, (LANES, LANES))
    lane_row = iota(1, (1, LANES))

    back = jnp.exp(-rates * (LANES - 1.0 - lag))
    after = jnp.exp(-rates * (lag + 1.0))
    s_parts = split(back)
    l_parts = split((LANES - 1.0 - lag) * back)
    m_parts = split(after)
    n_parts = split((lag + 1.0) * after)
    for g in range(TILE_GROUPS):
        of = slice(g * MODES, (g + 1) * MODES)
        for part in range(2):
            s_of, l_of = s_parts[part][of], l_parts[part][of]
            m_of, n_of = m_parts[part][of], n_parts[part][of]
            table_all[g, :, part * LANES : (part + 1) * LANES] = jnp.concatenate(
                [s_of, s_of, s_of, l_of, m_of, m_of, n_of, m_of], axis=0
            )
        yield 0.5

    widen(feat_ref, wide, tokens)
    for b in range(blocks):
        query = short_block(wide, taps_ref, 0, b * LANES, LANES)
        key = short_block(wide, taps_ref, 1, b * LANES, LANES)
        value = short_block(wide, taps_ref, 2, b * LANES, LANES)
        short_ref[0, b * LANES : (b + 1) * LANES, :] = query
        short_ref[1, b * LANES : (b + 1) * LANES, :] = key
        short_ref[2, b * LANES : (b + 1) * LANES, :] = value
        product = key * value
        adjoint = cot_ref[b * LANES : (b + 1) * LANES, :].astype(f32) * query
        if b == 0:
            inside = iota(0, (LANES, LANES)) >= 2
            product = jnp.where(inside, product, 0.0)
            adjoint = jnp.where(inside, adjoint, 0.0)
        z_t = jnp.transpose(product.astype(bf16))
        e_t = jnp.transpose(adjoint)
        e_high, e_low = split(e_t)
        at = slice(b * MEMBERS, (b + 1) * MEMBERS)
        for g in range(TILE_GROUPS):
            of = slice(g * MEMBERS, (g + 1) * MEMBERS)
            z_ref[g, at, :] = z_t[of]
            eh_ref[g, at, :] = e_high[of]
            el_ref[g, at, :] = e_low[of]
        yield 1

    for g in range(TILE_GROUPS):
        of = slice(g * MEMBERS, (g + 1) * MEMBERS)
        z, eh, el = z_ref[g], eh_ref[g], el_ref[g]
        left = jnp.concatenate(
            [
                jnp.concatenate([z, z], axis=1),
                jnp.concatenate([eh, eh], axis=1),
                jnp.concatenate([el, jnp.zeros_like(el)], axis=1),
            ],
            axis=0,
        )
        got = dot_nt(left, table_all[g])
        rows = z.shape[0]
        from_e = got[rows : 2 * rows] + got[2 * rows :]
        for b in range(blocks):
            at = slice(b * MEMBERS, (b + 1) * MEMBERS)
            opposite = slice((blocks - 1 - b) * MEMBERS, (blocks - b) * MEMBERS)
            own_all[b, of, :] = jnp.where(
                iota(1, (MEMBERS, LANES)) < 64, got[at], from_e[opposite]
            )
        yield 2

    span = per_member(jnp.exp(rate_tile * (-float(LANES))))
    in_lag = jnp.where(
        ((lane_row >= 48) & (lane_row < 64)) | ((lane_row >= 96) & (lane_row < 112)),
        float(LANES),
        0.0,
    )
    now = jnp.zeros((LANES, LANES), f32)
    lagged = jnp.zeros((LANES, LANES), f32)
    cross = jnp.zeros((LANES, LANES), f32)
    for b in range(blocks):
        own = own_all[b]
        cross = cross + now * pltpu.roll(own_all[blocks - 1 - b], 4 * MODES, 1)
        carry_ref[b] = now
        now = span * (now + lagged) + own
        if b < blocks - 1:
            lagged = span * lagged + in_lag * pltpu.roll(own, MODES, 1)
        yield 3
    cross_ref[...] = jnp.sum(cross.reshape(TILE_GROUPS, MEMBERS, LANES), axis=1)
    turned = jnp.transpose(now)
    state_ref[0:16] = turned[0:16]
    state_ref[16:32] = turned[48:64]
    state_ref[32:48] = turned[64:80]
    state_ref[48:64] = turned[96:112]

    half = later_ref.shape[1] // 2
    here = pl.ds(pl.multiple_of(tile * LANES, LANES), LANES)
    edges = jnp.concatenate(
        [wide[i, 8:10, :] for i in range(3)]
        + [cot_ref[0:2, :].astype(f32)]
        + [wide[i, 6 + tokens : 8 + tokens, :] for i in range(3)]
        + [jnp.zeros((2, LANES), f32)],
        axis=0,
    )
    for out_ref, main in ((later_ref, turned[0:16]), (earlier_ref, turned[64:80])):
        out_ref[0:16, here] = main
        out_ref[24:40, here] = edges

    def place(out_ref, lag_rows, start):
        for part in range(2):
            at = pl.ds(pl.multiple_of(start + part * half, LANES), LANES)
            out_ref[16:24, at] = lag_rows[8 * part : 8 * part + 8]

    @pl.when(tile * LANES < half)
    def _():
        place(later_ref, turned[48:64], tile * LANES)

    @pl.when(tile * LANES >= half)
    def _():
        place(earlier_ref, turned[96:112], tile * LANES - half)


def inside_kernel(
    z_whole, eh_whole, el_whole, rate_ref, gain_ref,
    inner_whole, grad_whole, diag_ref,
    toep_all, power_all, fold_all, rate_rows, gain_rows,
):
    fill_tables(rate_ref, gain_ref, rate_rows, gain_rows)
    count = diag_ref.shape[0] // TILE_GROUPS
    parts = []
    for u in range(count):
        tile = pl.program_id(0) * count + u
        parts.append(
            inside_tile(
                tile, of_tile(z_whole, tile), of_tile(eh_whole, tile), of_tile(el_whole, tile),
                of_tile(inner_whole, tile), of_tile(grad_whole, tile),
                diag_ref.at[u * TILE_GROUPS : (u + 1) * TILE_GROUPS],
                toep_all.at[u], power_all.at[u], fold_all.at[u], rate_rows, gain_rows,
            )
        )
    staggered(parts)


def inside_tile(
    tile, z_ref, eh_ref, el_ref, inner_ref, grad_ref, diag_ref,
    toep_all, power_all, fold_all, rate_rows, gain_rows,
):
    rate_tile, coef_tile = parameters(tile, rate_rows, gain_rows)
    rates, coefs = per_mode(rate_tile), per_mode(coef_tile)
    lag = iota(1, (LANES, LANES)).astype(f32)
    row_at = iota(0, (LANES, LANES))
    lane_at = iota(1, (LANES, LANES))
    power = jnp.exp(-rates * lag)
    power_all[...] = power
    taps = jnp.sum((coefs * power).reshape(TILE_GROUPS, MODES, LANES), axis=1)
    for g in range(TILE_GROUPS):
        z_back = jnp.transpose(z_ref[g])
        gram = dot_nn(
            jnp.concatenate([z_back, z_back], axis=1),
            jnp.concatenate([eh_ref[g], el_ref[g]], axis=0),
        )
        gram = jnp.where(lane_at >= row_at, gram, 0.0)
        folded = [gram[0:8]] + [
            pltpu.roll(gram[8 * r : 8 * r + 8], LANES - 8 * r, 1) for r in range(1, LANES // 8)
        ]
        while len(folded) > 1:
            folded = [folded[i] + folded[i + 1] for i in range(0, len(folded), 2)]
        fold_all[8 * g : 8 * g + 8, :] = folded[0]
        yield 1
    for g in range(TILE_GROUPS):
        high, low = split(jnp.where(lane_at >= row_at, circulant(taps[g : g + 1]), 0.0))
        toep_all[g, 0:LANES, :] = high
        toep_all[g, LANES:, :] = low
        yield 2
    for g in range(TILE_GROUPS):
        z, eh, el = z_ref[g], eh_ref[g], el_ref[g]
        high = toep_all[g, 0:LANES, :]
        inner_ref[g] = dot_nn(jnp.concatenate([z, z], axis=1), toep_all[g])
        grad_ref[g] = dot_nt(
            jnp.concatenate([eh, el, eh], axis=1),
            jnp.concatenate([high, high, toep_all[g, LANES:, :]], axis=1),
        )
        yield 3
    corr = jnp.sum(sheared(fold_all[...], 8).reshape(TILE_GROUPS, 8, LANES), axis=1)
    weighted = power_all[...] * per_member(corr)
    first_col = jnp.sum(weighted, axis=1, keepdims=True)
    lag_col = jnp.sum(lag * weighted, axis=1, keepdims=True)
    mode_at = row_at % MODES
    placed = jnp.where(lane_at == mode_at, first_col, 0.0) + jnp.where(
        lane_at == mode_at + 32, lag_col, 0.0
    )
    diag_ref[...] = jnp.sum(placed.reshape(TILE_GROUPS, MODES, LANES), axis=1)


def exact_dot(left, right, dims):
    return lax.dot_general(
        left, right, (dims, ((), ())), precision=lax.Precision.HIGHEST, preferred_element_type=f32
    )


def join_kernel(
    tokens, me_ref, state_ref, own_ref, diag_ref, cross_ref, taps_ref, rate_ref, gain_ref, *refs
):
    gots, (bound_ref, local_ref, edges_all) = refs[:-3], refs[-3:]
    me = me_ref[0]
    channels = state_ref.shape[1]
    groups = rate_ref.shape[1]
    half = channels // 2
    chosen = (iota(0, (groups, channels)) == iota(1, (groups, channels)) // MEMBERS).astype(f32)
    rates = rate_ref[...]
    rate_cols = exact_dot(rates, chosen, ((1,), (0,)))
    edges_all[me] = own_ref[24:40]
    for key, got in enumerate(gots, 1):
        edges_all[me ^ key] = got[24:40]

    def tail_of(device):
        return jnp.where(device > 0, edges_all[jnp.maximum(device - 1, 0)][8:14], 0.0)

    def first_tokens(device):
        head, tail = edges_all[device], tail_of(device)
        shorts = []
        for i in range(3):
            tap = [taps_ref[i, j : j + 1, :] for j in range(3)]
            now, last = head[2 * i : 2 * i + 2], tail[2 * i : 2 * i + 2]
            shorts.append(
                (
                    tap[0] * now[0:1] + tap[1] * last[1:2] + tap[2] * last[0:1],
                    tap[0] * now[1:2] + tap[1] * now[0:1] + tap[2] * last[1:2],
                )
            )
        z = [(shorts[1][t] * shorts[2][t]).astype(bf16).astype(f32) for t in range(2)]
        e = [head[6 + t : 7 + t] * shorts[0][t] for t in range(2)]
        return z, e

    decay = jnp.exp(-rate_cols)
    decay_2 = decay * decay
    grow = jnp.exp(rate_cols)
    to_end = [jnp.exp(-rate_cols * float(tokens - 1)), jnp.exp(-rate_cols * float(tokens - 2))]
    from_start = [decay, decay_2]
    zero = jnp.zeros((MODES, channels), f32)
    zero_half = jnp.zeros((MODES, half), f32)
    s_prev, e_next = zero, zero
    s_lag, e_lag = zero_half, zero_half
    ahead = jnp.zeros((8, channels), f32)
    for key, got in enumerate(gots, 1):
        other = me ^ key
        earlier = other < me
        z, e = first_tokens(other)
        add = [
            jnp.where(earlier, to_end[t] * z[t], from_start[t] * e[t]) for t in range(2)
        ]
        steps = [
            jnp.where(earlier, tokens - 1 - t, t + 1).astype(f32) for t in range(2)
        ]
        added = steps[0] * add[0] + steps[1] * add[1]
        away = ((jnp.abs(me - other) - 1) * tokens).astype(f32)
        weight = jnp.exp(-rate_cols * away)
        part = weight * (got[0:16] + add[0] + add[1])

        def halved(value):
            return jnp.where(earlier, value[:, :half], value[:, half:])

        lagged = jnp.concatenate([got[16:24, :half], got[16:24, half:]], axis=0) + halved(added)
        lag_part = halved(weight) * lagged + away * halved(part)
        s_prev = s_prev + jnp.where(earlier, part, 0.0)
        s_lag = s_lag + jnp.where(earlier, lag_part, 0.0)
        e_next = e_next + jnp.where(earlier, 0.0, part)
        e_lag = e_lag + jnp.where(earlier, 0.0, lag_part)
        ahead = ahead + jnp.where(other == me + 1, got[24:32], 0.0)
    z, e = first_tokens(me)
    ends, lagged, moment_0, moment_1 = [state_ref[16 * i : 16 * i + 16] for i in range(4)]
    at_end = [to_end[t] * z[t] for t in range(2)]
    at_start = [from_start[t] * e[t] for t in range(2)]
    own_s = ends + at_end[0] + at_end[1]
    own_l = lagged + float(tokens - 1) * at_end[0] + float(tokens - 2) * at_end[1]
    own_m = moment_0 + at_start[0] + at_start[1]
    own_n = moment_1 + at_start[0] + 2.0 * at_start[1]
    early_0, early_1 = grow * z[0], grow * grow * z[1]
    early = early_0 + early_1
    bound_ref[0:16] = s_prev + early
    bound_ref[16:32] = e_next
    bound_ref[32:48] = own_s + jnp.exp(-rate_cols * float(tokens)) * s_prev
    bound_ref[48:56] = ahead
    bound_ref[56:62] = tail_of(me)
    bound_ref[62:64] = jnp.zeros((2, channels), f32)

    def joined(first_half, second_half):
        return jnp.concatenate([first_half[:, :half], second_half[:, half:]], axis=1)

    back = decay * e[1] * z[0]
    first_terms = (
        joined(own_m * s_prev, own_s * e_next) + moment_0 * early + e[0] * z[0] + e[1] * z[1] + back
    )
    lag_terms = (
        joined(own_n * s_prev, own_l * e_next)
        + jnp.concatenate([own_m[:, :half] * s_lag, own_s[:, half:] * e_lag], axis=1)
        + moment_1 * early
        - moment_0 * (early_0 + 2.0 * early_1)
        + back
    )
    sums = exact_dot(jnp.concatenate([first_terms, lag_terms], axis=0), chosen, ((1,), (1,)))
    own = jnp.transpose(cross_ref[...] + diag_ref[...])
    first = sums[0:16] + own[0:16]
    lag_sum = -(sums[16:32] + own[32:48] + own[48:64])
    root = jnp.sqrt(2.0 * rates)
    local_ref[0:16] = root * first
    local_ref[16:32] = gain_ref[...] * root * (0.5 * first + rates * lag_sum)


def output_kernel(
    first, start_ref, edge_ref, taps_ref, cot_ref, rate_ref, gain_ref,
    inner_whole, grad_whole, carry_whole, short_whole, bound_ref,
    *refs,
):
    (
        mixer_hbm, fgrad_hbm, mixer_all, fgrad_all, sems,
        wide, adj, inner_t, grad_t, left_all, rate_rows, gain_rows,
    ) = refs[-12:]
    fill_tables(rate_ref, gain_ref, rate_rows, gain_rows)
    count = cot_ref.shape[1] // LANES
    total = mixer_all.shape[0]

    def copies(local):
        lanes = pl.ds(pl.multiple_of((local + first) * LANES, LANES), LANES)
        return [
            pltpu.make_async_copy(mixer_all.at[local], mixer_hbm.at[:, lanes], sems.at[local, 3])
        ] + [
            pltpu.make_async_copy(
                fgrad_all.at[local, i], fgrad_hbm.at[i, :, lanes], sems.at[local, i]
            )
            for i in range(3)
        ]

    parts = []
    for u in range(count):
        tile = pl.program_id(0) * count + u + first
        lanes = slice(u * LANES, (u + 1) * LANES)
        parts.append(
            output_tile(
                tile, start_ref.at[:, :, lanes], edge_ref.at[:, :, lanes],
                taps_ref.at[:, :, lanes], cot_ref.at[:, lanes],
                of_tile(inner_whole, tile), of_tile(grad_whole, tile),
                carry_whole.at[tile], short_whole.at[tile], bound_ref.at[:, lanes],
                mixer_all.at[tile - first], fgrad_all.at[tile - first], copies(tile - first),
                wide.at[u], adj.at[u], inner_t.at[u], grad_t.at[u], left_all.at[u],
                rate_rows, gain_rows,
            )
        )
    staggered(parts)

    @pl.when(pl.program_id(0) == pl.num_programs(0) - 1)
    def _():
        for local in range(total):
            for copy in copies(local):
                copy.wait()


def output_tile(
    tile, start_ref, edge_ref, taps_ref, cot_ref,
    inner_ref, grad_ref, carry_ref, short_ref, bound_ref,
    mixer_ref, fgrad_ref, copies,
    wide, adj, inner_t, grad_t, left_all, rate_rows, gain_rows,
):
    tokens = cot_ref.shape[0]
    blocks = tokens // LANES
    rate_tile, coef_tile = parameters(tile, rate_rows, gain_rows)
    rates, coefs = per_mode(rate_tile), per_mode(coef_tile)
    lag = iota(1, (LANES, LANES)).astype(f32)
    lane_at = iota(1, (LANES, LANES))
    is_low = ((lane_at >= 16) & (lane_at < 32)) | ((lane_at >= 80) & (lane_at < 96))
    before = bound_ref[0:16]
    after = bound_ref[16:32]
    gap = jnp.zeros((MODES, LANES), f32)
    stacked = jnp.concatenate([before, before, before, gap, after, after, gap, after], axis=0)
    turned = jnp.transpose(stacked)
    none_16 = jnp.zeros((MODES, LANES), bf16)
    none_64 = jnp.zeros((4 * MODES, LANES), bf16)
    member_rates = per_member(rate_tile)
    span = jnp.exp(member_rates * (-float(LANES)))
    from_others = turned
    for b in range(blocks):
        value = carry_ref[b] + from_others
        from_others = from_others * span
        high = value.astype(bf16).astype(f32)
        mixed = jnp.where(is_low, value - high, value).astype(bf16)
        for g in range(TILE_GROUPS):
            left_all[g, b * MEMBERS : (b + 1) * MEMBERS, :] = mixed[
                g * MEMBERS : (g + 1) * MEMBERS
            ]
        yield 0.5
    cz_parts = split(coefs * jnp.exp(-rates * (lag + 1.0)))
    ce_parts = split(coefs * jnp.exp(-rates * (LANES - 1.0 - lag)))
    for g in range(TILE_GROUPS):
        of = slice(g * MODES, (g + 1) * MODES)
        cz_high, cz_low = cz_parts[0][of], cz_parts[1][of]
        ce_high, ce_low = ce_parts[0][of], ce_parts[1][of]
        right = jnp.concatenate(
            [
                jnp.concatenate([cz_high, cz_high, cz_low, none_16, none_64], axis=0),
                jnp.concatenate([none_64, ce_high, ce_high, none_16, ce_low], axis=0),
            ],
            axis=1,
        )
        carried = dot_nn(left_all[g], right)
        for b in range(blocks):
            at = slice(b * MEMBERS, (b + 1) * MEMBERS)
            opposite = slice((blocks - 1 - b) * MEMBERS, (blocks - b) * MEMBERS)
            inner_t[b, of, :] = inner_ref[g, at, :] + carried[at, :LANES]
            grad_t[b, of, :] = grad_ref[g, at, :] + carried[opposite, LANES:]
        yield 1
    rates = jnp.transpose(member_rates)[0:MODES]
    coefs = jnp.transpose(per_member(coef_tile))[0:MODES]
    decay = jnp.exp(-rates)
    grow = jnp.exp(rates)
    state = bound_ref[32:48]
    sum_0 = jnp.sum(coefs, axis=0, keepdims=True)
    sum_1 = jnp.sum(coefs * decay, axis=0, keepdims=True)
    for i in range(3):
        wide[i, 0:8, :] = jnp.zeros((8, LANES), f32)
        wide[i, 6:8, :] = bound_ref[56 + 2 * i : 58 + 2 * i]
        wide[i, 8:16, :] = start_ref[i, 0:8, :].astype(f32)
    begun = [short_block(wide, taps_ref, i, 0, 8) for i in range(3)]
    z_own = (begun[1] * begun[2]).astype(bf16).astype(f32)
    e_own = cot_ref[0:8, :].astype(f32) * begun[0]
    sum_up = jnp.sum(coefs * grow, axis=0, keepdims=True)
    which = iota(0, (8, LANES))
    inner_fix = jnp.where(which == 0, -sum_up * z_own[1:2], 0.0)
    grad_fix = jnp.where(
        which == 0,
        sum_0 * e_own[0:1] + sum_1 * e_own[1:2],
        jnp.where(which == 1, sum_0 * e_own[1:2], 0.0),
    )
    for b in range(blocks):
        at = slice(b * LANES, (b + 1) * LANES)
        inner = jnp.transpose(inner_t[b])
        query = short_ref[0, at, :]
        if b == 0:
            query = jnp.concatenate([begun[0], short_ref[0, 8:LANES, :]], axis=0)
            inner = jnp.concatenate([inner[0:8] + inner_fix, inner[8:]], axis=0)
        mixer_ref[at, :] = (query * inner).astype(bf16)
        adj[0, at, :] = cot_ref[at, :].astype(f32) * inner
        yield 2
    copies[0].start()
    for b in range(blocks):
        at = slice(b * LANES, (b + 1) * LANES)
        grad = jnp.transpose(grad_t[b])
        key, value = short_ref[1, at, :], short_ref[2, at, :]
        if b == 0:
            key = jnp.concatenate([begun[1], short_ref[1, 8:LANES, :]], axis=0)
            value = jnp.concatenate([begun[2], short_ref[2, 8:LANES, :]], axis=0)
            grad = jnp.concatenate([grad[0:8] + grad_fix, grad[8:]], axis=0)
        adj[1, at, :] = grad * value
        adj[2, at, :] = grad * key
        yield 2
    for i in range(3):
        wide[i, 0:8, :] = edge_ref[i, 8:16, :].astype(f32)
        wide[i, 8:16, :] = jnp.zeros((8, LANES), f32)
        wide[i, 8:10, :] = bound_ref[48 + 2 * i : 50 + 2 * i]
    query, key, value = [short_block(wide, taps_ref, i, 0, 8) for i in range(3)]
    z = (key * value).astype(bf16).astype(f32)
    upstream = jnp.concatenate([bound_ref[54:56], jnp.zeros((6, LANES), f32)], axis=0)
    e = upstream * query
    inner_0 = jnp.sum(coefs * decay * state, axis=0, keepdims=True) + sum_0 * z[0:1]
    inner_1 = (
        jnp.sum(coefs * decay * decay * state, axis=0, keepdims=True)
        + sum_1 * z[0:1]
        + sum_0 * z[1:2]
    )
    grad_0 = jnp.sum(coefs * grow * after, axis=0, keepdims=True)
    grad_1 = jnp.sum(coefs * grow * (grow * after - e[0:1]), axis=0, keepdims=True)
    inner_8 = jnp.where(which == 0, inner_0, jnp.where(which == 1, inner_1, 0.0))
    grad_8 = jnp.where(which == 0, grad_0, jnp.where(which == 1, grad_1, 0.0))
    adj[0, tokens : tokens + 8, :] = upstream * inner_8
    adj[1, tokens : tokens + 8, :] = grad_8 * value
    adj[2, tokens : tokens + 8, :] = grad_8 * key
    for i in range(3):
        for b in range(blocks):
            start = b * LANES
            fgrad_ref[i, start : start + LANES, :] = (
                taps_ref[i, 0:1, :] * adj[i, start : start + LANES, :]
                + taps_ref[i, 1:2, :] * adj[i, start + 1 : start + 1 + LANES, :]
                + taps_ref[i, 2:3, :] * adj[i, start + 2 : start + 2 + LANES, :]
            ).astype(bf16)
            yield 3
        copies[1 + i].start()


def resident(shape, dtype):
    return pltpu.VMEM(shape, dtype)


def sum_kernel(*refs):
    *terms, summed_ref, square_ref = refs
    terms = [term[...] for term in terms]
    while len(terms) > 1:
        terms = [terms[i] + terms[i + 1] for i in range(0, len(terms), 2)]
    summed_ref[...] = terms[0]
    square_ref[...] = jnp.broadcast_to(
        jnp.sum(jnp.sum(terms[0] * terms[0], axis=0, keepdims=True), axis=1, keepdims=True),
        square_ref.shape,
    )


def far(*arrays):
    return [pltpu.with_memory_space_constraint(array, pltpu.HBM) for array in arrays]


def near(*arrays):
    return [pltpu.with_memory_space_constraint(array, pltpu.VMEM) for array in arrays]


def swapped(value, axis, key):
    count = lax.axis_size(axis)
    return lax.ppermute(value, axis, [(i, i ^ key) for i in range(count)])


def per_device(features, short_taps, decay_rates, mode_gains, cotangent):
    tokens = features.shape[1]
    channels = features.shape[2]
    groups = decay_rates.shape[0]
    tiles = channels // LANES
    blocks = tokens // LANES
    ctx_count = lax.axis_size("ctx")
    ctx_index = lax.axis_index("ctx")

    me = ctx_index.astype(jnp.int32).reshape(1)
    rates, gains = decay_rates.T, mode_gains.T

    whole = pl.BlockSpec(memory_space=pltpu.VMEM)
    per = STATE_PER if tiles % STATE_PER == 0 else 1
    feat_spec = pl.BlockSpec((3, tokens, per * LANES), lambda j: (0, 0, j))
    taps_spec = pl.BlockSpec((3, 3, per * LANES), lambda j: (0, 0, j))
    cot_spec = pl.BlockSpec((tokens, per * LANES), lambda j: (0, j))
    table_spec = pl.BlockSpec((MODES, groups), lambda j: (0, 0))
    me_spec = pl.BlockSpec(memory_space=pltpu.SMEM)
    rows = blocks * MEMBERS
    turned = resident((groups, rows, LANES), bf16)
    wide_turned = resident((groups, rows, LANES), f32)
    slots = jax.ShapeDtypeStruct((groups, LANES), f32)
    table_scratch = [pltpu.VMEM((LANES, LANES), f32), pltpu.VMEM((LANES, LANES), f32)]

    def room(mebibytes):
        return pltpu.CompilerParams(vmem_limit_bytes=mebibytes * 2**20)

    z, eh, el, carry, short, states, cross, later, early = pl.pallas_call(
        state_kernel,
        grid=(tiles // per,),
        in_specs=[feat_spec, taps_spec, cot_spec, table_spec, table_spec],
        out_specs=[
            whole,
            whole,
            whole,
            whole,
            whole,
            pl.BlockSpec((4 * MODES, per * LANES), lambda j: (0, j)),
            pl.BlockSpec((per * TILE_GROUPS, LANES), lambda j: (j, 0)),
            whole,
            whole,
        ],
        out_shape=[
            turned,
            turned,
            turned,
            resident((tiles, blocks, LANES, LANES), f32),
            resident((tiles, 3, tokens, LANES), f32),
            jax.ShapeDtypeStruct((4 * MODES, channels), f32),
            slots,
            resident((40, channels), f32),
            resident((40, channels), f32),
        ],
        scratch_shapes=[
            pltpu.VMEM((per, 3, tokens + 8, LANES), f32),
            pltpu.VMEM((per, blocks, LANES, LANES), f32),
            pltpu.VMEM((per, TILE_GROUPS, LANES, 2 * LANES), bf16),
        ]
        + table_scratch,
        compiler_params=room(STATE_ROOM),
        name="state_part",
    )(*far(features, short_taps, cotangent, rates, gains))

    gots = []
    for key in range(1, ctx_count):
        sent = jnp.where((ctx_index ^ key) < ctx_index, early, later)
        gots.append(swapped(sent.astype(bf16), "ctx", key).astype(f32))

    inside_per = INSIDE_PER if tiles % INSIDE_PER == 0 else 1
    inner, grad, diag = pl.pallas_call(
        inside_kernel,
        grid=(tiles // inside_per,),
        in_specs=[whole, whole, whole, table_spec, table_spec],
        out_specs=[
            whole,
            whole,
            pl.BlockSpec((inside_per * TILE_GROUPS, LANES), lambda j: (j, 0)),
        ],
        out_shape=[wide_turned, wide_turned, slots],
        scratch_shapes=[
            pltpu.VMEM((inside_per, TILE_GROUPS, 2 * LANES, LANES), bf16),
            pltpu.VMEM((inside_per, LANES, LANES), f32),
            pltpu.VMEM((inside_per, 8 * TILE_GROUPS, LANES), f32),
        ]
        + table_scratch,
        compiler_params=room(14),
        cost_estimate=pl.CostEstimate(
            flops=2 * groups * rows * LANES * LANES * 7, bytes_accessed=14 * 2**20, transcendentals=0
        ),
        name="inside_part",
    )(*near(z, eh, el), *far(rates, gains))

    bound, local = pl.pallas_call(
        functools.partial(join_kernel, tokens),
        in_specs=[me_spec] + [whole] * (7 + len(gots)),
        out_specs=[whole, whole],
        out_shape=[
            jax.ShapeDtypeStruct((64, channels), f32),
            jax.ShapeDtypeStruct((2 * MODES, groups), f32),
        ],
        scratch_shapes=[pltpu.VMEM((ctx_count, 16, channels), f32)],
        compiler_params=room(14),
        name="join_part",
    )(me, states, later, diag, cross, short_taps, rates, gains, *gots)

    def outputs(first, count, *written):
        per = OUTPUT_PER if count % OUTPUT_PER == 0 and first % OUTPUT_PER == 0 else 1
        wide_lanes = per * LANES
        columns = lambda j: (0, j + first // per)
        layers = lambda j: (0, 0, j + first // per)
        return pl.pallas_call(
            functools.partial(output_kernel, first),
            grid=(count // per,),
            in_specs=[
                pl.BlockSpec((3, 16, wide_lanes), layers),
                pl.BlockSpec((3, 16, wide_lanes), lambda j: (0, tokens // 16 - 1, j + first // per)),
                pl.BlockSpec((3, 3, wide_lanes), layers),
                pl.BlockSpec((tokens, wide_lanes), columns),
                table_spec,
                table_spec,
                whole,
                whole,
                whole,
                whole,
                pl.BlockSpec((64, wide_lanes), columns),
            ]
            + [pl.BlockSpec(memory_space=pl.ANY)] * len(written),
            out_specs=[pl.BlockSpec(memory_space=pl.ANY)] * 2,
            out_shape=[
                jax.ShapeDtypeStruct((tokens, channels), bf16),
                jax.ShapeDtypeStruct((3, tokens, channels), bf16),
            ],
            scratch_shapes=[
                pltpu.VMEM((count, tokens, LANES), bf16),
                pltpu.VMEM((count, 3, tokens, LANES), bf16),
                pltpu.SemaphoreType.DMA((count, 4)),
                pltpu.VMEM((per, 3, 16, LANES), f32),
                pltpu.VMEM((per, 3, tokens + 8, LANES), f32),
                pltpu.VMEM((per, blocks, LANES, LANES), f32),
                pltpu.VMEM((per, blocks, LANES, LANES), f32),
                pltpu.VMEM((per, TILE_GROUPS, rows, LANES), bf16),
            ]
            + table_scratch,
            compiler_params=room(OUTPUT_ROOM),
            input_output_aliases={11: 0, 12: 1} if written else {},
            cost_estimate=pl.CostEstimate(
                flops=2 * count * TILE_GROUPS * rows * LANES * LANES * 8,
                bytes_accessed=count * 4 * 2**20,
                transcendentals=0,
            ),
            name="output_part",
        )(
            *far(features, features, short_taps, cotangent, rates, gains),
            *near(inner, grad, carry, short),
            bound,
            *written,
        )

    half = tiles // 2
    terms = [local] + [swapped(local, "ctx", key) for key in range(1, ctx_count)]
    written = outputs(0, half)
    terms, written = lax.optimization_barrier((terms, written))
    summed, squares = pl.pallas_call(
        sum_kernel,
        in_specs=[whole] * len(terms),
        out_specs=[whole, whole],
        out_shape=[
            jax.ShapeDtypeStruct((2 * MODES, groups), f32),
            jax.ShapeDtypeStruct((1, groups), f32),
        ],
        compiler_params=room(14),
        name="sum_part",
    )(*terms)
    fsdp_count = lax.axis_size("fsdp")
    step = 1
    while step * 4 < fsdp_count:
        squares = squares + swapped(squares, "fsdp", step)
        step *= 2
    squares, written = lax.optimization_barrier((squares, written))
    parts = [squares] + [swapped(squares, "fsdp", key) for key in range(step, fsdp_count, step)]
    mixer, feature_grads = outputs(half, tiles - half, *written)
    while len(parts) > 1:
        parts = [parts[i] + parts[i + 1] for i in range(0, len(parts), 2)]
    entry_count = 2 * groups * MODES * fsdp_count
    clipped = summed * jnp.minimum(1.0, lax.rsqrt(parts[0] / entry_count + 1e-06))
    return (mixer, feature_grads, clipped[:MODES].T, clipped[MODES:].T)


def solution(mesh):
    return jax.shard_map(
        per_device,
        mesh=mesh,
        in_specs=(
            P(None, "ctx", "fsdp"),
            P(None, None, "fsdp"),
            P("fsdp", None),
            P("fsdp", None),
            P("ctx", "fsdp"),
        ),
        out_specs=(P("ctx", "fsdp"), P(None, "ctx", "fsdp"), P("fsdp", None), P("fsdp", None)),
        check_vma=False,
    )
```
